32 devices in a mesh: row: 8 (over y, x, core), col: 4 (over z).
Axes of the slice: x: 2, y: 2, z: 4, core: 2. Of those that a mesh axis runs over, the one named last changes fastest.
Arguments:
- features: bfloat16 [16384, 256], P(('col', 'row')), may hold values from -6 to 6
- weight: bfloat16 [256, 256], replicated, may hold values from -0.375 to 0.375
- block_cols: int32 [8, 4, 128], P('row', 'col'), may hold values from 0 to 31, as said below
- row_starts: int32 [8, 4, 17], P('row', 'col'), may hold values from 0 to 128, as said below
- block_values: bfloat16 [8, 4, 128, 128, 128], P('row', 'col'), as said below
- cotangent: bfloat16 [16384, 256], P(('row', 'col')), may hold values from -6 to 6
Outputs:
- activations: bfloat16 [16384, 256], P(('row', 'col'))
- feature_grad: bfloat16 [16384, 256], P(('col', 'row'))
- weight_grad: float32 [256, 256], replicated
The draws below stay inside these ranges and needn't reach their ends.
Inputs may be any that keep to these rules, and one draw needn't show every extreme that they name: `block_cols`: each slot names one of the 32 block columns of its cell's column group. `row_starts`: in each cell the entries start at 0 and never fall; the last one is the cell's count of live slots, and it equals 128 in at least one cell. `block_values`: every entry is zero or positive.
All inputs are finite; a program needn't handle non-finite values.
Results may differ from the reference program's by a relative error of at most 0.018.
Values may be sent and summed in bfloat16 or wider, within the bound.
No kernel may reach another device: no remote copies, remote signals or barrier semaphores. Data moves between devices by JAX's collectives and lax.ppermute only.
A program may use at most 128 MiB of HBM per device.

```python
import jax
import jax.numpy as jnp
from jax import lax

FEAT = 256
BLOCK = 128
SLOTS = 128
NODES = 16384
NRB = 16
NCB = 32
N_ROW = 8
N_COL = 4


def cell_layout(key):
    key_cols, key_rows, key_count, key_order = jax.random.split(key, 4)
    cells = N_ROW * N_COL
    order = jax.random.permutation(key_order, cells)
    base = jax.random.randint(key_count, (cells,), SLOTS // 4, SLOTS // 2 + 1)
    counts = jnp.where(order == 0, SLOTS, base).astype(jnp.int32)
    rows = jnp.sort(jax.random.randint(key_rows, (cells, SLOTS), 0, NRB), axis=1)
    cols = jax.random.randint(key_cols, (cells, SLOTS), 0, NCB).astype(jnp.int32)
    index = jnp.arange(SLOTS, dtype=jnp.int32)
    bounds = jnp.arange(NRB + 1, dtype=jnp.int32)
    live = index[None, :] < counts[:, None]
    below = rows[:, None, :] < bounds[None, :, None]
    starts = jnp.sum((live[:, None, :] & below).astype(jnp.int32), axis=2)
    return (cols, starts)


def draw_block_cols(key, part):
    cols, starts = cell_layout(key)
    return cols.reshape(N_ROW, N_COL, SLOTS)


def draw_row_starts(key, part):
    cols, starts = cell_layout(key)
    return starts.reshape(N_ROW, N_COL, NRB + 1).astype(jnp.int32)


def draw_block_values(key, part):
    key = jax.random.fold_in(key, 13)
    key_mask, key_size = jax.random.split(key)
    shape = (N_ROW, N_COL, SLOTS, BLOCK, BLOCK)
    mask = (jax.random.uniform(key_mask, shape) < 0.5).astype(jnp.float32)
    sizes = jax.random.uniform(key_size, shape, minval=0.5, maxval=1.5)
    per_row = max(1.0, N_COL * (3.0 * SLOTS / 8.0) / NRB)
    norm = 1.0 / (0.5 * BLOCK * per_row) ** 0.5
    return (mask * sizes * norm).astype(jnp.bfloat16)


def block_scale(key, dims, cuts, least, high):
    level, own = 1.0, jax.random.fold_in(key, 6)
    for axis_at, shards_of in cuts:
        heights = jnp.exp(jax.random.uniform(jax.random.fold_in(own, axis_at), (shards_of,), jnp.float32, least / len(cuts), high / len(cuts)))
        level = level * jnp.repeat(heights, dims[axis_at] // shards_of).reshape([-1 if axis == axis_at else 1 for axis in range(len(dims))])
    return level


def noise(stream_key, extent, width, bound, pieces=(), kind=jnp.bfloat16):
    loudness = block_scale(stream_key, extent, pieces, -0.22, 0.18) if pieces else 1.0
    values = jax.random.normal(stream_key, extent, jnp.float32) * width * loudness
    return jnp.minimum(jnp.maximum(values, -bound), bound).astype(kind)


def setup_inputs(seed: int = 0) -> dict:
    key_list = jax.random.split(jax.random.key(seed), 7)
    return {
        "features": noise(key_list[0], (NODES, FEAT), 1.0, 6.0, ((0, 32),)),
        "weight": noise(key_list[1], (FEAT, FEAT), FEAT ** -0.5, 0.375),
        "block_cols": draw_block_cols(jax.random.fold_in(key_list[6], 71), 0),
        "row_starts": draw_row_starts(jax.random.fold_in(key_list[6], 71), 0),
        "block_values": draw_block_values(jax.random.fold_in(key_list[6], 71), 0),
        "cotangent": noise(key_list[5], (NODES, FEAT), 1.0, 6.0, ((0, 32),)),
    }


def slot_rows(starts, count):
    index = jnp.arange(count, dtype=jnp.int32)
    inner = starts[1:]
    rows = jnp.sum((inner[None, :] <= index[:, None]).astype(jnp.int32), axis=1)
    rows = jnp.minimum(rows, inner.shape[0] - 1).astype(jnp.int32)
    live = (index < starts[-1]).astype(jnp.float32)
    return rows, live


def rounded(value):
    narrow = lax.optimization_barrier(value.astype(jnp.bfloat16))
    return narrow.astype(jnp.float32)


def reference(features, weight, block_cols, row_starts, block_values, cotangent):
    panels = features.reshape(N_COL, NCB, BLOCK, FEAT)

    def forward_group(group):
        vals_r, cols_r, starts_r = group

        def one_cell(total, cell):
            vals, cols, starts, panel = cell
            rows, live = slot_rows(starts, SLOTS)
            masked = vals.astype(jnp.float32) * live[:, None, None]
            blocks = panel[cols].astype(jnp.float32)
            terms = jnp.einsum("kij,kjf->kif", masked, blocks)
            return total + rounded(jax.ops.segment_sum(terms, rows, num_segments=NRB)), None

        start_total = jnp.zeros((NRB, BLOCK, FEAT), jnp.float32)
        total, unused = lax.scan(one_cell, start_total, (vals_r, cols_r, starts_r, panels))
        return total

    aggregated = lax.map(forward_group, (block_values, block_cols, row_starts)).reshape(NODES, FEAT)
    weight_wide = weight.astype(jnp.float32)
    mixed = jnp.dot(aggregated, weight_wide, precision=lax.Precision.HIGHEST)
    sigma = jax.nn.sigmoid(mixed)
    activations = (mixed * sigma).astype(jnp.bfloat16)
    mixed_grad = cotangent.astype(jnp.float32) * (sigma * (1.0 + mixed * (1.0 - sigma)))
    weight_grad = jnp.dot(aggregated.T, mixed_grad, precision=lax.Precision.HIGHEST)
    aggregated_grad = jnp.dot(mixed_grad, weight_wide.T, precision=lax.Precision.HIGHEST).astype(jnp.bfloat16)
    grad_panels = aggregated_grad.reshape(N_ROW, NRB, BLOCK, FEAT)

    def backward_group(total, group):
        vals_r, cols_r, starts_r, panel = group

        def one_cell(cell):
            vals, cols, starts = cell
            rows, live = slot_rows(starts, SLOTS)
            masked = vals.astype(jnp.float32) * live[:, None, None]
            blocks = panel[rows].astype(jnp.float32)
            terms = jnp.einsum("kij,kif->kjf", masked, blocks)
            return rounded(jax.ops.segment_sum(terms, cols, num_segments=NCB))

        return total + lax.map(one_cell, (vals_r, cols_r, starts_r)), None

    start_grad = jnp.zeros((N_COL, NCB, BLOCK, FEAT), jnp.float32)
    grad_total, unused = lax.scan(backward_group, start_grad, (block_values, block_cols, row_starts, grad_panels))
    feature_grad = grad_total.reshape(NODES, FEAT).astype(jnp.bfloat16)
    return activations, feature_grad, weight_grad
```

```python
import functools

import jax
import jax.numpy as jnp
from jax import lax
from jax.experimental import pallas as pl
from jax.experimental.pallas import tpu as pltpu
from jax.sharding import PartitionSpec as P

F32 = jnp.float32
BF16 = jnp.bfloat16
GROUP = 8
ANY = pl.BlockSpec(memory_space=pl.ANY)
VMEM = pl.BlockSpec(memory_space=pltpu.VMEM)
SMEM = pl.BlockSpec(memory_space=pltpu.SMEM)


def params(mib):
    return pltpu.CompilerParams(vmem_limit_bytes=mib << 20)


def cost(flops, nbytes):
    return pl.CostEstimate(flops=flops, bytes_accessed=nbytes, transcendentals=0)


def sparse_kernel(parts, outs, transposed, meta, to, source, *refs):
    panel_refs = refs[:parts]
    values_ref = refs[parts]
    out_refs = refs[parts + 1 : parts + 1 + len(outs)]
    panel, values, total, panel_sem, values_sem = refs[parts + 1 + len(outs) :]
    live, here, mine = meta[0], meta[1], meta[2]
    chunk = panel_refs[0].shape[0]
    size = values.shape[1]
    groups = values.shape[0] // GROUP
    loads = []
    for m in range(parts):
        start = pl.multiple_of((here ^ m) * chunk, chunk)
        copy = pltpu.make_async_copy(
            panel_refs[m], panel.at[pl.ds(start, chunk)], panel_sem.at[m]
        )
        copy.start()
        loads.append(copy)

    def load(g):
        span = pl.ds(pl.multiple_of(g * GROUP, GROUP), GROUP)
        return pltpu.make_async_copy(values_ref.at[span], values.at[span], values_sem.at[g])

    used = (live + GROUP - 1) // GROUP

    def begin(g, carry):
        load(g).start()
        return carry

    lax.fori_loop(0, used, begin, 0)
    total[...] = jnp.zeros_like(total)
    for copy in loads:
        copy.wait()

    def step(g, carry):
        load(g).wait()
        for u in range(GROUP):
            k = g * GROUP + u
            i = pl.multiple_of(to[k] * size, size)
            j = pl.multiple_of(source[k] * size, size)
            block = values[k]
            if transposed:
                term = lax.dot_general(
                    block,
                    panel[pl.ds(j, size), :],
                    (((0,), (0,)), ((), ())),
                    preferred_element_type=F32,
                )
            else:
                term = jnp.dot(block, panel[pl.ds(j, size), :], preferred_element_type=F32)
            total[pl.ds(i, size), :] += term
        return carry

    lax.fori_loop(0, used, step, 0)
    for out_ref, members in zip(out_refs, outs):
        rows = out_ref.shape[0] // len(members)
        for at, m in enumerate(members):
            start = pl.multiple_of((mine ^ m) * rows, rows)
            out_ref[at * rows : (at + 1) * rows, :] = total[pl.ds(start, rows), :].astype(
                out_ref.dtype
            )


def sparse_product(panel_parts, values, meta, to, source, blocks, outs, transposed):
    parts = len(panel_parts)
    slots, size, _ = values.shape
    chunk, width = panel_parts[0].shape
    rows = chunk
    flops = 2 * slots * size * size * width
    return pl.pallas_call(
        functools.partial(sparse_kernel, parts, outs, transposed),
        out_shape=[jax.ShapeDtypeStruct((rows * len(members), width), BF16) for members in outs],
        in_specs=[SMEM] * 3 + [ANY] * (parts + 1),
        out_specs=[VMEM] * len(outs),
        scratch_shapes=[
            pltpu.VMEM((parts * chunk, width), BF16),
            pltpu.VMEM((slots, size, size), BF16),
            pltpu.VMEM(((blocks + 1) * size, width), F32),
            pltpu.SemaphoreType.DMA((parts,)),
            pltpu.SemaphoreType.DMA((slots // GROUP,)),
        ],
        compiler_params=params(48),
        cost_estimate=cost(flops, 2 * values.size + 2 * parts * chunk * width),
    )(meta, to, source, *panel_parts, values)


def split(value):
    high = value.astype(BF16)
    return high, (value - high.astype(F32)).astype(BF16)


def mm(a, b, dims):
    return lax.dot_general(a, b, (dims, ((), ())), preferred_element_type=F32)


def middle_kernel(count, *refs):
    terms = refs[:count]
    weight_ref, cotangent_ref, act_ref, back_ref, agg_ref, grad_ref = refs[count:]
    aggregated = terms[0][...].astype(F32)
    for term in terms[1:]:
        aggregated += term[...].astype(F32)
    agg_ref[...] = aggregated
    weight = weight_ref[...]
    high, low = split(aggregated)
    mixed = mm(high, weight, ((1,), (0,))) + mm(low, weight, ((1,), (0,)))
    sigma = jax.nn.sigmoid(mixed)
    act_ref[...] = (mixed * sigma).astype(BF16)
    mixed_grad = cotangent_ref[...].astype(F32) * (sigma * (1.0 + mixed * (1.0 - sigma)))
    grad_ref[...] = mixed_grad
    high, low = split(mixed_grad)
    back = mm(high, weight, ((1,), (1,))) + mm(low, weight, ((1,), (1,)))
    back_ref[...] = back.astype(BF16)


def middle(terms, weight, cotangent):
    rows, width = cotangent.shape
    return pl.pallas_call(
        functools.partial(middle_kernel, len(terms)),
        out_shape=[
            jax.ShapeDtypeStruct((rows, width), BF16),
            jax.ShapeDtypeStruct((rows, width), BF16),
            jax.ShapeDtypeStruct((rows, width), F32),
            jax.ShapeDtypeStruct((rows, width), F32),
        ],
        in_specs=[VMEM] * (len(terms) + 2),
        out_specs=[VMEM] * 4,
        compiler_params=params(40),
        cost_estimate=cost(8 * rows * width * width, 20 * rows * width),
    )(*terms, weight, cotangent)


def weight_kernel(chunks, me, agg_ref, grad_ref, *outs):
    high, low = split(agg_ref[...])
    grad_high, grad_low = split(grad_ref[...])
    contract = ((0,), (0,))
    term = (
        mm(high, grad_high, contract) + mm(low, grad_high, contract) + mm(high, grad_low, contract)
    )
    scratch = outs[-1]
    scratch[...] = term
    rows = term.shape[0] // chunks
    for m in range(chunks):
        start = pl.multiple_of((me[0] ^ m) * rows, rows)
        outs[m][...] = scratch[pl.ds(start, rows), :]


def weight_term(aggregated, mixed_grad, me, chunks):
    rows, width = aggregated.shape
    return pl.pallas_call(
        functools.partial(weight_kernel, chunks),
        out_shape=[jax.ShapeDtypeStruct((width // chunks, width), F32)] * chunks,
        in_specs=[SMEM, VMEM, VMEM],
        out_specs=[VMEM] * chunks,
        scratch_shapes=[pltpu.VMEM((width, width), F32)],
        compiler_params=params(40),
        cost_estimate=cost(6 * rows * width * width, 8 * rows * width),
    )(me, aggregated, mixed_grad)


def pair_kernel(count, own_ref, other_ref, *outs):
    rows = own_ref.shape[0] // count
    for m in range(count):
        span = slice(m * rows, (m + 1) * rows)
        outs[m][...] = (own_ref[span, :].astype(F32) + other_ref[span, :].astype(F32)).astype(BF16)


def pair_sum(own, other, count):
    rows, width = own.shape
    return pl.pallas_call(
        functools.partial(pair_kernel, count),
        out_shape=[jax.ShapeDtypeStruct((rows // count, width), BF16)] * count,
        in_specs=[VMEM] * 2,
        out_specs=[VMEM] * count,
        compiler_params=params(40),
        cost_estimate=cost(rows * width, 6 * rows * width),
    )(own, other)


def swap(x, axis, n, m):
    return lax.ppermute(x, axis, [(i, i ^ m) for i in range(n)])


def total_of(terms):
    result = terms[0].astype(F32)
    for term in terms[1:]:
        result = result + term.astype(F32)
    return result


def on_device(n_row, n_col, features, weight, block_cols, row_starts, block_values, cotangent):
    values = block_values[0, 0]
    starts = row_starts[0, 0]
    slots, size, _ = values.shape
    row_blocks = starts.shape[0] - 1
    col_blocks = n_row * features.shape[0] // size
    me_row = lax.axis_index("row")
    me_col = lax.axis_index("col")

    panel = [features] + [None] * (n_row - 1)
    for m in range(2, n_row, 2):
        panel[m] = swap(features, "row", n_row, m)
    for m in range(0, n_row, 2):
        panel[m + 1] = swap(panel[m], "row", n_row, 1)

    index = jnp.arange(slots, dtype=jnp.int32)
    rows = jnp.sum((starts[None, 1:] <= index[:, None]).astype(jnp.int32), axis=1)
    live = starts[-1]
    cols = block_cols[0, 0]
    cols_to = jnp.where(index < live, cols, col_blocks)
    rows_from = jnp.minimum(rows, row_blocks - 1)
    meta = jnp.stack([live, me_row, me_col]).astype(jnp.int32)
    meta_back = jnp.stack([live, me_col, me_row]).astype(jnp.int32)

    terms = sparse_product(
        panel, values, meta, rows, cols, row_blocks, [[m] for m in range(n_col)], False
    )
    terms = [terms[0]] + [swap(terms[m], "col", n_col, m) for m in range(1, n_col)]
    activations, back, aggregated, mixed_grad = middle(terms, weight, cotangent)

    back_panel = [back] + [swap(back, "col", n_col, m) for m in range(1, n_col)]

    pieces = weight_term(aggregated, mixed_grad, me_row[None].astype(jnp.int32), n_row)
    piece = total_of([pieces[0]] + [swap(pieces[m], "row", n_row, m) for m in range(1, n_row)])
    piece = total_of([piece] + [swap(piece, "col", n_col, m) for m in range(1, n_col)])

    even = list(range(0, n_row, 2))
    own, other = sparse_product(
        back_panel,
        values,
        meta_back,
        cols_to,
        rows_from,
        col_blocks,
        [even, [m + 1 for m in even]],
        True,
    )
    sums = pair_sum(own, swap(other, "row", n_row, 1), len(even))
    feature_grad = total_of(
        [sums[0]] + [swap(s, "row", n_row, m) for s, m in zip(sums[1:], even[1:])]
    ).astype(BF16)

    weight_grad = jnp.zeros(weight.shape, F32)
    depth = weight.shape[0] // n_row
    gathered = [piece] + [swap(piece, "row", n_row, m) for m in range(1, n_row)]
    for m in range(n_row):
        weight_grad = lax.dynamic_update_slice(
            weight_grad, gathered[m], ((me_row ^ m) * depth, jnp.int32(0))
        )
    return (activations, feature_grad, weight_grad)


def solution(mesh):
    placed = (
        P(("col", "row"), None),
        P(),
        P("row", "col", None),
        P("row", "col", None),
        P("row", "col", None, None, None),
        P(("row", "col"), None),
    )
    return jax.shard_map(
        functools.partial(on_device, mesh.shape["row"], mesh.shape["col"]),
        mesh=mesh,
        in_specs=placed,
        out_specs=(P(("row", "col"), None), P(("col", "row"), None), P()),
        check_vma=False,
    )
```

```python
import functools

import jax
import jax.numpy as jnp
from jax import lax
from jax.experimental import pallas as pl
from jax.experimental.pallas import tpu as pltpu
from jax.sharding import PartitionSpec as P

F32 = jnp.float32
BF16 = jnp.bfloat16
GROUP = 8
ANY = pl.BlockSpec(memory_space=pl.ANY)
VMEM = pl.BlockSpec(memory_space=pltpu.VMEM)
SMEM = pl.BlockSpec(memory_space=pltpu.SMEM)


def params(mib):
    return pltpu.CompilerParams(vmem_limit_bytes=mib << 20)


def cost(flops, nbytes):
    return pl.CostEstimate(flops=flops, bytes_accessed=nbytes, transcendentals=0)


def prepare_kernel(starts, cols, features, row_of, col_of, own):
    own[...] = features[...]
    slots = cols.shape[2]
    row_blocks = starts.shape[2] - 1

    def name_row(i, carry):
        def name_slot(k, carry):
            row_of[k] = i
            return carry

        return lax.fori_loop(starts[0, 0, i], starts[0, 0, i + 1], name_slot, carry)

    lax.fori_loop(0, row_blocks, name_row, 0)
    live = starts[0, 0, row_blocks]

    def name_dead(k, carry):
        row_of[k] = row_blocks
        return carry

    lax.fori_loop(live, slots, name_dead, 0)
    row_of[slots] = live

    def name_col(k, carry):
        col_of[k] = cols[0, 0, k]
        return carry

    lax.fori_loop(0, slots, name_col, 0)


def prepare(starts, cols, features):
    slots = cols.shape[2]
    return pl.pallas_call(
        prepare_kernel,
        out_shape=[
            jax.ShapeDtypeStruct((slots + 1,), jnp.int32),
            jax.ShapeDtypeStruct((slots,), jnp.int32),
            jax.ShapeDtypeStruct(features.shape, BF16),
        ],
        in_specs=[SMEM, SMEM, VMEM],
        out_specs=[SMEM, SMEM, VMEM],
        compiler_params=params(32),
    )(starts, cols, features)


def sparse_kernel(parts, outs, backward, row_of, col_of, here_ref, mine_ref, *refs):
    panel_refs = refs[:parts]
    values_ref = refs[parts]
    out_refs = refs[parts + 1 : parts + 1 + len(outs)]
    panel, values, total, panel_sem, values_sem = refs[parts + 1 + len(outs) :]
    slots, size, _ = values.shape
    live, here, mine = row_of[slots], here_ref[0], mine_ref[0]
    chunk = panel_refs[0].shape[0]
    loads = []
    for m in range(parts):
        start = pl.multiple_of((here ^ m) * chunk, chunk)
        copy = pltpu.make_async_copy(
            panel_refs[m], panel.at[pl.ds(start, chunk)], panel_sem.at[m]
        )
        copy.start()
        loads.append(copy)

    def load(g):
        span = pl.ds(pl.multiple_of(g * GROUP, GROUP), GROUP)
        return pltpu.make_async_copy(values_ref.at[span], values.at[span], values_sem.at[g])

    def begin(g, carry):
        load(g).start()
        return carry

    used = (live + GROUP - 1) // GROUP
    lax.fori_loop(0, used, begin, 0)
    total[...] = jnp.zeros_like(total)
    for copy in loads:
        copy.wait()
    spare = total.shape[0] // size - 1
    last = panel.shape[0] // size - 1

    def step(g, carry):
        load(g).wait()
        for u in range(GROUP):
            k = g * GROUP + u
            row, col = row_of[k], col_of[k]
            to, source = (col, jnp.minimum(row, last)) if backward else (row, col)
            to = pl.multiple_of(jnp.where(k < live, to, spare) * size, size)
            source = pl.multiple_of(source * size, size)
            term = lax.dot_general(
                values[k],
                panel[pl.ds(source, size), :],
                (((0 if backward else 1,), (0,)), ((), ())),
                preferred_element_type=F32,
            )
            total[pl.ds(to, size), :] += term
        return carry

    lax.fori_loop(0, used, step, 0)
    for out_ref, members in zip(out_refs, outs):
        rows = out_ref.shape[0] // len(members)
        for at, m in enumerate(members):
            start = pl.multiple_of((mine ^ m) * rows, rows)
            out_ref[at * rows : (at + 1) * rows, :] = total[pl.ds(start, rows), :].astype(
                out_ref.dtype
            )


def sparse_product(panel_parts, values, row_of, col_of, here, mine, blocks, outs, backward):
    parts = len(panel_parts)
    slots, size, _ = values.shape
    chunk, width = panel_parts[0].shape
    flops = 2 * slots * size * size * width
    return pl.pallas_call(
        functools.partial(sparse_kernel, parts, outs, backward),
        out_shape=[jax.ShapeDtypeStruct((chunk * len(members), width), BF16) for members in outs],
        in_specs=[SMEM] * 4 + [ANY] * (parts + 1),
        out_specs=[VMEM] * len(outs),
        scratch_shapes=[
            pltpu.VMEM((parts * chunk, width), BF16),
            pltpu.VMEM((slots, size, size), BF16),
            pltpu.VMEM(((blocks + 1) * size, width), F32),
            pltpu.SemaphoreType.DMA((parts,)),
            pltpu.SemaphoreType.DMA((slots // GROUP,)),
        ],
        compiler_params=params(48),
        cost_estimate=cost(flops, 2 * values.size + 2 * parts * chunk * width),
    )(row_of, col_of, here, mine, *panel_parts, values)


def split(value):
    high = value.astype(BF16)
    return high, (value - high.astype(F32)).astype(BF16)


def mm(a, b, dims):
    return lax.dot_general(a, b, (dims, ((), ())), preferred_element_type=F32)


def middle_kernel(count, *refs):
    terms = refs[:count]
    weight_ref, cotangent_ref, act_ref, back_ref, agg_ref, grad_ref = refs[count:]
    aggregated = terms[0][...].astype(F32)
    for term in terms[1:]:
        aggregated += term[...].astype(F32)
    agg_ref[...] = aggregated
    weight = weight_ref[...]
    high, low = split(aggregated)
    mixed = mm(high, weight, ((1,), (0,))) + mm(low, weight, ((1,), (0,)))
    sigma = jax.nn.sigmoid(mixed)
    act_ref[...] = (mixed * sigma).astype(BF16)
    mixed_grad = cotangent_ref[...].astype(F32) * (sigma * (1.0 + mixed * (1.0 - sigma)))
    grad_ref[...] = mixed_grad
    high, low = split(mixed_grad)
    back = mm(high, weight, ((1,), (1,))) + mm(low, weight, ((1,), (1,)))
    back_ref[...] = back.astype(BF16)


def middle(terms, weight, cotangent):
    rows, width = cotangent.shape
    return pl.pallas_call(
        functools.partial(middle_kernel, len(terms)),
        out_shape=[
            jax.ShapeDtypeStruct((rows, width), BF16),
            jax.ShapeDtypeStruct((rows, width), BF16),
            jax.ShapeDtypeStruct((rows, width), F32),
            jax.ShapeDtypeStruct((rows, width), F32),
        ],
        in_specs=[VMEM] * (len(terms) + 2),
        out_specs=[VMEM] * 4,
        compiler_params=params(40),
        cost_estimate=cost(8 * rows * width * width, 20 * rows * width),
    )(*terms, weight, cotangent)


def weight_kernel(agg_ref, grad_ref, out_ref):
    high, low = split(agg_ref[...])
    grad_high, grad_low = split(grad_ref[...])
    contract = ((0,), (0,))
    out_ref[...] = (
        mm(high, grad_high, contract) + mm(low, grad_high, contract) + mm(high, grad_low, contract)
    )


def weight_term(aggregated, mixed_grad):
    rows, width = aggregated.shape
    return pl.pallas_call(
        weight_kernel,
        out_shape=jax.ShapeDtypeStruct((width, width), F32),
        in_specs=[VMEM, VMEM],
        out_specs=VMEM,
        compiler_params=params(40),
        cost_estimate=cost(6 * rows * width * width, 8 * rows * width),
    )(aggregated, mixed_grad)


def assemble_kernel(parts, me, *refs):
    out_ref = refs[parts]
    depth = refs[0].shape[0] // 2
    for p in range(parts):
        for core in range(2):
            start = pl.multiple_of((me[0] ^ (2 * p + core)) * depth, depth)
            out_ref[pl.ds(start, depth), :] = refs[p][core * depth : (core + 1) * depth, :]


def assemble(parts, me):
    depth, width = parts[0].shape
    return pl.pallas_call(
        functools.partial(assemble_kernel, len(parts)),
        out_shape=jax.ShapeDtypeStruct((depth * len(parts), width), F32),
        in_specs=[SMEM] + [VMEM] * len(parts),
        out_specs=VMEM,
        compiler_params=params(32),
    )(me, *parts)


def pair_kernel(count, own_ref, other_ref, *outs):
    rows = own_ref.shape[0] // count
    for m in range(count):
        span = slice(m * rows, (m + 1) * rows)
        outs[m][...] = (own_ref[span, :].astype(F32) + other_ref[span, :].astype(F32)).astype(BF16)


def pair_sum(own, other, count):
    rows, width = own.shape
    return pl.pallas_call(
        functools.partial(pair_kernel, count),
        out_shape=[jax.ShapeDtypeStruct((rows // count, width), BF16)] * count,
        in_specs=[VMEM] * 2,
        out_specs=[VMEM] * count,
        compiler_params=params(40),
        cost_estimate=cost(rows * width, 6 * rows * width),
    )(own, other)


def swap(x, axis, n, m):
    return lax.ppermute(x, axis, [(i, i ^ m) for i in range(n)])


def total_of(terms):
    result = terms[0].astype(F32)
    for term in terms[1:]:
        result = result + term.astype(F32)
    return result


def exchange(x, axis):
    return lax.all_to_all(x, axis, 0, 0, tiled=True)


def on_device(n_row, n_col, features, weight, block_cols, row_starts, block_values, cotangent):
    values = block_values[0, 0]
    size = values.shape[1]
    row_blocks = row_starts.shape[2] - 1
    col_blocks = n_row * features.shape[0] // size
    me_row = lax.axis_index("row")[None].astype(jnp.int32)
    me_col = lax.axis_index("col")[None].astype(jnp.int32)

    panel = [features] + [None] * (n_row - 1)
    for m in range(2, n_row, 2):
        panel[m] = swap(features, "row", n_row, m)
    prepared = prepare(row_starts, block_cols, features)
    panel[2], (row_of, col_of, panel[0]) = lax.optimization_barrier((panel[2], prepared))
    for m in range(0, n_row, 2):
        panel[m + 1] = swap(panel[m], "row", n_row, 1)

    each = [[m] for m in range(n_col)]
    terms = sparse_product(panel, values, row_of, col_of, me_row, me_col, row_blocks, each, False)
    terms = [terms[0]] + [swap(terms[m], "col", n_col, m) for m in range(1, n_col)]
    activations, back, aggregated, mixed_grad = middle(terms, weight, cotangent)

    back_panel = [back] + [swap(back, "col", n_col, m) for m in range(1, n_col)]

    depth = weight.shape[0] // n_row
    piece = exchange(weight_term(aggregated, mixed_grad), "row")
    piece = jnp.sum(piece.reshape(n_row, depth, -1), axis=0)
    piece = exchange(jnp.tile(piece, (n_col, 1)), "col")
    piece = jnp.sum(piece.reshape(n_col, depth, -1), axis=0)
    piece, back_panel[0] = lax.optimization_barrier((piece, back_panel[0]))
    piece = jnp.concatenate([piece, swap(piece, "row", n_row, 1)])
    gathered = [piece] + [swap(piece, "row", n_row, m) for m in range(2, n_row, 2)]

    even = list(range(0, n_row, 2))
    pair = [even, [m + 1 for m in even]]
    own, other = sparse_product(
        back_panel, values, row_of, col_of, me_col, me_row, col_blocks, pair, True
    )
    sums = pair_sum(own, swap(other, "row", n_row, 1), len(even))
    feature_grad = total_of(
        [sums[0]] + [swap(s, "row", n_row, m) for s, m in zip(sums[1:], even[1:])]
    ).astype(BF16)
    weight_grad = assemble(gathered, me_row)
    return (activations, feature_grad, weight_grad)


def solution(mesh):
    placed = (
        P(("col", "row"), None),
        P(),
        P("row", "col", None),
        P("row", "col", None),
        P("row", "col", None, None, None),
        P(("row", "col"), None),
    )
    return jax.shard_map(
        functools.partial(on_device, mesh.shape["row"], mesh.shape["col"]),
        mesh=mesh,
        in_specs=placed,
        out_specs=(P(("row", "col"), None), P(("col", "row"), None), P()),
        check_vma=False,
    )
```

```python
import functools

import jax
import jax.numpy as jnp
from jax import lax
from jax.experimental import pallas as pl
from jax.experimental.pallas import tpu as pltpu
from jax.sharding import PartitionSpec as P

F32 = jnp.float32
BF16 = jnp.bfloat16
GROUP = 8
ANY = pl.BlockSpec(memory_space=pl.ANY)
VMEM = pl.BlockSpec(memory_space=pltpu.VMEM)
SMEM = pl.BlockSpec(memory_space=pltpu.SMEM)


def params(mib):
    return pltpu.CompilerParams(vmem_limit_bytes=mib << 20)


def cost(flops, nbytes):
    return pl.CostEstimate(flops=flops, bytes_accessed=nbytes, transcendentals=0)


def prepare_kernel(starts, cols, features, row_of, col_of, own):
    own[...] = features[...]
    slots = cols.shape[2]
    row_blocks = starts.shape[2] - 1

    def name_row(i, carry):
        def name_slot(k, carry):
            row_of[k] = i
            return carry

        return lax.fori_loop(starts[0, 0, i], starts[0, 0, i + 1], name_slot, carry)

    lax.fori_loop(0, row_blocks, name_row, 0)
    live = starts[0, 0, row_blocks]

    def name_dead(k, carry):
        row_of[k] = row_blocks
        return carry

    lax.fori_loop(live, slots, name_dead, 0)
    row_of[slots] = live

    def name_col(k, carry):
        col_of[k] = cols[0, 0, k]
        return carry

    lax.fori_loop(0, slots, name_col, 0)


def prepare(starts, cols, features):
    slots = cols.shape[2]
    return pl.pallas_call(
        prepare_kernel,
        out_shape=[
            jax.ShapeDtypeStruct((slots + 1,), jnp.int32),
            jax.ShapeDtypeStruct((slots,), jnp.int32),
            jax.ShapeDtypeStruct(features.shape, BF16),
        ],
        in_specs=[SMEM, SMEM, VMEM],
        out_specs=[SMEM, SMEM, VMEM],
        compiler_params=params(32),
    )(starts, cols, features)


def sparse_kernel(parts, outs, backward, row_of, col_of, here_ref, mine_ref, *refs):
    panel_refs = refs[:parts]
    values_ref = refs[parts]
    out_refs = refs[parts + 1 : parts + 1 + len(outs)]
    panel, values, total, panel_sem, values_sem = refs[parts + 1 + len(outs) :]
    slots, size, _ = values.shape
    live, here, mine = row_of[slots], here_ref[0], mine_ref[0]
    chunk = panel_refs[0].shape[0]
    loads = []
    for m in range(parts):
        start = pl.multiple_of((here ^ m) * chunk, chunk)
        copy = pltpu.make_async_copy(
            panel_refs[m], panel.at[pl.ds(start, chunk)], panel_sem.at[m]
        )
        copy.start()
        loads.append(copy)

    def load(g):
        span = pl.ds(pl.multiple_of(g * GROUP, GROUP), GROUP)
        return pltpu.make_async_copy(values_ref.at[span], values.at[span], values_sem.at[g])

    def begin(g, carry):
        load(g).start()
        return carry

    used = (live + GROUP - 1) // GROUP
    lax.fori_loop(0, used, begin, 0)
    total[...] = jnp.zeros_like(total)
    for copy in loads:
        copy.wait()
    spare = total.shape[0] // size - 1
    last = panel.shape[0] // size - 1

    def step(g, carry):
        load(g).wait()
        for u in range(GROUP):
            k = g * GROUP + u
            row, col = row_of[k], col_of[k]
            to, source = (col, jnp.minimum(row, last)) if backward else (row, col)
            to = pl.multiple_of(jnp.where(k < live, to, spare) * size, size)
            source = pl.multiple_of(source * size, size)
            term = lax.dot_general(
                values[k],
                panel[pl.ds(source, size), :],
                (((0 if backward else 1,), (0,)), ((), ())),
                preferred_element_type=F32,
            )
            total[pl.ds(to, size), :] += term
        return carry

    lax.fori_loop(0, used, step, 0)
    for out_ref, members in zip(out_refs, outs):
        rows = out_ref.shape[0] // len(members)
        for at, m in enumerate(members):
            start = pl.multiple_of((mine ^ m) * rows, rows)
            out_ref[at * rows : (at + 1) * rows, :] = total[pl.ds(start, rows), :].astype(
                out_ref.dtype
            )


def sparse_product(panel_parts, values, row_of, col_of, here, mine, blocks, outs, backward):
    parts = len(panel_parts)
    slots, size, _ = values.shape
    chunk, width = panel_parts[0].shape
    flops = 2 * slots * size * size * width
    return pl.pallas_call(
        functools.partial(sparse_kernel, parts, outs, backward),
        out_shape=[jax.ShapeDtypeStruct((chunk * len(members), width), BF16) for members in outs],
        in_specs=[SMEM] * 4 + [ANY] * (parts + 1),
        out_specs=[VMEM] * len(outs),
        scratch_shapes=[
            pltpu.VMEM((parts * chunk, width), BF16),
            pltpu.VMEM((slots, size, size), BF16),
            pltpu.VMEM(((blocks + 1) * size, width), F32),
            pltpu.SemaphoreType.DMA((parts,)),
            pltpu.SemaphoreType.DMA((slots // GROUP,)),
        ],
        compiler_params=params(48),
        cost_estimate=cost(flops, 2 * values.size + 2 * parts * chunk * width),
    )(row_of, col_of, here, mine, *panel_parts, values)


def split(value):
    high = value.astype(BF16)
    return high, (value - high.astype(F32)).astype(BF16)


def mm(a, b, dims):
    return lax.dot_general(a, b, (dims, ((), ())), preferred_element_type=F32)


def middle_kernel(count, *refs):
    terms = refs[:count]
    weight_ref, cotangent_ref, act_ref, back_ref, agg_ref, grad_ref = refs[count:]
    aggregated = terms[0][...].astype(F32)
    for term in terms[1:]:
        aggregated += term[...].astype(F32)
    agg_ref[...] = aggregated
    weight = weight_ref[...]
    high, low = split(aggregated)
    mixed = mm(high, weight, ((1,), (0,))) + mm(low, weight, ((1,), (0,)))
    sigma = jax.nn.sigmoid(mixed)
    act_ref[...] = (mixed * sigma).astype(BF16)
    mixed_grad = cotangent_ref[...].astype(F32) * (sigma * (1.0 + mixed * (1.0 - sigma)))
    grad_ref[...] = mixed_grad
    high, low = split(mixed_grad)
    back = mm(high, weight, ((1,), (1,))) + mm(low, weight, ((1,), (1,)))
    back_ref[...] = back.astype(BF16)


def middle(terms, weight, cotangent):
    rows, width = cotangent.shape
    return pl.pallas_call(
        functools.partial(middle_kernel, len(terms)),
        out_shape=[
            jax.ShapeDtypeStruct((rows, width), BF16),
            jax.ShapeDtypeStruct((rows, width), BF16),
            jax.ShapeDtypeStruct((rows, width), F32),
            jax.ShapeDtypeStruct((rows, width), F32),
        ],
        in_specs=[VMEM] * (len(terms) + 2),
        out_specs=[VMEM] * 4,
        compiler_params=params(40),
        cost_estimate=cost(8 * rows * width * width, 20 * rows * width),
    )(*terms, weight, cotangent)


def weight_kernel(agg_ref, grad_ref, out_ref):
    high, low = split(agg_ref[...])
    grad_high, grad_low = split(grad_ref[...])
    contract = ((0,), (0,))
    out_ref[...] = (
        mm(high, grad_high, contract) + mm(low, grad_high, contract) + mm(high, grad_low, contract)
    )


def weight_term(aggregated, mixed_grad):
    rows, width = aggregated.shape
    return pl.pallas_call(
        weight_kernel,
        out_shape=jax.ShapeDtypeStruct((width, width), F32),
        in_specs=[VMEM, VMEM],
        out_specs=VMEM,
        compiler_params=params(40),
        cost_estimate=cost(6 * rows * width * width, 8 * rows * width),
    )(aggregated, mixed_grad)


def assemble_kernel(parts, me, *refs):
    out_ref = refs[parts]
    depth = refs[0].shape[0] // 2
    for p in range(parts):
        for core in range(2):
            start = pl.multiple_of((me[0] ^ (2 * p + core)) * depth, depth)
            out_ref[pl.ds(start, depth), :] = refs[p][core * depth : (core + 1) * depth, :]


def assemble(parts, me):
    depth, width = parts[0].shape
    return pl.pallas_call(
        functools.partial(assemble_kernel, len(parts)),
        out_shape=jax.ShapeDtypeStruct((depth * len(parts), width), F32),
        in_specs=[SMEM] + [VMEM] * len(parts),
        out_specs=VMEM,
        compiler_params=params(32),
    )(me, *parts)


def pair_kernel(count, own_ref, other_ref, *outs):
    rows = own_ref.shape[0] // count
    for m in range(count):
        span = slice(m * rows, (m + 1) * rows)
        outs[m][...] = (own_ref[span, :].astype(F32) + other_ref[span, :].astype(F32)).astype(BF16)


def pair_sum(own, other, count):
    rows, width = own.shape
    return pl.pallas_call(
        functools.partial(pair_kernel, count),
        out_shape=[jax.ShapeDtypeStruct((rows // count, width), BF16)] * count,
        in_specs=[VMEM] * 2,
        out_specs=[VMEM] * count,
        compiler_params=params(40),
        cost_estimate=cost(rows * width, 6 * rows * width),
    )(own, other)


def swap(x, axis, n, m):
    return lax.ppermute(x, axis, [(i, i ^ m) for i in range(n)])


def total_of(terms):
    result = terms[0].astype(F32)
    for term in terms[1:]:
        result = result + term.astype(F32)
    return result


def exchange(x, axis):
    return lax.all_to_all(x, axis, 0, 0, tiled=True)


def on_device(n_row, n_col, features, weight, block_cols, row_starts, block_values, cotangent):
    values = block_values[0, 0]
    size = values.shape[1]
    row_blocks = row_starts.shape[2] - 1
    col_blocks = n_row * features.shape[0] // size
    me_row = lax.axis_index("row")[None].astype(jnp.int32)
    me_col = lax.axis_index("col")[None].astype(jnp.int32)

    panel = [features] + [None] * (n_row - 1)
    for m in range(2, n_row, 2):
        panel[m] = swap(features, "row", n_row, m)
    prepared = prepare(row_starts, block_cols, features)
    panel[2], (row_of, col_of, panel[0]) = lax.optimization_barrier((panel[2], prepared))
    for m in range(0, n_row, 2):
        panel[m + 1] = swap(panel[m], "row", n_row, 1)

    each = [[m] for m in range(n_col)]
    terms = sparse_product(panel, values, row_of, col_of, me_row, me_col, row_blocks, each, False)
    terms = [terms[0]] + [swap(terms[m], "col", n_col, m) for m in range(1, n_col)]
    activations, back, aggregated, mixed_grad = middle(terms, weight, cotangent)

    back_panel = [back] + [swap(back, "col", n_col, m) for m in range(1, n_col)]

    depth = weight.shape[0] // n_row
    piece = exchange(weight_term(aggregated, mixed_grad), "row")
    piece = jnp.sum(piece.reshape(n_row, depth, -1), axis=0)
    piece, back_panel[0] = lax.optimization_barrier((piece, back_panel[0]))
    piece = total_of([piece] + [swap(piece, "col", n_col, m) for m in range(1, n_col)])
    piece = jnp.concatenate([piece, swap(piece, "row", n_row, 1)])
    gathered = [piece] + [swap(piece, "row", n_row, m) for m in range(2, n_row, 2)]

    even = list(range(0, n_row, 2))
    pair = [even, [m + 1 for m in even]]
    own, other = sparse_product(
        back_panel, values, row_of, col_of, me_col, me_row, col_blocks, pair, True
    )
    sums = pair_sum(own, swap(other, "row", n_row, 1), len(even))
    feature_grad = total_of(
        [sums[0]] + [swap(s, "row", n_row, m) for s, m in zip(sums[1:], even[1:])]
    ).astype(BF16)
    weight_grad = assemble(gathered, me_row)
    return (activations, feature_grad, weight_grad)


def solution(mesh):
    placed = (
        P(("col", "row"), None),
        P(),
        P("row", "col", None),
        P("row", "col", None),
        P("row", "col", None, None, None),
        P(("row", "col"), None),
    )
    return jax.shard_map(
        functools.partial(on_device, mesh.shape["row"], mesh.shape["col"]),
        mesh=mesh,
        in_specs=placed,
        out_specs=(P(("row", "col"), None), P(("col", "row"), None), P()),
        check_vma=False,
    )
```

```python
import functools

import jax
import jax.numpy as jnp
from jax import lax
from jax.experimental import pallas as pl
from jax.experimental.pallas import tpu as pltpu
from jax.sharding import PartitionSpec as P

F32 = jnp.float32
BF16 = jnp.bfloat16
GROUP = 8
ANY = pl.BlockSpec(memory_space=pl.ANY)
VMEM = pl.BlockSpec(memory_space=pltpu.VMEM)
SMEM = pl.BlockSpec(memory_space=pltpu.SMEM)


def params(mib):
    return pltpu.CompilerParams(vmem_limit_bytes=mib << 20)


def cost(flops, nbytes):
    return pl.CostEstimate(flops=flops, bytes_accessed=nbytes, transcendentals=0)


def prepare_kernel(starts, cols, features, row_of, col_of, own):
    own[...] = features[...]
    slots = cols.shape[2]
    row_blocks = starts.shape[2] - 1

    def name_row(i, carry):
        def name_slot(k, carry):
            row_of[k] = i
            return carry

        return lax.fori_loop(starts[0, 0, i], starts[0, 0, i + 1], name_slot, carry)

    lax.fori_loop(0, row_blocks, name_row, 0)
    live = starts[0, 0, row_blocks]

    def name_dead(k, carry):
        row_of[k] = row_blocks
        return carry

    lax.fori_loop(live, slots, name_dead, 0)
    row_of[slots] = live

    def name_col(k, carry):
        col_of[k] = cols[0, 0, k]
        return carry

    lax.fori_loop(0, slots, name_col, 0)


def prepare(starts, cols, features):
    slots = cols.shape[2]
    return pl.pallas_call(
        prepare_kernel,
        out_shape=[
            jax.ShapeDtypeStruct((slots + 1,), jnp.int32),
            jax.ShapeDtypeStruct((slots,), jnp.int32),
            jax.ShapeDtypeStruct(features.shape, BF16),
        ],
        in_specs=[SMEM, SMEM, VMEM],
        out_specs=[SMEM, SMEM, VMEM],
        compiler_params=params(32),
    )(starts, cols, features)


def sparse_kernel(parts, outs, backward, row_of, col_of, here_ref, mine_ref, *refs):
    panel_refs = refs[:parts]
    values_ref = refs[parts]
    out_refs = refs[parts + 1 : parts + 1 + len(outs)]
    panel, values, total, panel_sem, values_sem = refs[parts + 1 + len(outs) :]
    slots, size, _ = values.shape
    live, here, mine = row_of[slots], here_ref[0], mine_ref[0]
    chunk = panel_refs[0].shape[0]
    loads = []
    for m in range(parts):
        start = pl.multiple_of((here ^ m) * chunk, chunk)
        copy = pltpu.make_async_copy(
            panel_refs[m], panel.at[pl.ds(start, chunk)], panel_sem.at[m]
        )
        copy.start()
        loads.append(copy)

    def load(g):
        span = pl.ds(pl.multiple_of(g * GROUP, GROUP), GROUP)
        return pltpu.make_async_copy(values_ref.at[span], values.at[span], values_sem.at[g])

    def begin(g, carry):
        load(g).start()
        return carry

    used = (live + GROUP - 1) // GROUP
    lax.fori_loop(0, used, begin, 0)
    total[...] = jnp.zeros_like(total)
    for copy in loads:
        copy.wait()
    spare = total.shape[0] // size - 1
    last = panel.shape[0] // size - 1

    def step(g, carry):
        load(g).wait()
        for u in range(GROUP):
            k = g * GROUP + u
            row, col = row_of[k], col_of[k]
            to, source = (col, jnp.minimum(row, last)) if backward else (row, col)
            to = pl.multiple_of(jnp.where(k < live, to, spare) * size, size)
            source = pl.multiple_of(source * size, size)
            term = lax.dot_general(
                values[k],
                panel[pl.ds(source, size), :],
                (((0 if backward else 1,), (0,)), ((), ())),
                preferred_element_type=F32,
            )
            total[pl.ds(to, size), :] += term
        return carry

    lax.fori_loop(0, used, step, 0)
    for out_ref, members in zip(out_refs, outs):
        rows = out_ref.shape[0] // len(members)
        for at, m in enumerate(members):
            start = pl.multiple_of((mine ^ m) * rows, rows)
            out_ref[at * rows : (at + 1) * rows, :] = total[pl.ds(start, rows), :].astype(
                out_ref.dtype
            )


def sparse_product(panel_parts, values, row_of, col_of, here, mine, blocks, outs, backward):
    parts = len(panel_parts)
    slots, size, _ = values.shape
    chunk, width = panel_parts[0].shape
    flops = 2 * slots * size * size * width
    return pl.pallas_call(
        functools.partial(sparse_kernel, parts, outs, backward),
        out_shape=[jax.ShapeDtypeStruct((chunk * len(members), width), BF16) for members in outs],
        in_specs=[SMEM] * 4 + [ANY] * (parts + 1),
        out_specs=[VMEM] * len(outs),
        scratch_shapes=[
            pltpu.VMEM((parts * chunk, width), BF16),
            pltpu.VMEM((slots, size, size), BF16),
            pltpu.VMEM(((blocks + 1) * size, width), F32),
            pltpu.SemaphoreType.DMA((parts,)),
            pltpu.SemaphoreType.DMA((slots // GROUP,)),
        ],
        compiler_params=params(48),
        cost_estimate=cost(flops, 2 * values.size + 2 * parts * chunk * width),
    )(row_of, col_of, here, mine, *panel_parts, values)


def split(value):
    high = value.astype(BF16)
    return high, (value - high.astype(F32)).astype(BF16)


def mm(a, b, dims):
    return lax.dot_general(a, b, (dims, ((), ())), preferred_element_type=F32)


def middle_kernel(count, *refs):
    terms = refs[:count]
    weight_ref, cotangent_ref, act_ref, back_ref, agg_ref, grad_ref = refs[count:]
    aggregated = terms[0][...].astype(F32)
    for term in terms[1:]:
        aggregated += term[...].astype(F32)
    agg_ref[...] = aggregated
    weight = weight_ref[...]
    high, low = split(aggregated)
    mixed = mm(high, weight, ((1,), (0,))) + mm(low, weight, ((1,), (0,)))
    sigma = jax.nn.sigmoid(mixed)
    act_ref[...] = (mixed * sigma).astype(BF16)
    mixed_grad = cotangent_ref[...].astype(F32) * (sigma * (1.0 + mixed * (1.0 - sigma)))
    grad_ref[...] = mixed_grad
    high, low = split(mixed_grad)
    back = mm(high, weight, ((1,), (1,))) + mm(low, weight, ((1,), (1,)))
    back_ref[...] = back.astype(BF16)


def middle(terms, weight, cotangent):
    rows, width = cotangent.shape
    return pl.pallas_call(
        functools.partial(middle_kernel, len(terms)),
        out_shape=[
            jax.ShapeDtypeStruct((rows, width), BF16),
            jax.ShapeDtypeStruct((rows, width), BF16),
            jax.ShapeDtypeStruct((rows, width), F32),
            jax.ShapeDtypeStruct((rows, width), F32),
        ],
        in_specs=[VMEM] * (len(terms) + 2),
        out_specs=[VMEM] * 4,
        compiler_params=params(40),
        cost_estimate=cost(8 * rows * width * width, 20 * rows * width),
    )(*terms, weight, cotangent)


def weight_kernel(chunks, me, agg_ref, grad_ref, own_ref, other_ref, scratch):
    high, low = split(agg_ref[...])
    grad_high, grad_low = split(grad_ref[...])
    contract = ((0,), (0,))
    scratch[...] = (
        mm(high, grad_high, contract) + mm(low, grad_high, contract) + mm(high, grad_low, contract)
    )
    depth = scratch.shape[0] // chunks
    for c in range(chunks // 2):
        for ref, other in ((own_ref, 0), (other_ref, 1)):
            start = pl.multiple_of((2 * c + (me[0] % 2 ^ other)) * depth, depth)
            ref[c * depth : (c + 1) * depth, :] = scratch[pl.ds(start, depth), :]


def weight_term(aggregated, mixed_grad, me, chunks):
    rows, width = aggregated.shape
    return pl.pallas_call(
        functools.partial(weight_kernel, chunks),
        out_shape=[jax.ShapeDtypeStruct((width // 2, width), F32)] * 2,
        in_specs=[SMEM, VMEM, VMEM],
        out_specs=[VMEM, VMEM],
        scratch_shapes=[pltpu.VMEM((width, width), F32)],
        compiler_params=params(40),
        cost_estimate=cost(6 * rows * width * width, 8 * rows * width),
    )(me, aggregated, mixed_grad)


def assemble_kernel(parts, me, *refs):
    out_ref = refs[parts]
    depth = refs[0].shape[0] // 2
    for p in range(parts):
        for core in range(2):
            start = pl.multiple_of((me[0] ^ (2 * p + core)) * depth, depth)
            out_ref[pl.ds(start, depth), :] = refs[p][core * depth : (core + 1) * depth, :]


def assemble(parts, me):
    depth, width = parts[0].shape
    return pl.pallas_call(
        functools.partial(assemble_kernel, len(parts)),
        out_shape=jax.ShapeDtypeStruct((depth * len(parts), width), F32),
        in_specs=[SMEM] + [VMEM] * len(parts),
        out_specs=VMEM,
        compiler_params=params(32),
    )(me, *parts)


def pair_kernel(count, own_ref, other_ref, *outs):
    rows = own_ref.shape[0] // count
    for m in range(count):
        span = slice(m * rows, (m + 1) * rows)
        outs[m][...] = (own_ref[span, :].astype(F32) + other_ref[span, :].astype(F32)).astype(BF16)


def pair_sum(own, other, count):
    rows, width = own.shape
    return pl.pallas_call(
        functools.partial(pair_kernel, count),
        out_shape=[jax.ShapeDtypeStruct((rows // count, width), BF16)] * count,
        in_specs=[VMEM] * 2,
        out_specs=[VMEM] * count,
        compiler_params=params(40),
        cost_estimate=cost(rows * width, 6 * rows * width),
    )(own, other)


def swap(x, axis, n, m):
    return lax.ppermute(x, axis, [(i, i ^ m) for i in range(n)])


def total_of(terms):
    result = terms[0].astype(F32)
    for term in terms[1:]:
        result = result + term.astype(F32)
    return result


def exchange(x, axis):
    return lax.all_to_all(x, axis, 0, 0, tiled=True)


def on_device(n_row, n_col, features, weight, block_cols, row_starts, block_values, cotangent):
    values = block_values[0, 0]
    size = values.shape[1]
    row_blocks = row_starts.shape[2] - 1
    col_blocks = n_row * features.shape[0] // size
    me_row = lax.axis_index("row")[None].astype(jnp.int32)
    me_col = lax.axis_index("col")[None].astype(jnp.int32)

    panel = [features] + [None] * (n_row - 1)
    for m in range(2, n_row, 2):
        panel[m] = swap(features, "row", n_row, m)
    prepared = prepare(row_starts, block_cols, features)
    panel[2], (row_of, col_of, panel[0]) = lax.optimization_barrier((panel[2], prepared))
    for m in range(0, n_row, 2):
        panel[m + 1] = swap(panel[m], "row", n_row, 1)

    each = [[m] for m in range(n_col)]
    terms = sparse_product(panel, values, row_of, col_of, me_row, me_col, row_blocks, each, False)
    terms = [terms[0]] + [swap(terms[m], "col", n_col, m) for m in range(1, n_col)]
    activations, back, aggregated, mixed_grad = middle(terms, weight, cotangent)

    back_panel = [back] + [swap(back, "col", n_col, m) for m in range(1, n_col)]

    depth = weight.shape[0] // n_row
    own_term, other_term = weight_term(aggregated, mixed_grad, me_row, n_row)
    term = own_term + swap(other_term, "row", n_row, 1)
    cores = [list(range(0, n_row, 2)), list(range(1, n_row, 2))]
    term = lax.all_to_all(term, "row", 0, 0, axis_index_groups=cores, tiled=True)
    piece = jnp.sum(term.reshape(n_row // 2, depth, -1), axis=0)
    piece = lax.all_gather(piece, "col", axis=0, tiled=True)
    piece, back_panel[0] = lax.optimization_barrier((piece, back_panel[0]))
    piece = jnp.sum(piece.reshape(n_col, depth, -1), axis=0)

    even = list(range(0, n_row, 2))
    pair = [even, [m + 1 for m in even]]
    own, other = sparse_product(
        back_panel, values, row_of, col_of, me_col, me_row, col_blocks, pair, True
    )
    sums = pair_sum(own, swap(other, "row", n_row, 1), len(even))
    feature_grad = total_of(
        [sums[0]] + [swap(s, "row", n_row, m) for s, m in zip(sums[1:], even[1:])]
    ).astype(BF16)
    weight_grad = lax.all_gather(piece, 'row', axis=0, tiled=True)
    return (activations, feature_grad, weight_grad)


def solution(mesh):
    placed = (
        P(("col", "row"), None),
        P(),
        P("row", "col", None),
        P("row", "col", None),
        P("row", "col", None, None, None),
        P(("row", "col"), None),
    )
    return jax.shard_map(
        functools.partial(on_device, mesh.shape["row"], mesh.shape["col"]),
        mesh=mesh,
        in_specs=placed,
        out_specs=(P(("row", "col"), None), P(("col", "row"), None), P()),
        check_vma=False,
    )
```

```python
import functools

import jax
import jax.numpy as jnp
from jax import lax
from jax.experimental import pallas as pl
from jax.experimental.pallas import tpu as pltpu
from jax.sharding import PartitionSpec as P

F32 = jnp.float32
BF16 = jnp.bfloat16
GROUP = 8
ANY = pl.BlockSpec(memory_space=pl.ANY)
VMEM = pl.BlockSpec(memory_space=pltpu.VMEM)
SMEM = pl.BlockSpec(memory_space=pltpu.SMEM)


def params(mib):
    return pltpu.CompilerParams(vmem_limit_bytes=mib << 20)


def cost(flops, nbytes):
    return pl.CostEstimate(flops=flops, bytes_accessed=nbytes, transcendentals=0)


def prepare_kernel(starts, cols, features, row_of, col_of, own):
    own[...] = features[...]
    slots = cols.shape[2]
    row_blocks = starts.shape[2] - 1

    def name_row(i, carry):
        def name_slot(k, carry):
            row_of[k] = i
            return carry

        return lax.fori_loop(starts[0, 0, i], starts[0, 0, i + 1], name_slot, carry)

    lax.fori_loop(0, row_blocks, name_row, 0)
    live = starts[0, 0, row_blocks]

    def name_dead(k, carry):
        row_of[k] = row_blocks
        return carry

    lax.fori_loop(live, slots, name_dead, 0)
    row_of[slots] = live

    def name_col(k, carry):
        col_of[k] = cols[0, 0, k]
        return carry

    lax.fori_loop(0, slots, name_col, 0)


def prepare(starts, cols, features):
    slots = cols.shape[2]
    return pl.pallas_call(
        prepare_kernel,
        out_shape=[
            jax.ShapeDtypeStruct((slots + 1,), jnp.int32),
            jax.ShapeDtypeStruct((slots,), jnp.int32),
            jax.ShapeDtypeStruct(features.shape, BF16),
        ],
        in_specs=[SMEM, SMEM, VMEM],
        out_specs=[SMEM, SMEM, VMEM],
        compiler_params=params(32),
    )(starts, cols, features)


def sparse_kernel(parts, outs, backward, row_of, col_of, here_ref, mine_ref, *refs):
    panel_refs = refs[:parts]
    values_ref = refs[parts]
    out_refs = refs[parts + 1 : parts + 1 + len(outs)]
    panel, values, total, panel_sem, values_sem = refs[parts + 1 + len(outs) :]
    slots, size, _ = values.shape
    live, here, mine = row_of[slots], here_ref[0], mine_ref[0]
    chunk = panel_refs[0].shape[0]
    loads = []
    for m in range(parts):
        start = pl.multiple_of((here ^ m) * chunk, chunk)
        copy = pltpu.make_async_copy(
            panel_refs[m], panel.at[pl.ds(start, chunk)], panel_sem.at[m]
        )
        copy.start()
        loads.append(copy)

    def load(g):
        span = pl.ds(pl.multiple_of(g * GROUP, GROUP), GROUP)
        return pltpu.make_async_copy(values_ref.at[span], values.at[span], values_sem.at[g])

    def begin(g, carry):
        load(g).start()
        return carry

    used = (live + GROUP - 1) // GROUP
    lax.fori_loop(0, used, begin, 0)
    total[...] = jnp.zeros_like(total)
    for copy in loads:
        copy.wait()
    spare = total.shape[0] // size - 1
    last = panel.shape[0] // size - 1

    def step(g, carry):
        load(g).wait()
        for u in range(GROUP):
            k = g * GROUP + u
            row, col = row_of[k], col_of[k]
            to, source = (col, jnp.minimum(row, last)) if backward else (row, col)
            to = pl.multiple_of(jnp.where(k < live, to, spare) * size, size)
            source = pl.multiple_of(source * size, size)
            term = lax.dot_general(
                values[k],
                panel[pl.ds(source, size), :],
                (((0 if backward else 1,), (0,)), ((), ())),
                preferred_element_type=F32,
            )
            total[pl.ds(to, size), :] += term
        return carry

    lax.fori_loop(0, used, step, 0)
    for out_ref, members in zip(out_refs, outs):
        rows = out_ref.shape[0] // len(members)
        for at, m in enumerate(members):
            start = pl.multiple_of((mine ^ m) * rows, rows)
            out_ref[at * rows : (at + 1) * rows, :] = total[pl.ds(start, rows), :].astype(
                out_ref.dtype
            )


def sparse_product(panel_parts, values, row_of, col_of, here, mine, blocks, outs, backward):
    parts = len(panel_parts)
    slots, size, _ = values.shape
    chunk, width = panel_parts[0].shape
    flops = 2 * slots * size * size * width
    return pl.pallas_call(
        functools.partial(sparse_kernel, parts, outs, backward),
        out_shape=[jax.ShapeDtypeStruct((chunk * len(members), width), BF16) for members in outs],
        in_specs=[SMEM] * 4 + [ANY] * (parts + 1),
        out_specs=[VMEM] * len(outs),
        scratch_shapes=[
            pltpu.VMEM((parts * chunk, width), BF16),
            pltpu.VMEM((slots, size, size), BF16),
            pltpu.VMEM(((blocks + 1) * size, width), F32),
            pltpu.SemaphoreType.DMA((parts,)),
            pltpu.SemaphoreType.DMA((slots // GROUP,)),
        ],
        compiler_params=params(48),
        cost_estimate=cost(flops, 2 * values.size + 2 * parts * chunk * width),
    )(row_of, col_of, here, mine, *panel_parts, values)


def split(value):
    high = value.astype(BF16)
    return high, (value - high.astype(F32)).astype(BF16)


def mm(a, b, dims):
    return lax.dot_general(a, b, (dims, ((), ())), preferred_element_type=F32)


def middle_kernel(count, *refs):
    terms = refs[:count]
    weight_ref, cotangent_ref, act_ref, back_ref, agg_ref, grad_ref = refs[count:]
    aggregated = terms[0][...].astype(F32)
    for term in terms[1:]:
        aggregated += term[...].astype(F32)
    agg_ref[...] = aggregated
    weight = weight_ref[...]
    high, low = split(aggregated)
    mixed = mm(high, weight, ((1,), (0,))) + mm(low, weight, ((1,), (0,)))
    sigma = jax.nn.sigmoid(mixed)
    act_ref[...] = (mixed * sigma).astype(BF16)
    mixed_grad = cotangent_ref[...].astype(F32) * (sigma * (1.0 + mixed * (1.0 - sigma)))
    grad_ref[...] = mixed_grad
    high, low = split(mixed_grad)
    back = mm(high, weight, ((1,), (1,))) + mm(low, weight, ((1,), (1,)))
    back_ref[...] = back.astype(BF16)


def middle(terms, weight, cotangent):
    rows, width = cotangent.shape
    return pl.pallas_call(
        functools.partial(middle_kernel, len(terms)),
        out_shape=[
            jax.ShapeDtypeStruct((rows, width), BF16),
            jax.ShapeDtypeStruct((rows, width), BF16),
            jax.ShapeDtypeStruct((rows, width), F32),
            jax.ShapeDtypeStruct((rows, width), F32),
        ],
        in_specs=[VMEM] * (len(terms) + 2),
        out_specs=[VMEM] * 4,
        compiler_params=params(40),
        cost_estimate=cost(8 * rows * width * width, 20 * rows * width),
    )(*terms, weight, cotangent)


def weight_kernel(chunks, me, agg_ref, grad_ref, own_ref, other_ref, scratch):
    high, low = split(agg_ref[...])
    grad_high, grad_low = split(grad_ref[...])
    contract = ((0,), (0,))
    scratch[...] = (
        mm(high, grad_high, contract) + mm(low, grad_high, contract) + mm(high, grad_low, contract)
    )
    depth = scratch.shape[0] // chunks
    for c in range(chunks // 2):
        for ref, other in ((own_ref, 0), (other_ref, 1)):
            start = pl.multiple_of((2 * c + (me[0] % 2 ^ other)) * depth, depth)
            ref[c * depth : (c + 1) * depth, :] = scratch[pl.ds(start, depth), :]


def weight_term(aggregated, mixed_grad, me, chunks):
    rows, width = aggregated.shape
    return pl.pallas_call(
        functools.partial(weight_kernel, chunks),
        out_shape=[jax.ShapeDtypeStruct((width // 2, width), F32)] * 2,
        in_specs=[SMEM, VMEM, VMEM],
        out_specs=[VMEM, VMEM],
        scratch_shapes=[pltpu.VMEM((width, width), F32)],
        compiler_params=params(40),
        cost_estimate=cost(6 * rows * width * width, 8 * rows * width),
    )(me, aggregated, mixed_grad)


def assemble_kernel(chunks, me, own_ref, other_ref, out_ref):
    depth = own_ref.shape[0] // chunks
    for c in range(chunks):
        for ref, other in ((own_ref, 0), (other_ref, 1)):
            start = pl.multiple_of((2 * c + (me[0] % 2 ^ other)) * depth, depth)
            out_ref[pl.ds(start, depth), :] = ref[c * depth : (c + 1) * depth, :]


def assemble(own, other, me, chunks):
    depth, width = own.shape
    return pl.pallas_call(
        functools.partial(assemble_kernel, chunks),
        out_shape=jax.ShapeDtypeStruct((2 * depth, width), own.dtype),
        in_specs=[SMEM, VMEM, VMEM],
        out_specs=VMEM,
        compiler_params=params(32),
    )(me, own, other)


def pair_kernel(count, own_ref, other_ref, *outs):
    rows = own_ref.shape[0] // count
    for m in range(count):
        span = slice(m * rows, (m + 1) * rows)
        outs[m][...] = (own_ref[span, :].astype(F32) + other_ref[span, :].astype(F32)).astype(BF16)


def pair_sum(own, other, count):
    rows, width = own.shape
    return pl.pallas_call(
        functools.partial(pair_kernel, count),
        out_shape=[jax.ShapeDtypeStruct((rows // count, width), BF16)] * count,
        in_specs=[VMEM] * 2,
        out_specs=[VMEM] * count,
        compiler_params=params(40),
        cost_estimate=cost(rows * width, 6 * rows * width),
    )(own, other)


def swap(x, axis, n, m):
    return lax.ppermute(x, axis, [(i, i ^ m) for i in range(n)])


def total_of(terms):
    result = terms[0].astype(F32)
    for term in terms[1:]:
        result = result + term.astype(F32)
    return result


def exchange(x, axis):
    return lax.all_to_all(x, axis, 0, 0, tiled=True)


def on_device(n_row, n_col, features, weight, block_cols, row_starts, block_values, cotangent):
    values = block_values[0, 0]
    size = values.shape[1]
    row_blocks = row_starts.shape[2] - 1
    col_blocks = n_row * features.shape[0] // size
    me_row = lax.axis_index("row")[None].astype(jnp.int32)
    me_col = lax.axis_index("col")[None].astype(jnp.int32)

    panel = [features] + [None] * (n_row - 1)
    for m in range(2, n_row, 2):
        panel[m] = swap(features, "row", n_row, m)
    prepared = prepare(row_starts, block_cols, features)
    panel[2], (row_of, col_of, panel[0]) = lax.optimization_barrier((panel[2], prepared))
    for m in range(0, n_row, 2):
        panel[m + 1] = swap(panel[m], "row", n_row, 1)

    each = [[m] for m in range(n_col)]
    terms = sparse_product(panel, values, row_of, col_of, me_row, me_col, row_blocks, each, False)
    terms = [terms[0]] + [swap(terms[m], "col", n_col, m) for m in range(1, n_col)]
    activations, back, aggregated, mixed_grad = middle(terms, weight, cotangent)

    back_panel = [back] + [swap(back, "col", n_col, m) for m in range(1, n_col)]

    depth = weight.shape[0] // n_row
    own_term, other_term = weight_term(aggregated, mixed_grad, me_row, n_row)
    term = own_term + swap(other_term, "row", n_row, 1)
    cores = [list(range(0, n_row, 2)), list(range(1, n_row, 2))]
    term = lax.all_to_all(term, "row", 0, 0, axis_index_groups=cores, tiled=True)
    piece = jnp.sum(term.reshape(n_row // 2, depth, -1), axis=0)
    half = lax.all_gather(piece, "row", axis=0, axis_index_groups=cores, tiled=True)
    half, back_panel[0] = lax.optimization_barrier((half, back_panel[0]))

    even = list(range(0, n_row, 2))
    pair = [even, [m + 1 for m in even]]
    own, other = sparse_product(
        back_panel, values, row_of, col_of, me_col, me_row, col_blocks, pair, True
    )
    sums = pair_sum(own, swap(other, "row", n_row, 1), len(even))
    feature_grad = total_of(
        [sums[0]] + [swap(s, "row", n_row, m) for s, m in zip(sums[1:], even[1:])]
    ).astype(BF16)
    halves = lax.all_gather(half.astype(BF16), "col", axis=0, tiled=True)
    half = jnp.sum(halves.reshape(n_col, -1, half.shape[1]).astype(F32), axis=0)
    weight_grad = assemble(half, swap(half, "row", n_row, 1), me_row, n_row // 2)
    return (activations, feature_grad, weight_grad)


def solution(mesh):
    placed = (
        P(("col", "row"), None),
        P(),
        P("row", "col", None),
        P("row", "col", None),
        P("row", "col", None, None, None),
        P(("row", "col"), None),
    )
    return jax.shard_map(
        functools.partial(on_device, mesh.shape["row"], mesh.shape["col"]),
        mesh=mesh,
        in_specs=placed,
        out_specs=(P(("row", "col"), None), P(("col", "row"), None), P()),
        check_vma=False,
    )
```

```python
import functools

import jax
import jax.numpy as jnp
from jax import lax
from jax.experimental import pallas as pl
from jax.experimental.pallas import tpu as pltpu
from jax.sharding import PartitionSpec as P

F32 = jnp.float32
BF16 = jnp.bfloat16
GROUP = 8
LONG = 32
ANY = pl.BlockSpec(memory_space=pl.ANY)
VMEM = pl.BlockSpec(memory_space=pltpu.VMEM)
SMEM = pl.BlockSpec(memory_space=pltpu.SMEM)


def params(mib):
    return pltpu.CompilerParams(vmem_limit_bytes=mib << 20)


def cost(flops, nbytes):
    return pl.CostEstimate(flops=flops, bytes_accessed=nbytes, transcendentals=0)


def prepare_kernel(starts, cols, features, row_of, col_of, own):
    own[...] = features[...]
    slots = cols.shape[2]
    row_blocks = starts.shape[2] - 1

    def name_row(i, carry):
        def name_slot(k, carry):
            row_of[k] = i
            return carry

        return lax.fori_loop(starts[0, 0, i], starts[0, 0, i + 1], name_slot, carry)

    lax.fori_loop(0, row_blocks, name_row, 0)
    live = starts[0, 0, row_blocks]

    def name_dead(k, carry):
        row_of[k] = row_blocks
        return carry

    lax.fori_loop(live, slots, name_dead, 0)
    row_of[slots] = live

    def name_col(k, carry):
        col_of[k] = cols[0, 0, k]
        return carry

    lax.fori_loop(0, slots, name_col, 0)


def prepare(starts, cols, features):
    slots = cols.shape[2]
    return pl.pallas_call(
        prepare_kernel,
        out_shape=[
            jax.ShapeDtypeStruct((slots + 1,), jnp.int32),
            jax.ShapeDtypeStruct((slots,), jnp.int32),
            jax.ShapeDtypeStruct(features.shape, BF16),
        ],
        in_specs=[SMEM, SMEM, VMEM],
        out_specs=[SMEM, SMEM, VMEM],
        compiler_params=params(32),
    )(starts, cols, features)


def sparse_kernel(parts, outs, backward, row_of, col_of, here_ref, mine_ref, *refs):
    panel_refs = refs[:parts]
    values_ref = refs[parts]
    out_refs = refs[parts + 1 : parts + 1 + len(outs)]
    panel, values, total, values_sem = refs[parts + 1 + len(outs) :]
    slots, size, _ = values.shape
    live, here, mine = row_of[slots], here_ref[0], mine_ref[0]
    chunk = panel_refs[0].shape[0]
    def load(g):
        span = pl.ds(pl.multiple_of(g * GROUP, GROUP), GROUP)
        return pltpu.make_async_copy(values_ref.at[span], values.at[span], values_sem.at[g])

    def begin(g, carry):
        load(g).start()
        return carry

    used = (live + GROUP - 1) // GROUP
    lax.fori_loop(0, used, begin, 0)
    total[...] = jnp.zeros_like(total)
    for m in range(parts):
        start = pl.multiple_of((here ^ m) * chunk, chunk)
        panel[pl.ds(start, chunk), :] = panel_refs[m][...]
    spare = total.shape[0] // size - 1
    last = panel.shape[0] // size - 1

    def add_slot(k):
        row, col = row_of[k], col_of[k]
        to, source = (col, jnp.minimum(row, last)) if backward else (row, col)
        to = pl.multiple_of(jnp.where(k < live, to, spare) * size, size)
        source = pl.multiple_of(source * size, size)
        term = lax.dot_general(
            values[k],
            panel[pl.ds(source, size), :],
            (((0 if backward else 1,), (0,)), ((), ())),
            preferred_element_type=F32,
        )
        total[pl.ds(to, size), :] += term

    def steps(count):
        def step(g, carry):
            for part in range(count // GROUP):
                load(g * (count // GROUP) + part).wait()
            for u in range(count):
                add_slot(g * count + u)
            return carry

        return step

    long = live // LONG
    lax.fori_loop(0, long, steps(LONG), 0)
    lax.fori_loop(long * (LONG // GROUP), used, steps(GROUP), 0)
    for out_ref, members in zip(out_refs, outs):
        rows = out_ref.shape[0] // len(members)
        for at, m in enumerate(members):
            start = pl.multiple_of((mine ^ m) * rows, rows)
            out_ref[at * rows : (at + 1) * rows, :] = total[pl.ds(start, rows), :].astype(
                out_ref.dtype
            )


def sparse_product(panel_parts, values, row_of, col_of, here, mine, blocks, outs, backward):
    parts = len(panel_parts)
    slots, size, _ = values.shape
    chunk, width = panel_parts[0].shape
    flops = 2 * slots * size * size * width
    return pl.pallas_call(
        functools.partial(sparse_kernel, parts, outs, backward),
        out_shape=[jax.ShapeDtypeStruct((chunk * len(members), width), BF16) for members in outs],
        in_specs=[SMEM] * 4 + [VMEM] * parts + [ANY],
        out_specs=[VMEM] * len(outs),
        scratch_shapes=[
            pltpu.VMEM((parts * chunk, width), BF16),
            pltpu.VMEM((slots, size, size), BF16),
            pltpu.VMEM(((blocks + 1) * size, width), F32),
            pltpu.SemaphoreType.DMA((slots // GROUP,)),
        ],
        compiler_params=params(48),
        cost_estimate=cost(flops, 2 * values.size + 2 * parts * chunk * width),
    )(row_of, col_of, here, mine, *panel_parts, values)


def split(value):
    high = value.astype(BF16)
    return high, (value - high.astype(F32)).astype(BF16)


def mm(a, b, dims):
    return lax.dot_general(a, b, (dims, ((), ())), preferred_element_type=F32)


def middle_kernel(count, *refs):
    terms = refs[:count]
    weight_ref, cotangent_ref, act_ref, back_ref, agg_ref, grad_ref = refs[count:]
    aggregated = terms[0][...].astype(F32)
    for term in terms[1:]:
        aggregated += term[...].astype(F32)
    agg_ref[...] = aggregated
    weight = weight_ref[...]
    high, low = split(aggregated)
    mixed = mm(high, weight, ((1,), (0,))) + mm(low, weight, ((1,), (0,)))
    sigma = jax.nn.sigmoid(mixed)
    act_ref[...] = (mixed * sigma).astype(BF16)
    mixed_grad = cotangent_ref[...].astype(F32) * (sigma * (1.0 + mixed * (1.0 - sigma)))
    grad_ref[...] = mixed_grad
    high, low = split(mixed_grad)
    back = mm(high, weight, ((1,), (1,))) + mm(low, weight, ((1,), (1,)))
    back_ref[...] = back.astype(BF16)


def middle(terms, weight, cotangent):
    rows, width = cotangent.shape
    return pl.pallas_call(
        functools.partial(middle_kernel, len(terms)),
        out_shape=[
            jax.ShapeDtypeStruct((rows, width), BF16),
            jax.ShapeDtypeStruct((rows, width), BF16),
            jax.ShapeDtypeStruct((rows, width), F32),
            jax.ShapeDtypeStruct((rows, width), F32),
        ],
        in_specs=[VMEM] * (len(terms) + 2),
        out_specs=[VMEM] * 4,
        compiler_params=params(40),
        cost_estimate=cost(8 * rows * width * width, 20 * rows * width),
    )(*terms, weight, cotangent)


def weight_kernel(chunks, me, agg_ref, grad_ref, own_ref, other_ref, scratch):
    high, low = split(agg_ref[...])
    grad_high, grad_low = split(grad_ref[...])
    contract = ((0,), (0,))
    scratch[...] = (
        mm(high, grad_high, contract) + mm(low, grad_high, contract) + mm(high, grad_low, contract)
    )
    depth = scratch.shape[0] // chunks
    for c in range(chunks // 2):
        for ref, other in ((own_ref, 0), (other_ref, 1)):
            start = pl.multiple_of((2 * c + (me[0] % 2 ^ other)) * depth, depth)
            ref[c * depth : (c + 1) * depth, :] = scratch[pl.ds(start, depth), :]


def weight_term(aggregated, mixed_grad, me, chunks):
    rows, width = aggregated.shape
    return pl.pallas_call(
        functools.partial(weight_kernel, chunks),
        out_shape=[jax.ShapeDtypeStruct((width // 2, width), F32)] * 2,
        in_specs=[SMEM, VMEM, VMEM],
        out_specs=[VMEM, VMEM],
        scratch_shapes=[pltpu.VMEM((width, width), F32)],
        compiler_params=params(40),
        cost_estimate=cost(6 * rows * width * width, 8 * rows * width),
    )(me, aggregated, mixed_grad)


def assemble_kernel(chunks, me, own_ref, other_ref, out_ref):
    depth = own_ref.shape[0] // chunks
    for c in range(chunks):
        for ref, other in ((own_ref, 0), (other_ref, 1)):
            start = pl.multiple_of((2 * c + (me[0] % 2 ^ other)) * depth, depth)
            out_ref[pl.ds(start, depth), :] = ref[c * depth : (c + 1) * depth, :]


def assemble(own, other, me, chunks):
    depth, width = own.shape
    return pl.pallas_call(
        functools.partial(assemble_kernel, chunks),
        out_shape=jax.ShapeDtypeStruct((2 * depth, width), own.dtype),
        in_specs=[SMEM, VMEM, VMEM],
        out_specs=VMEM,
        compiler_params=params(32),
    )(me, own, other)


def pair_kernel(count, own_ref, other_ref, *outs):
    rows = own_ref.shape[0] // count
    for m in range(count):
        span = slice(m * rows, (m + 1) * rows)
        outs[m][...] = (own_ref[span, :].astype(F32) + other_ref[span, :].astype(F32)).astype(BF16)


def pair_sum(own, other, count):
    rows, width = own.shape
    return pl.pallas_call(
        functools.partial(pair_kernel, count),
        out_shape=[jax.ShapeDtypeStruct((rows // count, width), BF16)] * count,
        in_specs=[VMEM] * 2,
        out_specs=[VMEM] * count,
        compiler_params=params(40),
        cost_estimate=cost(rows * width, 6 * rows * width),
    )(own, other)


def swap(x, axis, n, m):
    return lax.ppermute(x, axis, [(i, i ^ m) for i in range(n)])


def total_of(terms):
    result = terms[0].astype(F32)
    for term in terms[1:]:
        result = result + term.astype(F32)
    return result


def exchange(x, axis):
    return lax.all_to_all(x, axis, 0, 0, tiled=True)


def on_device(n_row, n_col, features, weight, block_cols, row_starts, block_values, cotangent):
    values = block_values[0, 0]
    size = values.shape[1]
    row_blocks = row_starts.shape[2] - 1
    col_blocks = n_row * features.shape[0] // size
    me_row = lax.axis_index("row")[None].astype(jnp.int32)
    me_col = lax.axis_index("col")[None].astype(jnp.int32)

    panel = [features] + [None] * (n_row - 1)
    for m in range(2, n_row, 2):
        panel[m] = swap(features, "row", n_row, m)
    prepared = prepare(row_starts, block_cols, features)
    panel[2], (row_of, col_of, panel[0]) = lax.optimization_barrier((panel[2], prepared))
    for m in range(0, n_row, 2):
        panel[m + 1] = swap(panel[m], "row", n_row, 1)

    each = [[m] for m in range(n_col)]
    terms = sparse_product(panel, values, row_of, col_of, me_row, me_col, row_blocks, each, False)
    terms = [terms[0]] + [swap(terms[m], "col", n_col, m) for m in range(1, n_col)]
    activations, back, aggregated, mixed_grad = middle(terms, weight, cotangent)

    back_panel = [back] + [swap(back, "col", n_col, m) for m in range(1, n_col)]

    depth = weight.shape[0] // n_row
    own_term, other_term = weight_term(aggregated, mixed_grad, me_row, n_row)
    term = own_term + swap(other_term, "row", n_row, 1)
    cores = [list(range(0, n_row, 2)), list(range(1, n_row, 2))]
    term = lax.all_to_all(term, "row", 0, 0, axis_index_groups=cores, tiled=True)
    piece = jnp.sum(term.reshape(n_row // 2, depth, -1), axis=0)
    half = lax.all_gather(piece, "row", axis=0, axis_index_groups=cores, tiled=True)
    half, back_panel[0] = lax.optimization_barrier((half, back_panel[0]))

    even = list(range(0, n_row, 2))
    pair = [even, [m + 1 for m in even]]
    own, other = sparse_product(
        back_panel, values, row_of, col_of, me_col, me_row, col_blocks, pair, True
    )
    sums = pair_sum(own, swap(other, "row", n_row, 1), len(even))
    feature_grad = total_of(
        [sums[0]] + [swap(s, "row", n_row, m) for s, m in zip(sums[1:], even[1:])]
    ).astype(BF16)
    halves = lax.all_gather(half.astype(BF16), "col", axis=0, tiled=True)
    half = jnp.sum(halves.reshape(n_col, -1, half.shape[1]).astype(F32), axis=0)
    weight_grad = assemble(half, swap(half, "row", n_row, 1), me_row, n_row // 2)
    return (activations, feature_grad, weight_grad)


def solution(mesh):
    placed = (
        P(("col", "row"), None),
        P(),
        P("row", "col", None),
        P("row", "col", None),
        P("row", "col", None, None, None),
        P(("row", "col"), None),
    )
    return jax.shard_map(
        functools.partial(on_device, mesh.shape["row"], mesh.shape["col"]),
        mesh=mesh,
        in_specs=placed,
        out_specs=(P(("row", "col"), None), P(("col", "row"), None), P()),
        check_vma=False,
    )
```

```python
import functools

import jax
import jax.numpy as jnp
from jax import lax
from jax.experimental import pallas as pl
from jax.experimental.pallas import tpu as pltpu
from jax.sharding import PartitionSpec as P

F32 = jnp.float32
BF16 = jnp.bfloat16
GROUP = 8
LONG = 32
ANY = pl.BlockSpec(memory_space=pl.ANY)
VMEM = pl.BlockSpec(memory_space=pltpu.VMEM)
SMEM = pl.BlockSpec(memory_space=pltpu.SMEM)


def params(mib):
    return pltpu.CompilerParams(vmem_limit_bytes=mib << 20)


def cost(flops, nbytes):
    return pl.CostEstimate(flops=flops, bytes_accessed=nbytes, transcendentals=0)


def prepare_kernel(starts, cols, features, row_of, col_of, own):
    own[...] = features[...]
    slots = cols.shape[2]
    row_blocks = starts.shape[2] - 1

    def name_row(i, carry):
        def name_slot(k, carry):
            row_of[k] = i
            return carry

        return lax.fori_loop(starts[0, 0, i], starts[0, 0, i + 1], name_slot, carry)

    lax.fori_loop(0, row_blocks, name_row, 0)
    live = starts[0, 0, row_blocks]

    def name_dead(k, carry):
        row_of[k] = row_blocks
        return carry

    lax.fori_loop(live, slots, name_dead, 0)
    row_of[slots] = live

    def name_col(k, carry):
        col_of[k] = cols[0, 0, k]
        return carry

    lax.fori_loop(0, slots, name_col, 0)


def prepare(starts, cols, features):
    slots = cols.shape[2]
    return pl.pallas_call(
        prepare_kernel,
        out_shape=[
            jax.ShapeDtypeStruct((slots + 1,), jnp.int32),
            jax.ShapeDtypeStruct((slots,), jnp.int32),
            jax.ShapeDtypeStruct(features.shape, BF16),
        ],
        in_specs=[SMEM, SMEM, VMEM],
        out_specs=[SMEM, SMEM, VMEM],
        compiler_params=params(32),
    )(starts, cols, features)


def sparse_kernel(parts, outs, backward, row_of, col_of, here_ref, mine_ref, *refs):
    panel_refs = refs[:parts]
    values_ref = refs[parts]
    out_refs = refs[parts + 1 : parts + 1 + len(outs)]
    panel, values, total, values_sem = refs[parts + 1 + len(outs) :]
    slots, size, _ = values.shape
    live, here, mine = row_of[slots], here_ref[0], mine_ref[0]
    chunk = panel_refs[0].shape[0]
    def load(g):
        span = pl.ds(pl.multiple_of(g * GROUP, GROUP), GROUP)
        return pltpu.make_async_copy(values_ref.at[span], values.at[span], values_sem.at[g])

    def begin(g, carry):
        load(g).start()
        return carry

    used = (live + GROUP - 1) // GROUP
    lax.fori_loop(0, used, begin, 0)
    total[...] = jnp.zeros_like(total)
    for m in range(parts):
        start = pl.multiple_of((here ^ m) * chunk, chunk)
        panel[pl.ds(start, chunk), :] = panel_refs[parts - 1 - m][...]
    spare = total.shape[0] // size - 1
    last = panel.shape[0] // size - 1

    def add_slot(k):
        row, col = row_of[k], col_of[k]
        to, source = (col, jnp.minimum(row, last)) if backward else (row, col)
        to = pl.multiple_of(jnp.where(k < live, to, spare) * size, size)
        source = pl.multiple_of(source * size, size)
        term = lax.dot_general(
            values[k],
            panel[pl.ds(source, size), :],
            (((0 if backward else 1,), (0,)), ((), ())),
            preferred_element_type=F32,
        )
        total[pl.ds(to, size), :] += term

    def steps(count):
        def step(g, carry):
            for part in range(count // GROUP):
                load(g * (count // GROUP) + part).wait()
            for u in range(count):
                add_slot(g * count + u)
            return carry

        return step

    long = live // LONG
    lax.fori_loop(0, long, steps(LONG), 0)
    lax.fori_loop(long * (LONG // GROUP), used, steps(GROUP), 0)
    for out_ref, members in zip(out_refs, outs):
        rows = out_ref.shape[0] // len(members)
        for at, m in enumerate(members):
            start = pl.multiple_of((mine ^ m) * rows, rows)
            out_ref[at * rows : (at + 1) * rows, :] = total[pl.ds(start, rows), :].astype(
                out_ref.dtype
            )


def sparse_product(panel_parts, values, row_of, col_of, here, mine, blocks, outs, backward):
    parts = len(panel_parts)
    slots, size, _ = values.shape
    chunk, width = panel_parts[0].shape
    flops = 2 * slots * size * size * width
    return pl.pallas_call(
        functools.partial(sparse_kernel, parts, outs, backward),
        out_shape=[jax.ShapeDtypeStruct((chunk * len(members), width), BF16) for members in outs],
        in_specs=[SMEM] * 4 + [VMEM] * parts + [ANY],
        out_specs=[VMEM] * len(outs),
        scratch_shapes=[
            pltpu.VMEM((parts * chunk, width), BF16),
            pltpu.VMEM((slots, size, size), BF16),
            pltpu.VMEM(((blocks + 1) * size, width), F32),
            pltpu.SemaphoreType.DMA((slots // GROUP,)),
        ],
        compiler_params=params(48),
        cost_estimate=cost(flops, 2 * values.size + 2 * parts * chunk * width),
    )(row_of, col_of, here, mine, *panel_parts[::-1], values)


def split(value):
    high = value.astype(BF16)
    return high, (value - high.astype(F32)).astype(BF16)


def mm(a, b, dims):
    return lax.dot_general(a, b, (dims, ((), ())), preferred_element_type=F32)


def middle_kernel(count, *refs):
    terms = refs[:count]
    weight_ref, cotangent_ref, act_ref, back_ref, agg_ref, grad_ref = refs[count:]
    aggregated = terms[0][...].astype(F32)
    for term in terms[1:]:
        aggregated += term[...].astype(F32)
    agg_ref[...] = aggregated
    weight = weight_ref[...]
    high, low = split(aggregated)
    mixed = mm(high, weight, ((1,), (0,))) + mm(low, weight, ((1,), (0,)))
    sigma = jax.nn.sigmoid(mixed)
    act_ref[...] = (mixed * sigma).astype(BF16)
    mixed_grad = cotangent_ref[...].astype(F32) * (sigma * (1.0 + mixed * (1.0 - sigma)))
    grad_ref[...] = mixed_grad
    high, low = split(mixed_grad)
    back = mm(high, weight, ((1,), (1,))) + mm(low, weight, ((1,), (1,)))
    back_ref[...] = back.astype(BF16)


def middle(terms, weight, cotangent):
    rows, width = cotangent.shape
    return pl.pallas_call(
        functools.partial(middle_kernel, len(terms)),
        out_shape=[
            jax.ShapeDtypeStruct((rows, width), BF16),
            jax.ShapeDtypeStruct((rows, width), BF16),
            jax.ShapeDtypeStruct((rows, width), F32),
            jax.ShapeDtypeStruct((rows, width), F32),
        ],
        in_specs=[VMEM] * (len(terms) + 2),
        out_specs=[VMEM] * 4,
        compiler_params=params(40),
        cost_estimate=cost(8 * rows * width * width, 20 * rows * width),
    )(*terms, weight, cotangent)


def weight_kernel(chunks, me, agg_ref, grad_ref, own_ref, other_ref, scratch):
    high, low = split(agg_ref[...])
    grad_high, grad_low = split(grad_ref[...])
    contract = ((0,), (0,))
    scratch[...] = (
        mm(high, grad_high, contract) + mm(low, grad_high, contract) + mm(high, grad_low, contract)
    )
    depth = scratch.shape[0] // chunks
    for c in range(chunks // 2):
        for ref, other in ((own_ref, 0), (other_ref, 1)):
            start = pl.multiple_of((2 * c + (me[0] % 2 ^ other)) * depth, depth)
            ref[c * depth : (c + 1) * depth, :] = scratch[pl.ds(start, depth), :]


def weight_term(aggregated, mixed_grad, me, chunks):
    rows, width = aggregated.shape
    return pl.pallas_call(
        functools.partial(weight_kernel, chunks),
        out_shape=[jax.ShapeDtypeStruct((width // 2, width), F32)] * 2,
        in_specs=[SMEM, VMEM, VMEM],
        out_specs=[VMEM, VMEM],
        scratch_shapes=[pltpu.VMEM((width, width), F32)],
        compiler_params=params(40),
        cost_estimate=cost(6 * rows * width * width, 8 * rows * width),
    )(me, aggregated, mixed_grad)


def assemble_kernel(chunks, me, own_ref, other_ref, out_ref):
    depth = own_ref.shape[0] // chunks
    for c in range(chunks):
        for ref, other in ((own_ref, 0), (other_ref, 1)):
            start = pl.multiple_of((2 * c + (me[0] % 2 ^ other)) * depth, depth)
            out_ref[pl.ds(start, depth), :] = ref[c * depth : (c + 1) * depth, :]


def assemble(own, other, me, chunks):
    depth, width = own.shape
    return pl.pallas_call(
        functools.partial(assemble_kernel, chunks),
        out_shape=jax.ShapeDtypeStruct((2 * depth, width), own.dtype),
        in_specs=[SMEM, VMEM, VMEM],
        out_specs=VMEM,
        compiler_params=params(32),
    )(me, own, other)


def pair_kernel(count, own_ref, other_ref, *outs):
    rows = own_ref.shape[0] // count
    for m in range(count):
        span = slice(m * rows, (m + 1) * rows)
        outs[m][...] = (own_ref[span, :].astype(F32) + other_ref[span, :].astype(F32)).astype(BF16)


def pair_sum(own, other, count):
    rows, width = own.shape
    return pl.pallas_call(
        functools.partial(pair_kernel, count),
        out_shape=[jax.ShapeDtypeStruct((rows // count, width), BF16)] * count,
        in_specs=[VMEM] * 2,
        out_specs=[VMEM] * count,
        compiler_params=params(40),
        cost_estimate=cost(rows * width, 6 * rows * width),
    )(own, other)


def swap(x, axis, n, m):
    return lax.ppermute(x, axis, [(i, i ^ m) for i in range(n)])


def total_of(terms):
    result = terms[0].astype(F32)
    for term in terms[1:]:
        result = result + term.astype(F32)
    return result


def exchange(x, axis):
    return lax.all_to_all(x, axis, 0, 0, tiled=True)


def on_device(n_row, n_col, features, weight, block_cols, row_starts, block_values, cotangent):
    values = block_values[0, 0]
    size = values.shape[1]
    row_blocks = row_starts.shape[2] - 1
    col_blocks = n_row * features.shape[0] // size
    me_row = lax.axis_index("row")[None].astype(jnp.int32)
    me_col = lax.axis_index("col")[None].astype(jnp.int32)

    panel = [features] + [None] * (n_row - 1)
    for m in range(n_row - 2, 0, -2):
        panel[m] = swap(features, "row", n_row, m)
    prepared = prepare(row_starts, block_cols, features)
    panel[n_row - 2], (row_of, col_of, panel[0]) = lax.optimization_barrier(
        (panel[n_row - 2], prepared)
    )
    for m in range(0, n_row, 2):
        panel[m + 1] = swap(panel[m], "row", n_row, 1)

    each = [[m] for m in range(n_col)]
    terms = sparse_product(panel, values, row_of, col_of, me_row, me_col, row_blocks, each, False)
    terms = [terms[0]] + [swap(terms[m], "col", n_col, m) for m in range(n_col - 1, 0, -1)]
    activations, back, aggregated, mixed_grad = middle(terms, weight, cotangent)

    back_panel = [back] + [swap(back, "col", n_col, m) for m in range(n_col - 1, 0, -1)][::-1]

    depth = weight.shape[0] // n_row
    own_term, other_term = weight_term(aggregated, mixed_grad, me_row, n_row)
    term = own_term + swap(other_term, "row", n_row, 1)
    cores = [list(range(0, n_row, 2)), list(range(1, n_row, 2))]
    term = lax.all_to_all(term, "row", 0, 0, axis_index_groups=cores, tiled=True)
    piece = jnp.sum(term.reshape(n_row // 2, depth, -1), axis=0)
    half = lax.all_gather(piece, "row", axis=0, axis_index_groups=cores, tiled=True)
    half, back_panel[0] = lax.optimization_barrier((half, back_panel[0]))

    even = list(range(0, n_row, 2))
    pair = [even, [m + 1 for m in even]]
    own, other = sparse_product(
        back_panel, values, row_of, col_of, me_col, me_row, col_blocks, pair, True
    )
    sums = pair_sum(own, swap(other, "row", n_row, 1), len(even))
    feature_grad = total_of(
        [swap(s, "row", n_row, m) for s, m in zip(sums[:0:-1], even[:0:-1])] + [sums[0]]
    ).astype(BF16)
    halves = lax.all_gather(half.astype(BF16), "col", axis=0, tiled=True)
    half = jnp.sum(halves.reshape(n_col, -1, half.shape[1]).astype(F32), axis=0)
    other = swap(half, "row", n_row, 1)
    other, feature_grad = lax.optimization_barrier((other, feature_grad))
    weight_grad = assemble(half, other, me_row, n_row // 2)
    return (activations, feature_grad, weight_grad)


def solution(mesh):
    placed = (
        P(("col", "row"), None),
        P(),
        P("row", "col", None),
        P("row", "col", None),
        P("row", "col", None, None, None),
        P(("row", "col"), None),
    )
    return jax.shard_map(
        functools.partial(on_device, mesh.shape["row"], mesh.shape["col"]),
        mesh=mesh,
        in_specs=placed,
        out_specs=(P(("row", "col"), None), P(("col", "row"), None), P()),
        check_vma=False,
    )
```

```python
import functools

import jax
import jax.numpy as jnp
from jax import lax
from jax.experimental import pallas as pl
from jax.experimental.pallas import tpu as pltpu
from jax.sharding import PartitionSpec as P

F32 = jnp.float32
BF16 = jnp.bfloat16
GROUP = 8
LONG = 32
ANY = pl.BlockSpec(memory_space=pl.ANY)
VMEM = pl.BlockSpec(memory_space=pltpu.VMEM)
SMEM = pl.BlockSpec(memory_space=pltpu.SMEM)


def params(mib):
    return pltpu.CompilerParams(vmem_limit_bytes=mib << 20)


def cost(flops, nbytes):
    return pl.CostEstimate(flops=flops, bytes_accessed=nbytes, transcendentals=0)


def prepare_kernel(starts, cols, features, row_of, col_of, own):
    own[...] = features[...]
    slots = cols.shape[2]
    row_blocks = starts.shape[2] - 1

    def name_row(i, carry):
        def name_slot(k, carry):
            row_of[k] = i
            return carry

        return lax.fori_loop(starts[0, 0, i], starts[0, 0, i + 1], name_slot, carry)

    lax.fori_loop(0, row_blocks, name_row, 0)
    live = starts[0, 0, row_blocks]

    def name_dead(k, carry):
        row_of[k] = row_blocks
        return carry

    lax.fori_loop(live, slots, name_dead, 0)
    row_of[slots] = live

    def name_col(k, carry):
        col_of[k] = cols[0, 0, k]
        return carry

    lax.fori_loop(0, slots, name_col, 0)


def prepare(starts, cols, features):
    slots = cols.shape[2]
    return pl.pallas_call(
        prepare_kernel,
        out_shape=[
            jax.ShapeDtypeStruct((slots + 1,), jnp.int32),
            jax.ShapeDtypeStruct((slots,), jnp.int32),
            jax.ShapeDtypeStruct(features.shape, BF16),
        ],
        in_specs=[SMEM, SMEM, VMEM],
        out_specs=[SMEM, SMEM, VMEM],
        compiler_params=params(32),
    )(starts, cols, features)


def sparse_kernel(parts, outs, backward, row_of, col_of, here_ref, mine_ref, *refs):
    panel_refs = refs[:parts]
    values_ref = refs[parts]
    out_refs = refs[parts + 1 : parts + 1 + len(outs)]
    panel, values, total, values_sem = refs[parts + 1 + len(outs) :]
    slots, size, _ = values.shape
    live, here, mine = row_of[slots], here_ref[0], mine_ref[0]
    chunk = panel_refs[0].shape[0]
    def load(g):
        span = pl.ds(pl.multiple_of(g * GROUP, GROUP), GROUP)
        return pltpu.make_async_copy(values_ref.at[span], values.at[span], values_sem.at[g])

    def begin(g, carry):
        load(g).start()
        return carry

    used = (live + GROUP - 1) // GROUP
    lax.fori_loop(0, used, begin, 0)
    total[...] = jnp.zeros_like(total)
    for m in range(parts):
        start = pl.multiple_of((here ^ m) * chunk, chunk)
        panel[pl.ds(start, chunk), :] = panel_refs[parts - 1 - m][...]
    spare = total.shape[0] // size - 1
    last = panel.shape[0] // size - 1

    def add_slot(k):
        row, col = row_of[k], col_of[k]
        to, source = (col, jnp.minimum(row, last)) if backward else (row, col)
        to = pl.multiple_of(jnp.where(k < live, to, spare) * size, size)
        source = pl.multiple_of(source * size, size)
        term = lax.dot_general(
            values[k],
            panel[pl.ds(source, size), :],
            (((0 if backward else 1,), (0,)), ((), ())),
            preferred_element_type=F32,
        )
        total[pl.ds(to, size), :] += term

    def steps(count):
        def step(g, carry):
            for part in range(count // GROUP):
                load(g * (count // GROUP) + part).wait()
            for u in range(count):
                add_slot(g * count + u)
            return carry

        return step

    long = live // LONG
    lax.fori_loop(0, long, steps(LONG), 0)
    lax.fori_loop(long * (LONG // GROUP), used, steps(GROUP), 0)
    for out_ref, members in zip(out_refs, outs):
        rows = out_ref.shape[0] // len(members)
        for at, m in enumerate(members):
            start = pl.multiple_of((mine ^ m) * rows, rows)
            out_ref[at * rows : (at + 1) * rows, :] = total[pl.ds(start, rows), :].astype(
                out_ref.dtype
            )


def sparse_product(panel_parts, values, row_of, col_of, here, mine, blocks, outs, backward):
    parts = len(panel_parts)
    slots, size, _ = values.shape
    chunk, width = panel_parts[0].shape
    flops = 2 * slots * size * size * width
    return pl.pallas_call(
        functools.partial(sparse_kernel, parts, outs, backward),
        out_shape=[jax.ShapeDtypeStruct((chunk * len(members), width), BF16) for members in outs],
        in_specs=[SMEM] * 4 + [VMEM] * parts + [ANY],
        out_specs=[VMEM] * len(outs),
        scratch_shapes=[
            pltpu.VMEM((parts * chunk, width), BF16),
            pltpu.VMEM((slots, size, size), BF16),
            pltpu.VMEM(((blocks + 1) * size, width), F32),
            pltpu.SemaphoreType.DMA((slots // GROUP,)),
        ],
        compiler_params=params(48),
        cost_estimate=cost(flops, 2 * values.size + 2 * parts * chunk * width),
    )(row_of, col_of, here, mine, *panel_parts[::-1], values)


def split(value):
    high = value.astype(BF16)
    return high, (value - high.astype(F32)).astype(BF16)


def mm(a, b, dims):
    return lax.dot_general(a, b, (dims, ((), ())), preferred_element_type=F32)


def middle_kernel(count, *refs):
    terms = refs[:count]
    weight_ref, cotangent_ref, act_ref, back_ref, agg_ref, grad_ref = refs[count:]
    aggregated = terms[0][...].astype(F32)
    for term in terms[1:]:
        aggregated += term[...].astype(F32)
    agg_ref[...] = aggregated
    weight = weight_ref[...]
    high, low = split(aggregated)
    mixed = mm(high, weight, ((1,), (0,))) + mm(low, weight, ((1,), (0,)))
    sigma = jax.nn.sigmoid(mixed)
    act_ref[...] = (mixed * sigma).astype(BF16)
    mixed_grad = cotangent_ref[...].astype(F32) * (sigma * (1.0 + mixed * (1.0 - sigma)))
    grad_ref[...] = mixed_grad
    high, low = split(mixed_grad)
    back = mm(high, weight, ((1,), (1,))) + mm(low, weight, ((1,), (1,)))
    back_ref[...] = back.astype(BF16)


def middle(terms, weight, cotangent):
    rows, width = cotangent.shape
    return pl.pallas_call(
        functools.partial(middle_kernel, len(terms)),
        out_shape=[
            jax.ShapeDtypeStruct((rows, width), BF16),
            jax.ShapeDtypeStruct((rows, width), BF16),
            jax.ShapeDtypeStruct((rows, width), F32),
            jax.ShapeDtypeStruct((rows, width), F32),
        ],
        in_specs=[VMEM] * (len(terms) + 2),
        out_specs=[VMEM] * 4,
        compiler_params=params(40),
        cost_estimate=cost(8 * rows * width * width, 20 * rows * width),
    )(*terms, weight, cotangent)


def weight_kernel(chunks, me, agg_ref, grad_ref, own_ref, other_ref, scratch):
    high, low = split(agg_ref[...])
    grad_high, grad_low = split(grad_ref[...])
    contract = ((0,), (0,))
    scratch[...] = (
        mm(high, grad_high, contract) + mm(low, grad_high, contract) + mm(high, grad_low, contract)
    )
    depth = scratch.shape[0] // chunks
    for c in range(chunks // 2):
        for ref, other in ((own_ref, 0), (other_ref, 1)):
            start = pl.multiple_of((2 * c + (me[0] % 2 ^ other)) * depth, depth)
            ref[c * depth : (c + 1) * depth, :] = scratch[pl.ds(start, depth), :]


def weight_term(aggregated, mixed_grad, me, chunks):
    rows, width = aggregated.shape
    return pl.pallas_call(
        functools.partial(weight_kernel, chunks),
        out_shape=[jax.ShapeDtypeStruct((width // 2, width), F32)] * 2,
        in_specs=[SMEM, VMEM, VMEM],
        out_specs=[VMEM, VMEM],
        scratch_shapes=[pltpu.VMEM((width, width), F32)],
        compiler_params=params(40),
        cost_estimate=cost(6 * rows * width * width, 8 * rows * width),
    )(me, aggregated, mixed_grad)


def assemble_kernel(chunks, me, own_ref, other_ref, out_ref):
    depth = own_ref.shape[0] // chunks
    for c in range(chunks):
        for ref, other in ((own_ref, 0), (other_ref, 1)):
            start = pl.multiple_of((2 * c + (me[0] % 2 ^ other)) * depth, depth)
            out_ref[pl.ds(start, depth), :] = ref[c * depth : (c + 1) * depth, :]


def assemble(own, other, me, chunks):
    depth, width = own.shape
    return pl.pallas_call(
        functools.partial(assemble_kernel, chunks),
        out_shape=jax.ShapeDtypeStruct((2 * depth, width), own.dtype),
        in_specs=[SMEM, VMEM, VMEM],
        out_specs=VMEM,
        compiler_params=params(32),
    )(me, own, other)


def pair_kernel(count, own_ref, other_ref, *outs):
    rows = own_ref.shape[0] // count
    for m in range(count):
        span = slice(m * rows, (m + 1) * rows)
        outs[m][...] = (own_ref[span, :].astype(F32) + other_ref[span, :].astype(F32)).astype(BF16)


def pair_sum(own, other, count):
    rows, width = own.shape
    return pl.pallas_call(
        functools.partial(pair_kernel, count),
        out_shape=[jax.ShapeDtypeStruct((rows // count, width), BF16)] * count,
        in_specs=[VMEM] * 2,
        out_specs=[VMEM] * count,
        compiler_params=params(40),
        cost_estimate=cost(rows * width, 6 * rows * width),
    )(own, other)


def swap(x, axis, n, m):
    return lax.ppermute(x, axis, [(i, i ^ m) for i in range(n)])


def total_of(terms):
    result = terms[0].astype(F32)
    for term in terms[1:]:
        result = result + term.astype(F32)
    return result


def exchange(x, axis):
    return lax.all_to_all(x, axis, 0, 0, tiled=True)


def on_device(n_row, n_col, features, weight, block_cols, row_starts, block_values, cotangent):
    values = block_values[0, 0]
    size = values.shape[1]
    row_blocks = row_starts.shape[2] - 1
    col_blocks = n_row * features.shape[0] // size
    me_row = lax.axis_index("row")[None].astype(jnp.int32)
    me_col = lax.axis_index("col")[None].astype(jnp.int32)

    panel = [features] + [None] * (n_row - 1)
    for m in range(n_row - 2, 0, -2):
        panel[m] = swap(features, "row", n_row, m)
    prepared = prepare(row_starts, block_cols, features)
    panel[n_row - 2], (row_of, col_of, panel[0]) = lax.optimization_barrier(
        (panel[n_row - 2], prepared)
    )
    for m in range(0, n_row, 2):
        panel[m + 1] = swap(panel[m], "row", n_row, 1)

    each = [[m] for m in range(n_col)]
    terms = sparse_product(panel, values, row_of, col_of, me_row, me_col, row_blocks, each, False)
    terms = [terms[0]] + [swap(terms[m], "col", n_col, m) for m in range(n_col - 1, 0, -1)]
    activations, back, aggregated, mixed_grad = middle(terms, weight, cotangent)

    back_panel = [back] + [swap(back, "col", n_col, m) for m in range(n_col - 1, 0, -1)][::-1]

    depth = weight.shape[0] // n_row
    own_term, other_term = weight_term(aggregated, mixed_grad, me_row, n_row)
    term = own_term + swap(other_term, "row", n_row, 1)
    cores = [list(range(0, n_row, 2)), list(range(1, n_row, 2))]
    term = lax.all_to_all(term, "row", 0, 0, axis_index_groups=cores, tiled=True)
    piece = jnp.sum(term.reshape(n_row // 2, depth, -1), axis=0)
    half = lax.all_gather(piece, "row", axis=0, axis_index_groups=cores, tiled=True)
    half, back_panel[0] = lax.optimization_barrier((half, back_panel[0]))

    even = list(range(0, n_row, 2))
    pair = [even, [m + 1 for m in even]]
    own, other = sparse_product(
        back_panel, values, row_of, col_of, me_col, me_row, col_blocks, pair, True
    )
    sums = pair_sum(own, swap(other, "row", n_row, 1), len(even))
    feature_grad = total_of(
        [swap(s, "row", n_row, m) for s, m in zip(sums[:0:-1], even[:0:-1])] + [sums[0]]
    ).astype(BF16)
    halves = exchange(jnp.tile(half.astype(BF16), (n_col, 1)), "col")
    half = jnp.sum(halves.reshape(n_col, -1, half.shape[1]).astype(F32), axis=0)
    other = swap(half, "row", n_row, 1)
    other, feature_grad = lax.optimization_barrier((other, feature_grad))
    weight_grad = assemble(half, other, me_row, n_row // 2)
    return (activations, feature_grad, weight_grad)


def solution(mesh):
    placed = (
        P(("col", "row"), None),
        P(),
        P("row", "col", None),
        P("row", "col", None),
        P("row", "col", None, None, None),
        P(("row", "col"), None),
    )
    return jax.shard_map(
        functools.partial(on_device, mesh.shape["row"], mesh.shape["col"]),
        mesh=mesh,
        in_specs=placed,
        out_specs=(P(("row", "col"), None), P(("col", "row"), None), P()),
        check_vma=False,
    )
```

```python
import functools

import jax
import jax.numpy as jnp
from jax import lax
from jax.experimental import pallas as pl
from jax.experimental.pallas import tpu as pltpu
from jax.sharding import PartitionSpec as P

F32 = jnp.float32
BF16 = jnp.bfloat16
GROUP = 8
LONG = 32
ANY = pl.BlockSpec(memory_space=pl.ANY)
VMEM = pl.BlockSpec(memory_space=pltpu.VMEM)
SMEM = pl.BlockSpec(memory_space=pltpu.SMEM)


def params(mib):
    return pltpu.CompilerParams(vmem_limit_bytes=mib << 20)


def cost(flops, nbytes):
    return pl.CostEstimate(flops=flops, bytes_accessed=nbytes, transcendentals=0)


def prepare_kernel(starts, cols, features, row_of, col_of, own):
    own[...] = features[...]
    slots = cols.shape[2]
    row_blocks = starts.shape[2] - 1

    def name_row(i, carry):
        def name_slot(k, carry):
            row_of[k] = i
            return carry

        return lax.fori_loop(starts[0, 0, i], starts[0, 0, i + 1], name_slot, carry)

    lax.fori_loop(0, row_blocks, name_row, 0)
    live = starts[0, 0, row_blocks]

    def name_dead(k, carry):
        row_of[k] = row_blocks
        return carry

    lax.fori_loop(live, slots, name_dead, 0)
    row_of[slots] = live

    def name_col(k, carry):
        col_of[k] = cols[0, 0, k]
        return carry

    lax.fori_loop(0, slots, name_col, 0)


def prepare(starts, cols, features):
    slots = cols.shape[2]
    return pl.pallas_call(
        prepare_kernel,
        out_shape=[
            jax.ShapeDtypeStruct((slots + 1,), jnp.int32),
            jax.ShapeDtypeStruct((slots,), jnp.int32),
            jax.ShapeDtypeStruct(features.shape, BF16),
        ],
        in_specs=[SMEM, SMEM, VMEM],
        out_specs=[SMEM, SMEM, VMEM],
        compiler_params=params(32),
    )(starts, cols, features)


def sparse_kernel(parts, outs, backward, row_of, col_of, here_ref, mine_ref, *refs):
    panel_refs = refs[:parts]
    values_ref = refs[parts]
    out_refs = refs[parts + 1 : parts + 1 + len(outs)]
    panel, values, total, values_sem = refs[parts + 1 + len(outs) :]
    slots, size, _ = values.shape
    live, here, mine = row_of[slots], here_ref[0], mine_ref[0]
    chunk = panel_refs[0].shape[0]
    def load(g):
        span = pl.ds(pl.multiple_of(g * GROUP, GROUP), GROUP)
        return pltpu.make_async_copy(values_ref.at[span], values.at[span], values_sem.at[g])

    def begin(g, carry):
        load(g).start()
        return carry

    used = (live + GROUP - 1) // GROUP
    lax.fori_loop(0, used, begin, 0)
    total[...] = jnp.zeros_like(total)
    for m in range(parts):
        start = pl.multiple_of((here ^ m) * chunk, chunk)
        panel[pl.ds(start, chunk), :] = panel_refs[parts - 1 - m][...]
    spare = total.shape[0] // size - 1
    last = panel.shape[0] // size - 1

    def add_slot(k):
        row, col = row_of[k], col_of[k]
        to, source = (col, jnp.minimum(row, last)) if backward else (row, col)
        to = pl.multiple_of(jnp.where(k < live, to, spare) * size, size)
        source = pl.multiple_of(source * size, size)
        term = lax.dot_general(
            values[k],
            panel[pl.ds(source, size), :],
            (((0 if backward else 1,), (0,)), ((), ())),
            preferred_element_type=F32,
        )
        total[pl.ds(to, size), :] += term

    def steps(count):
        def step(g, carry):
            for part in range(count // GROUP):
                load(g * (count // GROUP) + part).wait()
            for u in range(count):
                add_slot(g * count + u)
            return carry

        return step

    long = live // LONG
    lax.fori_loop(0, long, steps(LONG), 0)
    lax.fori_loop(long * (LONG // GROUP), used, steps(GROUP), 0)
    for out_ref, members in zip(out_refs, outs):
        rows = out_ref.shape[0] // len(members)
        for at, m in enumerate(members):
            start = pl.multiple_of((mine ^ m) * rows, rows)
            out_ref[at * rows : (at + 1) * rows, :] = total[pl.ds(start, rows), :].astype(
                out_ref.dtype
            )


def sparse_product(panel_parts, values, row_of, col_of, here, mine, blocks, outs, backward):
    parts = len(panel_parts)
    slots, size, _ = values.shape
    chunk, width = panel_parts[0].shape
    flops = 2 * slots * size * size * width
    return pl.pallas_call(
        functools.partial(sparse_kernel, parts, outs, backward),
        out_shape=[jax.ShapeDtypeStruct((chunk * len(members), width), BF16) for members in outs],
        in_specs=[SMEM] * 4 + [VMEM] * parts + [ANY],
        out_specs=[VMEM] * len(outs),
        scratch_shapes=[
            pltpu.VMEM((parts * chunk, width), BF16),
            pltpu.VMEM((slots, size, size), BF16),
            pltpu.VMEM(((blocks + 1) * size, width), F32),
            pltpu.SemaphoreType.DMA((slots // GROUP,)),
        ],
        compiler_params=params(48),
        cost_estimate=cost(flops, 2 * values.size + 2 * parts * chunk * width),
    )(row_of, col_of, here, mine, *panel_parts[::-1], values)


def split(value):
    high = value.astype(BF16)
    return high, (value - high.astype(F32)).astype(BF16)


def mm(a, b, dims):
    return lax.dot_general(a, b, (dims, ((), ())), preferred_element_type=F32)


def middle_kernel(count, *refs):
    terms = refs[:count]
    weight_ref, cotangent_ref, act_ref, back_ref, agg_ref, grad_ref = refs[count:]
    aggregated = terms[0][...].astype(F32)
    for term in terms[1:]:
        aggregated += term[...].astype(F32)
    agg_ref[...] = aggregated
    weight = weight_ref[...]
    high, low = split(aggregated)
    mixed = mm(high, weight, ((1,), (0,))) + mm(low, weight, ((1,), (0,)))
    sigma = jax.nn.sigmoid(mixed)
    act_ref[...] = (mixed * sigma).astype(BF16)
    mixed_grad = cotangent_ref[...].astype(F32) * (sigma * (1.0 + mixed * (1.0 - sigma)))
    grad_ref[...] = mixed_grad
    high, low = split(mixed_grad)
    back = mm(high, weight, ((1,), (1,))) + mm(low, weight, ((1,), (1,)))
    back_ref[...] = back.astype(BF16)


def middle(terms, weight, cotangent):
    rows, width = cotangent.shape
    return pl.pallas_call(
        functools.partial(middle_kernel, len(terms)),
        out_shape=[
            jax.ShapeDtypeStruct((rows, width), BF16),
            jax.ShapeDtypeStruct((rows, width), BF16),
            jax.ShapeDtypeStruct((rows, width), F32),
            jax.ShapeDtypeStruct((rows, width), F32),
        ],
        in_specs=[VMEM] * (len(terms) + 2),
        out_specs=[VMEM] * 4,
        compiler_params=params(40),
        cost_estimate=cost(8 * rows * width * width, 20 * rows * width),
    )(*terms, weight, cotangent)


def weight_kernel(chunks, me, agg_ref, grad_ref, own_ref, other_ref, scratch):
    high, low = split(agg_ref[...])
    grad_high, grad_low = split(grad_ref[...])
    contract = ((0,), (0,))
    scratch[...] = (
        mm(high, grad_high, contract) + mm(low, grad_high, contract) + mm(high, grad_low, contract)
    )
    depth = scratch.shape[0] // chunks
    for c in range(chunks // 2):
        for ref, other in ((own_ref, 0), (other_ref, 1)):
            start = pl.multiple_of((2 * c + (me[0] % 2 ^ other)) * depth, depth)
            ref[c * depth : (c + 1) * depth, :] = scratch[pl.ds(start, depth), :]


def weight_term(aggregated, mixed_grad, me, chunks):
    rows, width = aggregated.shape
    return pl.pallas_call(
        functools.partial(weight_kernel, chunks),
        out_shape=[jax.ShapeDtypeStruct((width // 2, width), F32)] * 2,
        in_specs=[SMEM, VMEM, VMEM],
        out_specs=[VMEM, VMEM],
        scratch_shapes=[pltpu.VMEM((width, width), F32)],
        compiler_params=params(40),
        cost_estimate=cost(6 * rows * width * width, 8 * rows * width),
    )(me, aggregated, mixed_grad)


def assemble_kernel(chunks, me, own_ref, other_ref, out_ref):
    depth = own_ref.shape[0] // chunks
    for c in range(chunks):
        for ref, other in ((own_ref, 0), (other_ref, 1)):
            start = pl.multiple_of((2 * c + (me[0] % 2 ^ other)) * depth, depth)
            out_ref[pl.ds(start, depth), :] = ref[c * depth : (c + 1) * depth, :]


def assemble(own, other, me, chunks):
    depth, width = own.shape
    return pl.pallas_call(
        functools.partial(assemble_kernel, chunks),
        out_shape=jax.ShapeDtypeStruct((2 * depth, width), own.dtype),
        in_specs=[SMEM, VMEM, VMEM],
        out_specs=VMEM,
        compiler_params=params(32),
    )(me, own, other)


def pair_kernel(count, own_ref, other_ref, *outs):
    rows = own_ref.shape[0] // count
    for m in range(count):
        span = slice(m * rows, (m + 1) * rows)
        outs[m][...] = (own_ref[span, :].astype(F32) + other_ref[span, :].astype(F32)).astype(BF16)


def pair_sum(own, other, count):
    rows, width = own.shape
    return pl.pallas_call(
        functools.partial(pair_kernel, count),
        out_shape=[jax.ShapeDtypeStruct((rows // count, width), BF16)] * count,
        in_specs=[VMEM] * 2,
        out_specs=[VMEM] * count,
        compiler_params=params(40),
        cost_estimate=cost(rows * width, 6 * rows * width),
    )(own, other)


def swap(x, axis, n, m):
    return lax.ppermute(x, axis, [(i, i ^ m) for i in range(n)])


def add_kernel(*refs):
    result = refs[0][...].astype(F32)
    for ref in refs[1:-1]:
        result += ref[...].astype(F32)
    refs[-1][...] = result


def add_up(terms):
    return pl.pallas_call(
        add_kernel,
        out_shape=jax.ShapeDtypeStruct(terms[0].shape, F32),
        in_specs=[VMEM] * len(terms),
        out_specs=VMEM,
        compiler_params=params(32),
        cost_estimate=cost(0, 64 * terms[0].size),
    )(*terms)


def exchange_terms(terms, n):
    if n != 4:
        return [terms[0]] + [swap(terms[m], "col", n, m) for m in range(n - 1, 0, -1)]
    far = lax.ppermute(terms[3], "col", [(0, 1), (3, 2)])
    cross = lax.ppermute(terms[3], "col", [(1, 2), (2, 1)])
    inward = lax.ppermute(terms[2], "col", [(0, 2), (3, 1)])
    near = swap(terms[1], "col", n, 1)
    relay = total_of([terms[2], far]).astype(BF16)
    outward = lax.ppermute(relay, "col", [(1, 3), (2, 0)])
    return [add_up([cross, inward, near, terms[0]]), outward]


def total_of(terms):
    result = terms[0].astype(F32)
    for term in terms[1:]:
        result = result + term.astype(F32)
    return result


def exchange(x, axis):
    return lax.all_to_all(x, axis, 0, 0, tiled=True)


def on_device(n_row, n_col, features, weight, block_cols, row_starts, block_values, cotangent):
    values = block_values[0, 0]
    size = values.shape[1]
    row_blocks = row_starts.shape[2] - 1
    col_blocks = n_row * features.shape[0] // size
    me_row = lax.axis_index("row")[None].astype(jnp.int32)
    me_col = lax.axis_index("col")[None].astype(jnp.int32)

    panel = [features] + [None] * (n_row - 1)
    for m in range(n_row - 2, 0, -2):
        panel[m] = swap(features, "row", n_row, m)
    prepared = prepare(row_starts, block_cols, features)
    panel[n_row - 2], (row_of, col_of, panel[0]) = lax.optimization_barrier(
        (panel[n_row - 2], prepared)
    )
    for m in range(0, n_row, 2):
        panel[m + 1] = swap(panel[m], "row", n_row, 1)

    each = [[m] for m in range(n_col)]
    terms = sparse_product(panel, values, row_of, col_of, me_row, me_col, row_blocks, each, False)
    terms = exchange_terms(terms, n_col)
    activations, back, aggregated, mixed_grad = middle(terms, weight, cotangent)

    back_panel = [back] + [swap(back, "col", n_col, m) for m in range(n_col - 1, 0, -1)][::-1]

    depth = weight.shape[0] // n_row
    own_term, other_term = weight_term(aggregated, mixed_grad, me_row, n_row)
    term = own_term + swap(other_term, "row", n_row, 1)
    cores = [list(range(0, n_row, 2)), list(range(1, n_row, 2))]
    term = lax.all_to_all(term, "row", 0, 0, axis_index_groups=cores, tiled=True)
    piece = jnp.sum(term.reshape(n_row // 2, depth, -1), axis=0)
    half = lax.all_gather(piece, "row", axis=0, axis_index_groups=cores, tiled=True)
    half, back_panel[0] = lax.optimization_barrier((half, back_panel[0]))

    even = list(range(0, n_row, 2))
    pair = [even, [m + 1 for m in even]]
    own, other = sparse_product(
        back_panel, values, row_of, col_of, me_col, me_row, col_blocks, pair, True
    )
    sums = pair_sum(own, swap(other, "row", n_row, 1), len(even))
    feature_grad = total_of(
        [swap(s, "row", n_row, m) for s, m in zip(sums[:0:-1], even[:0:-1])] + [sums[0]]
    ).astype(BF16)
    halves = exchange(jnp.tile(half.astype(BF16), (n_col, 1)), "col")
    half = jnp.sum(halves.reshape(n_col, -1, half.shape[1]).astype(F32), axis=0)
    other = swap(half, "row", n_row, 1)
    other, feature_grad = lax.optimization_barrier((other, feature_grad))
    weight_grad = assemble(half, other, me_row, n_row // 2)
    return (activations, feature_grad, weight_grad)


def solution(mesh):
    placed = (
        P(("col", "row"), None),
        P(),
        P("row", "col", None),
        P("row", "col", None),
        P("row", "col", None, None, None),
        P(("row", "col"), None),
    )
    return jax.shard_map(
        functools.partial(on_device, mesh.shape["row"], mesh.shape["col"]),
        mesh=mesh,
        in_specs=placed,
        out_specs=(P(("row", "col"), None), P(("col", "row"), None), P()),
        check_vma=False,
    )
```

```python
import functools

import jax
import jax.numpy as jnp
from jax import lax
from jax.experimental import pallas as pl
from jax.experimental.pallas import tpu as pltpu
from jax.sharding import PartitionSpec as P

F32 = jnp.float32
BF16 = jnp.bfloat16
GROUP = 8
LONG = 32
ANY = pl.BlockSpec(memory_space=pl.ANY)
VMEM = pl.BlockSpec(memory_space=pltpu.VMEM)
SMEM = pl.BlockSpec(memory_space=pltpu.SMEM)


def params(mib):
    return pltpu.CompilerParams(vmem_limit_bytes=mib << 20)


def cost(flops, nbytes):
    return pl.CostEstimate(flops=flops, bytes_accessed=nbytes, transcendentals=0)


def prepare_kernel(starts, cols, features, row_of, col_of, own):
    own[...] = features[...]
    slots = cols.shape[2]
    row_blocks = starts.shape[2] - 1

    def name_row(i, carry):
        def name_slot(k, carry):
            row_of[k] = i
            return carry

        return lax.fori_loop(starts[0, 0, i], starts[0, 0, i + 1], name_slot, carry)

    lax.fori_loop(0, row_blocks, name_row, 0)
    live = starts[0, 0, row_blocks]

    def name_dead(k, carry):
        row_of[k] = row_blocks
        return carry

    lax.fori_loop(live, slots, name_dead, 0)
    row_of[slots] = live

    def name_col(k, carry):
        col_of[k] = cols[0, 0, k]
        return carry

    lax.fori_loop(0, slots, name_col, 0)


def prepare(starts, cols, features):
    slots = cols.shape[2]
    return pl.pallas_call(
        prepare_kernel,
        out_shape=[
            jax.ShapeDtypeStruct((slots + 1,), jnp.int32),
            jax.ShapeDtypeStruct((slots,), jnp.int32),
            jax.ShapeDtypeStruct(features.shape, BF16),
        ],
        in_specs=[SMEM, SMEM, VMEM],
        out_specs=[SMEM, SMEM, VMEM],
        compiler_params=params(32),
    )(starts, cols, features)


def sparse_kernel(counts, outs, backward, row_of, col_of, here_ref, mine_ref, *refs):
    parts = sum(counts)
    panel_refs = refs[:parts]
    values_ref = refs[parts]
    out_refs = refs[parts + 1 : parts + 1 + len(outs)]
    panel, values, total, values_sem = refs[parts + 1 + len(outs) :]
    slots, size, _ = values.shape
    live, here, mine = row_of[slots], here_ref[0], mine_ref[0]
    chunk = panel_refs[0].shape[0]
    def load(g):
        span = pl.ds(pl.multiple_of(g * GROUP, GROUP), GROUP)
        return pltpu.make_async_copy(values_ref.at[span], values.at[span], values_sem.at[g])

    def begin(g, carry):
        load(g).start()
        return carry

    used = (live + GROUP - 1) // GROUP
    lax.fori_loop(0, used, begin, 0)
    total[...] = jnp.zeros_like(total)
    at = parts
    for m, count in enumerate(counts):
        start = pl.multiple_of((here ^ m) * chunk, chunk)
        part = panel_refs[at - 1][...]
        for ref in panel_refs[at - count : at - 1]:
            part += ref[...]
        panel[pl.ds(start, chunk), :] = part
        at -= count
    spare = total.shape[0] // size - 1
    last = panel.shape[0] // size - 1

    def add_slot(k):
        row, col = row_of[k], col_of[k]
        to, source = (col, jnp.minimum(row, last)) if backward else (row, col)
        to = pl.multiple_of(jnp.where(k < live, to, spare) * size, size)
        source = pl.multiple_of(source * size, size)
        term = lax.dot_general(
            values[k],
            panel[pl.ds(source, size), :],
            (((0 if backward else 1,), (0,)), ((), ())),
            preferred_element_type=F32,
        )
        total[pl.ds(to, size), :] += term

    def steps(count):
        def step(g, carry):
            for part in range(count // GROUP):
                load(g * (count // GROUP) + part).wait()
            for u in range(count):
                add_slot(g * count + u)
            return carry

        return step

    long = live // LONG
    lax.fori_loop(0, long, steps(LONG), 0)
    lax.fori_loop(long * (LONG // GROUP), used, steps(GROUP), 0)
    for out_ref, members in zip(out_refs, outs):
        rows = out_ref.shape[0] // len(members)
        for at, m in enumerate(members):
            start = pl.multiple_of((mine ^ m) * rows, rows)
            out_ref[at * rows : (at + 1) * rows, :] = total[pl.ds(start, rows), :].astype(
                out_ref.dtype
            )


def sparse_product(panel_parts, values, row_of, col_of, here, mine, blocks, outs, backward):
    counts = [len(part) for part in panel_parts]
    operands = [operand for part in panel_parts for operand in part]
    parts = len(counts)
    slots, size, _ = values.shape
    chunk, width = operands[0].shape
    flops = 2 * slots * size * size * width
    return pl.pallas_call(
        functools.partial(sparse_kernel, counts, outs, backward),
        out_shape=[jax.ShapeDtypeStruct((chunk * len(members), width), BF16) for members in outs],
        in_specs=[SMEM] * 4 + [VMEM] * len(operands) + [ANY],
        out_specs=[VMEM] * len(outs),
        scratch_shapes=[
            pltpu.VMEM((parts * chunk, width), BF16),
            pltpu.VMEM((slots, size, size), BF16),
            pltpu.VMEM(((blocks + 1) * size, width), F32),
            pltpu.SemaphoreType.DMA((slots // GROUP,)),
        ],
        compiler_params=params(48),
        cost_estimate=cost(flops, 2 * values.size + 2 * parts * chunk * width),
    )(row_of, col_of, here, mine, *operands[::-1], values)


def split(value):
    high = value.astype(BF16)
    return high, (value - high.astype(F32)).astype(BF16)


def mm(a, b, dims):
    return lax.dot_general(a, b, (dims, ((), ())), preferred_element_type=F32)


def middle_kernel(count, *refs):
    terms = refs[:count]
    weight_ref, cotangent_ref, act_ref, back_ref, agg_ref, grad_ref = refs[count:]
    aggregated = terms[0][...].astype(F32)
    for term in terms[1:]:
        aggregated += term[...].astype(F32)
    agg_ref[...] = aggregated
    weight = weight_ref[...]
    high, low = split(aggregated)
    mixed = mm(high, weight, ((1,), (0,))) + mm(low, weight, ((1,), (0,)))
    sigma = jax.nn.sigmoid(mixed)
    act_ref[...] = (mixed * sigma).astype(BF16)
    mixed_grad = cotangent_ref[...].astype(F32) * (sigma * (1.0 + mixed * (1.0 - sigma)))
    grad_ref[...] = mixed_grad
    high, low = split(mixed_grad)
    back = mm(high, weight, ((1,), (1,))) + mm(low, weight, ((1,), (1,)))
    back_ref[...] = back.astype(BF16)


def middle(terms, weight, cotangent):
    rows, width = cotangent.shape
    return pl.pallas_call(
        functools.partial(middle_kernel, len(terms)),
        out_shape=[
            jax.ShapeDtypeStruct((rows, width), BF16),
            jax.ShapeDtypeStruct((rows, width), BF16),
            jax.ShapeDtypeStruct((rows, width), F32),
            jax.ShapeDtypeStruct((rows, width), F32),
        ],
        in_specs=[VMEM] * (len(terms) + 2),
        out_specs=[VMEM] * 4,
        compiler_params=params(40),
        cost_estimate=cost(8 * rows * width * width, 20 * rows * width),
    )(*terms, weight, cotangent)


def weight_kernel(chunks, me, agg_ref, grad_ref, own_ref, other_ref, scratch):
    high, low = split(agg_ref[...])
    grad_high, grad_low = split(grad_ref[...])
    contract = ((0,), (0,))
    scratch[...] = (
        mm(high, grad_high, contract) + mm(low, grad_high, contract) + mm(high, grad_low, contract)
    )
    depth = scratch.shape[0] // chunks
    for c in range(chunks // 2):
        for ref, other in ((own_ref, 0), (other_ref, 1)):
            start = pl.multiple_of((2 * c + (me[0] % 2 ^ other)) * depth, depth)
            ref[c * depth : (c + 1) * depth, :] = scratch[pl.ds(start, depth), :]


def weight_term(aggregated, mixed_grad, me, chunks):
    rows, width = aggregated.shape
    return pl.pallas_call(
        functools.partial(weight_kernel, chunks),
        out_shape=[jax.ShapeDtypeStruct((width // 2, width), F32)] * 2,
        in_specs=[SMEM, VMEM, VMEM],
        out_specs=[VMEM, VMEM],
        scratch_shapes=[pltpu.VMEM((width, width), F32)],
        compiler_params=params(40),
        cost_estimate=cost(6 * rows * width * width, 8 * rows * width),
    )(me, aggregated, mixed_grad)


def assemble_kernel(chunks, me, own_ref, other_ref, out_ref):
    depth = own_ref.shape[0] // chunks
    for c in range(chunks):
        for ref, other in ((own_ref, 0), (other_ref, 1)):
            start = pl.multiple_of((2 * c + (me[0] % 2 ^ other)) * depth, depth)
            out_ref[pl.ds(start, depth), :] = ref[c * depth : (c + 1) * depth, :]


def assemble(own, other, me, chunks):
    depth, width = own.shape
    return pl.pallas_call(
        functools.partial(assemble_kernel, chunks),
        out_shape=jax.ShapeDtypeStruct((2 * depth, width), own.dtype),
        in_specs=[SMEM, VMEM, VMEM],
        out_specs=VMEM,
        compiler_params=params(32),
    )(me, own, other)


def pair_kernel(count, own_ref, other_ref, *outs):
    rows = own_ref.shape[0] // count
    for m in range(count):
        span = slice(m * rows, (m + 1) * rows)
        outs[m][...] = (own_ref[span, :].astype(F32) + other_ref[span, :].astype(F32)).astype(BF16)


def pair_sum(own, other, count):
    rows, width = own.shape
    return pl.pallas_call(
        functools.partial(pair_kernel, count),
        out_shape=[jax.ShapeDtypeStruct((rows // count, width), BF16)] * count,
        in_specs=[VMEM] * 2,
        out_specs=[VMEM] * count,
        compiler_params=params(40),
        cost_estimate=cost(rows * width, 6 * rows * width),
    )(own, other)


def swap(x, axis, n, m):
    return lax.ppermute(x, axis, [(i, i ^ m) for i in range(n)])


def add_kernel(*refs):
    result = refs[0][...].astype(F32)
    for ref in refs[1:-1]:
        result += ref[...].astype(F32)
    refs[-1][...] = result


def add_up(terms):
    return pl.pallas_call(
        add_kernel,
        out_shape=jax.ShapeDtypeStruct(terms[0].shape, F32),
        in_specs=[VMEM] * len(terms),
        out_specs=VMEM,
        compiler_params=params(32),
        cost_estimate=cost(0, 64 * terms[0].size),
    )(*terms)


def exchange_terms(terms, n):
    if n != 4:
        return [terms[0]] + [swap(terms[m], "col", n, m) for m in range(n - 1, 0, -1)]
    far = lax.ppermute(terms[3], "col", [(0, 1), (3, 2)])
    cross = lax.ppermute(terms[3], "col", [(1, 2), (2, 1)])
    inward = lax.ppermute(terms[2], "col", [(0, 2), (3, 1)])
    near = swap(terms[1], "col", n, 1)
    relay = total_of([terms[2], far]).astype(BF16)
    outward = lax.ppermute(relay, "col", [(1, 3), (2, 0)])
    return [add_up([cross, inward, near, terms[0]]), outward]


def gather_parts(own, n, first):
    if n != 4:
        return [[own]] + [[swap(own, "col", n, m)] for m in range(n - 1, 0, -1)][::-1], first
    inward = lax.ppermute(own, "col", [(0, 2), (3, 1)])
    cross = lax.ppermute(own, "col", [(1, 2), (2, 1)])
    outward = lax.ppermute(own, "col", [(1, 3), (2, 0)])
    near = swap(own, "col", n, 1)
    inward, first = lax.optimization_barrier((inward, first))
    far = lax.ppermute(inward, "col", [(2, 3), (1, 0)])
    return [[own], [near], [inward, outward], [cross, far]], first


def total_of(terms):
    result = terms[0].astype(F32)
    for term in terms[1:]:
        result = result + term.astype(F32)
    return result


def exchange(x, axis):
    return lax.all_to_all(x, axis, 0, 0, tiled=True)


def on_device(n_row, n_col, features, weight, block_cols, row_starts, block_values, cotangent):
    values = block_values[0, 0]
    size = values.shape[1]
    row_blocks = row_starts.shape[2] - 1
    col_blocks = n_row * features.shape[0] // size
    me_row = lax.axis_index("row")[None].astype(jnp.int32)
    me_col = lax.axis_index("col")[None].astype(jnp.int32)

    panel = [features] + [None] * (n_row - 1)
    for m in range(n_row - 2, 0, -2):
        panel[m] = swap(features, "row", n_row, m)
    prepared = prepare(row_starts, block_cols, features)
    panel[n_row - 2], (row_of, col_of, panel[0]) = lax.optimization_barrier(
        (panel[n_row - 2], prepared)
    )
    for m in range(0, n_row, 2):
        panel[m + 1] = swap(panel[m], "row", n_row, 1)

    each = [[m] for m in range(n_col)]
    terms = sparse_product(
        [[part] for part in panel], values, row_of, col_of, me_row, me_col, row_blocks, each, False
    )
    terms = exchange_terms(terms, n_col)
    activations, back, aggregated, mixed_grad = middle(terms, weight, cotangent)

    own_term, other_term = weight_term(aggregated, mixed_grad, me_row, n_row)
    term = own_term + swap(other_term, "row", n_row, 1)
    back_panel, term = gather_parts(back, n_col, term)
    cores = [list(range(0, n_row, 2)), list(range(1, n_row, 2))]
    half = lax.all_gather(term, "row", axis=0, axis_index_groups=cores, tiled=True)
    half, back_panel[0] = lax.optimization_barrier((half, back_panel[0]))
    half = jnp.sum(half.reshape(n_row // 2, -1, half.shape[1]), axis=0)

    even = list(range(0, n_row, 2))
    pair = [even, [m + 1 for m in even]]
    own, other = sparse_product(
        back_panel, values, row_of, col_of, me_col, me_row, col_blocks, pair, True
    )
    sums = pair_sum(own, swap(other, "row", n_row, 1), len(even))
    feature_grad = total_of(
        [swap(s, "row", n_row, m) for s, m in zip(sums[:0:-1], even[:0:-1])] + [sums[0]]
    ).astype(BF16)
    halves = exchange(jnp.tile(half.astype(BF16), (n_col, 1)), "col")
    half = jnp.sum(halves.reshape(n_col, -1, half.shape[1]).astype(F32), axis=0)
    other = swap(half, "row", n_row, 1)
    other, feature_grad = lax.optimization_barrier((other, feature_grad))
    weight_grad = assemble(half, other, me_row, n_row // 2)
    return (activations, feature_grad, weight_grad)


def solution(mesh):
    placed = (
        P(("col", "row"), None),
        P(),
        P("row", "col", None),
        P("row", "col", None),
        P("row", "col", None, None, None),
        P(("row", "col"), None),
    )
    return jax.shard_map(
        functools.partial(on_device, mesh.shape["row"], mesh.shape["col"]),
        mesh=mesh,
        in_specs=placed,
        out_specs=(P(("row", "col"), None), P(("col", "row"), None), P()),
        check_vma=False,
    )
```

```python
import functools

import jax
import jax.numpy as jnp
from jax import lax
from jax.experimental import pallas as pl
from jax.experimental.pallas import tpu as pltpu
from jax.sharding import PartitionSpec as P

F32 = jnp.float32
BF16 = jnp.bfloat16
GROUP = 8
LONG = 32
ANY = pl.BlockSpec(memory_space=pl.ANY)
VMEM = pl.BlockSpec(memory_space=pltpu.VMEM)
SMEM = pl.BlockSpec(memory_space=pltpu.SMEM)


def params(mib):
    return pltpu.CompilerParams(vmem_limit_bytes=mib << 20)


def cost(flops, nbytes):
    return pl.CostEstimate(flops=flops, bytes_accessed=nbytes, transcendentals=0)


def prepare_kernel(starts, cols, features, row_of, col_of, own):
    own[...] = features[...]
    slots = cols.shape[2]
    row_blocks = starts.shape[2] - 1

    def name_row(i, carry):
        def name_slot(k, carry):
            row_of[k] = i
            return carry

        return lax.fori_loop(starts[0, 0, i], starts[0, 0, i + 1], name_slot, carry)

    lax.fori_loop(0, row_blocks, name_row, 0)
    live = starts[0, 0, row_blocks]

    def name_dead(k, carry):
        row_of[k] = row_blocks
        return carry

    lax.fori_loop(live, slots, name_dead, 0)
    row_of[slots] = live

    def name_col(k, carry):
        col_of[k] = cols[0, 0, k]
        return carry

    lax.fori_loop(0, slots, name_col, 0)


def prepare(starts, cols, features):
    slots = cols.shape[2]
    return pl.pallas_call(
        prepare_kernel,
        out_shape=[
            jax.ShapeDtypeStruct((slots + 1,), jnp.int32),
            jax.ShapeDtypeStruct((slots,), jnp.int32),
            jax.ShapeDtypeStruct(features.shape, BF16),
        ],
        in_specs=[SMEM, SMEM, VMEM],
        out_specs=[SMEM, SMEM, VMEM],
        compiler_params=params(32),
    )(starts, cols, features)


def sparse_kernel(counts, outs, backward, row_of, col_of, here_ref, mine_ref, *refs):
    parts = sum(counts)
    panel_refs = refs[:parts]
    values_ref = refs[parts]
    out_refs = refs[parts + 1 : parts + 1 + len(outs)]
    panel, values, total, values_sem = refs[parts + 1 + len(outs) :]
    slots, size, _ = values.shape
    live, here, mine = row_of[slots], here_ref[0], mine_ref[0]
    chunk = panel_refs[0].shape[0]
    def load(g):
        span = pl.ds(pl.multiple_of(g * GROUP, GROUP), GROUP)
        return pltpu.make_async_copy(values_ref.at[span], values.at[span], values_sem.at[g])

    def begin(g, carry):
        load(g).start()
        return carry

    used = (live + GROUP - 1) // GROUP
    lax.fori_loop(0, used, begin, 0)
    total[...] = jnp.zeros_like(total)
    at = parts
    for m, count in enumerate(counts):
        start = pl.multiple_of((here ^ m) * chunk, chunk)
        part = panel_refs[at - 1][...]
        for ref in panel_refs[at - count : at - 1]:
            part += ref[...]
        panel[pl.ds(start, chunk), :] = part
        at -= count
    spare = total.shape[0] // size - 1
    last = panel.shape[0] // size - 1

    def add_slot(k):
        row, col = row_of[k], col_of[k]
        to, source = (col, jnp.minimum(row, last)) if backward else (row, col)
        to = pl.multiple_of(jnp.where(k < live, to, spare) * size, size)
        source = pl.multiple_of(source * size, size)
        term = lax.dot_general(
            values[k],
            panel[pl.ds(source, size), :],
            (((0 if backward else 1,), (0,)), ((), ())),
            preferred_element_type=F32,
        )
        total[pl.ds(to, size), :] += term

    def steps(count):
        def step(g, carry):
            for part in range(count // GROUP):
                load(g * (count // GROUP) + part).wait()
            for u in range(count):
                add_slot(g * count + u)
            return carry

        return step

    long = live // LONG
    lax.fori_loop(0, long, steps(LONG), 0)
    lax.fori_loop(long * (LONG // GROUP), used, steps(GROUP), 0)
    for out_ref, members in zip(out_refs, outs):
        rows = out_ref.shape[0] // len(members)
        for at, m in enumerate(members):
            start = pl.multiple_of((mine ^ m) * rows, rows)
            out_ref[at * rows : (at + 1) * rows, :] = total[pl.ds(start, rows), :].astype(
                out_ref.dtype
            )


def sparse_product(panel_parts, values, row_of, col_of, here, mine, blocks, outs, backward):
    counts = [len(part) for part in panel_parts]
    operands = [operand for part in panel_parts for operand in part]
    parts = len(counts)
    slots, size, _ = values.shape
    chunk, width = operands[0].shape
    flops = 2 * slots * size * size * width
    return pl.pallas_call(
        functools.partial(sparse_kernel, counts, outs, backward),
        out_shape=[jax.ShapeDtypeStruct((chunk * len(members), width), BF16) for members in outs],
        in_specs=[SMEM] * 4 + [VMEM] * len(operands) + [ANY],
        out_specs=[VMEM] * len(outs),
        scratch_shapes=[
            pltpu.VMEM((parts * chunk, width), BF16),
            pltpu.VMEM((slots, size, size), BF16),
            pltpu.VMEM(((blocks + 1) * size, width), F32),
            pltpu.SemaphoreType.DMA((slots // GROUP,)),
        ],
        compiler_params=params(48),
        cost_estimate=cost(flops, 2 * values.size + 2 * parts * chunk * width),
    )(row_of, col_of, here, mine, *operands[::-1], values)


def split(value):
    high = value.astype(BF16)
    return high, (value - high.astype(F32)).astype(BF16)


def mm(a, b, dims):
    return lax.dot_general(a, b, (dims, ((), ())), preferred_element_type=F32)


def middle_kernel(count, *refs):
    terms = refs[:count]
    weight_ref, cotangent_ref, act_ref, back_ref, agg_ref, grad_ref = refs[count:]
    aggregated = terms[0][...].astype(F32)
    for term in terms[1:]:
        aggregated += term[...].astype(F32)
    agg_ref[...] = aggregated
    weight = weight_ref[...]
    high, low = split(aggregated)
    mixed = mm(high, weight, ((1,), (0,))) + mm(low, weight, ((1,), (0,)))
    sigma = jax.nn.sigmoid(mixed)
    act_ref[...] = (mixed * sigma).astype(BF16)
    mixed_grad = cotangent_ref[...].astype(F32) * (sigma * (1.0 + mixed * (1.0 - sigma)))
    grad_ref[...] = mixed_grad
    high, low = split(mixed_grad)
    back = mm(high, weight, ((1,), (1,))) + mm(low, weight, ((1,), (1,)))
    back_ref[...] = back.astype(BF16)


def middle(terms, weight, cotangent):
    rows, width = cotangent.shape
    return pl.pallas_call(
        functools.partial(middle_kernel, len(terms)),
        out_shape=[
            jax.ShapeDtypeStruct((rows, width), BF16),
            jax.ShapeDtypeStruct((rows, width), BF16),
            jax.ShapeDtypeStruct((rows, width), F32),
            jax.ShapeDtypeStruct((rows, width), F32),
        ],
        in_specs=[VMEM] * (len(terms) + 2),
        out_specs=[VMEM] * 4,
        compiler_params=params(40),
        cost_estimate=cost(8 * rows * width * width, 20 * rows * width),
    )(*terms, weight, cotangent)


def weight_kernel(chunks, me, agg_ref, grad_ref, own_ref, other_ref, scratch):
    high, low = split(agg_ref[...])
    grad_high, grad_low = split(grad_ref[...])
    contract = ((0,), (0,))
    scratch[...] = (
        mm(high, grad_high, contract) + mm(low, grad_high, contract) + mm(high, grad_low, contract)
    )
    depth = scratch.shape[0] // chunks
    for c in range(chunks // 2):
        for ref, other in ((own_ref, 0), (other_ref, 1)):
            start = pl.multiple_of((2 * c + (me[0] % 2 ^ other)) * depth, depth)
            ref[c * depth : (c + 1) * depth, :] = scratch[pl.ds(start, depth), :]


def weight_term(aggregated, mixed_grad, me, chunks):
    rows, width = aggregated.shape
    return pl.pallas_call(
        functools.partial(weight_kernel, chunks),
        out_shape=[jax.ShapeDtypeStruct((width // 2, width), F32)] * 2,
        in_specs=[SMEM, VMEM, VMEM],
        out_specs=[VMEM, VMEM],
        scratch_shapes=[pltpu.VMEM((width, width), F32)],
        compiler_params=params(40),
        cost_estimate=cost(6 * rows * width * width, 8 * rows * width),
    )(me, aggregated, mixed_grad)


def assemble_kernel(chunks, me, own_ref, other_ref, out_ref):
    depth = own_ref.shape[0] // chunks
    for c in range(chunks):
        for ref, other in ((own_ref, 0), (other_ref, 1)):
            start = pl.multiple_of((2 * c + (me[0] % 2 ^ other)) * depth, depth)
            out_ref[pl.ds(start, depth), :] = ref[c * depth : (c + 1) * depth, :]


def assemble(own, other, me, chunks):
    depth, width = own.shape
    return pl.pallas_call(
        functools.partial(assemble_kernel, chunks),
        out_shape=jax.ShapeDtypeStruct((2 * depth, width), own.dtype),
        in_specs=[SMEM, VMEM, VMEM],
        out_specs=VMEM,
        compiler_params=params(32),
    )(me, own, other)


def pair_kernel(count, own_ref, other_ref, *outs):
    rows = own_ref.shape[0] // count
    for m in range(count):
        span = slice(m * rows, (m + 1) * rows)
        outs[m][...] = (own_ref[span, :].astype(F32) + other_ref[span, :].astype(F32)).astype(BF16)


def pair_sum(own, other, count):
    rows, width = own.shape
    return pl.pallas_call(
        functools.partial(pair_kernel, count),
        out_shape=[jax.ShapeDtypeStruct((rows // count, width), BF16)] * count,
        in_specs=[VMEM] * 2,
        out_specs=[VMEM] * count,
        compiler_params=params(40),
        cost_estimate=cost(rows * width, 6 * rows * width),
    )(own, other)


def swap(x, axis, n, m):
    return lax.ppermute(x, axis, [(i, i ^ m) for i in range(n)])


def copies_kernel(parts, copies, in_ref, out_ref):
    rows = in_ref.shape[0] // parts
    result = in_ref[:rows, :]
    for p in range(1, parts):
        result += in_ref[p * rows : (p + 1) * rows, :]
    result = result.astype(BF16)
    for c in range(copies):
        out_ref[c * rows : (c + 1) * rows, :] = result


def sum_copies(stacked, parts, copies):
    rows, width = stacked.shape
    return pl.pallas_call(
        functools.partial(copies_kernel, parts, copies),
        out_shape=jax.ShapeDtypeStruct((rows // parts * copies, width), BF16),
        in_specs=[VMEM],
        out_specs=VMEM,
        compiler_params=params(32),
        cost_estimate=cost(0, 0),
    )(stacked)


def add_kernel(*refs):
    result = refs[0][...].astype(F32)
    for ref in refs[1:-1]:
        result += ref[...].astype(F32)
    refs[-1][...] = result


def add_up(terms):
    return pl.pallas_call(
        add_kernel,
        out_shape=jax.ShapeDtypeStruct(terms[0].shape, F32),
        in_specs=[VMEM] * len(terms),
        out_specs=VMEM,
        compiler_params=params(32),
        cost_estimate=cost(0, 64 * terms[0].size),
    )(*terms)


def exchange_terms(terms, n):
    if n != 4:
        return [terms[0]] + [swap(terms[m], "col", n, m) for m in range(n - 1, 0, -1)]
    far = lax.ppermute(terms[3], "col", [(0, 1), (3, 2)])
    cross = lax.ppermute(terms[3], "col", [(1, 2), (2, 1)])
    inward = lax.ppermute(terms[2], "col", [(0, 2), (3, 1)])
    near = swap(terms[1], "col", n, 1)
    relay = total_of([terms[2], far]).astype(BF16)
    outward = lax.ppermute(relay, "col", [(1, 3), (2, 0)])
    return [add_up([cross, inward, near, terms[0]]), outward]


def gather_parts(own, n, first):
    if n != 4:
        return [[own]] + [[swap(own, "col", n, m)] for m in range(n - 1, 0, -1)][::-1], first
    inward = lax.ppermute(own, "col", [(0, 2), (3, 1)])
    cross = lax.ppermute(own, "col", [(1, 2), (2, 1)])
    outward = lax.ppermute(own, "col", [(1, 3), (2, 0)])
    near = swap(own, "col", n, 1)
    inward, first = lax.optimization_barrier((inward, first))
    far = lax.ppermute(inward, "col", [(2, 3), (1, 0)])
    return [[own], [near], [inward, outward], [cross, far]], first


def total_of(terms):
    result = terms[0].astype(F32)
    for term in terms[1:]:
        result = result + term.astype(F32)
    return result


def exchange(x, axis):
    return lax.all_to_all(x, axis, 0, 0, tiled=True)


def on_device(n_row, n_col, features, weight, block_cols, row_starts, block_values, cotangent):
    values = block_values[0, 0]
    size = values.shape[1]
    row_blocks = row_starts.shape[2] - 1
    col_blocks = n_row * features.shape[0] // size
    me_row = lax.axis_index("row")[None].astype(jnp.int32)
    me_col = lax.axis_index("col")[None].astype(jnp.int32)

    panel = [features] + [None] * (n_row - 1)
    for m in range(n_row - 2, 0, -2):
        panel[m] = swap(features, "row", n_row, m)
    prepared = prepare(row_starts, block_cols, features)
    panel[n_row - 2], (row_of, col_of, panel[0]) = lax.optimization_barrier(
        (panel[n_row - 2], prepared)
    )
    for m in range(0, n_row, 2):
        panel[m + 1] = swap(panel[m], "row", n_row, 1)

    each = [[m] for m in range(n_col)]
    terms = sparse_product(
        [[part] for part in panel], values, row_of, col_of, me_row, me_col, row_blocks, each, False
    )
    terms = exchange_terms(terms, n_col)
    activations, back, aggregated, mixed_grad = middle(terms, weight, cotangent)

    own_term, other_term = weight_term(aggregated, mixed_grad, me_row, n_row)
    term = own_term + swap(other_term, "row", n_row, 1)
    back_panel, term = gather_parts(back, n_col, term)
    cores = [list(range(0, n_row, 2)), list(range(1, n_row, 2))]
    half = lax.all_gather(term, "row", axis=0, axis_index_groups=cores, tiled=True)
    copies = sum_copies(half, n_row // 2, n_col)
    copies, back_panel[0] = lax.optimization_barrier((copies, back_panel[0]))

    even = list(range(0, n_row, 2))
    pair = [even, [m + 1 for m in even]]
    own, other = sparse_product(
        back_panel, values, row_of, col_of, me_col, me_row, col_blocks, pair, True
    )
    sums = pair_sum(own, swap(other, "row", n_row, 1), len(even))
    feature_grad = total_of(
        [swap(s, "row", n_row, m) for s, m in zip(sums[:0:-1], even[:0:-1])] + [sums[0]]
    ).astype(BF16)
    halves = exchange(copies, "col")
    half = jnp.sum(halves.reshape(n_col, -1, halves.shape[1]).astype(F32), axis=0)
    other = swap(half, "row", n_row, 1)
    other, feature_grad = lax.optimization_barrier((other, feature_grad))
    weight_grad = assemble(half, other, me_row, n_row // 2)
    return (activations, feature_grad, weight_grad)


def solution(mesh):
    placed = (
        P(("col", "row"), None),
        P(),
        P("row", "col", None),
        P("row", "col", None),
        P("row", "col", None, None, None),
        P(("row", "col"), None),
    )
    return jax.shard_map(
        functools.partial(on_device, mesh.shape["row"], mesh.shape["col"]),
        mesh=mesh,
        in_specs=placed,
        out_specs=(P(("row", "col"), None), P(("col", "row"), None), P()),
        check_vma=False,
    )
```

```python
import functools

import jax
import jax.numpy as jnp
from jax import lax
from jax.experimental import pallas as pl
from jax.experimental.pallas import tpu as pltpu
from jax.sharding import PartitionSpec as P

F32 = jnp.float32
BF16 = jnp.bfloat16
GROUP = 8
LONG = 32
ANY = pl.BlockSpec(memory_space=pl.ANY)
VMEM = pl.BlockSpec(memory_space=pltpu.VMEM)
SMEM = pl.BlockSpec(memory_space=pltpu.SMEM)


def params(mib):
    return pltpu.CompilerParams(vmem_limit_bytes=mib << 20)


def cost(flops, nbytes):
    return pl.CostEstimate(flops=flops, bytes_accessed=nbytes, transcendentals=0)


def prepare_kernel(starts, cols, features, row_of, col_of, own):
    own[...] = features[...]
    slots = cols.shape[2]
    row_blocks = starts.shape[2] - 1

    def name_row(i, carry):
        def name_slot(k, carry):
            row_of[k] = i
            return carry

        return lax.fori_loop(starts[0, 0, i], starts[0, 0, i + 1], name_slot, carry)

    lax.fori_loop(0, row_blocks, name_row, 0)
    live = starts[0, 0, row_blocks]

    def name_dead(k, carry):
        row_of[k] = row_blocks
        return carry

    lax.fori_loop(live, slots, name_dead, 0)
    row_of[slots] = live

    def name_col(k, carry):
        col_of[k] = cols[0, 0, k]
        return carry

    lax.fori_loop(0, slots, name_col, 0)


def prepare(starts, cols, features):
    slots = cols.shape[2]
    return pl.pallas_call(
        prepare_kernel,
        out_shape=[
            jax.ShapeDtypeStruct((slots + 1,), jnp.int32),
            jax.ShapeDtypeStruct((slots,), jnp.int32),
            jax.ShapeDtypeStruct(features.shape, BF16),
        ],
        in_specs=[SMEM, SMEM, VMEM],
        out_specs=[SMEM, SMEM, VMEM],
        compiler_params=params(32),
    )(starts, cols, features)


def sparse_kernel(counts, outs, backward, row_of, col_of, here_ref, mine_ref, *refs):
    parts = sum(counts)
    panel_refs = refs[:parts]
    values_ref = refs[parts]
    out_refs = refs[parts + 1 : parts + 1 + len(outs)]
    panel, values, total, values_sem = refs[parts + 1 + len(outs) :]
    slots, size, _ = values.shape
    live, here, mine = row_of[slots], here_ref[0], mine_ref[0]
    chunk = panel_refs[0].shape[0]
    def load(g):
        span = pl.ds(pl.multiple_of(g * GROUP, GROUP), GROUP)
        return pltpu.make_async_copy(values_ref.at[span], values.at[span], values_sem.at[g])

    def begin(g, carry):
        load(g).start()
        return carry

    used = (live + GROUP - 1) // GROUP
    lax.fori_loop(0, used, begin, 0)
    total[...] = jnp.zeros_like(total)
    at = parts
    for m, count in enumerate(counts):
        start = pl.multiple_of((here ^ m) * chunk, chunk)
        part = panel_refs[at - 1][...]
        for ref in panel_refs[at - count : at - 1]:
            part += ref[...]
        panel[pl.ds(start, chunk), :] = part
        at -= count
    spare = total.shape[0] // size - 1
    last = panel.shape[0] // size - 1

    def add_slot(k):
        row, col = row_of[k], col_of[k]
        to, source = (col, jnp.minimum(row, last)) if backward else (row, col)
        to = pl.multiple_of(jnp.where(k < live, to, spare) * size, size)
        source = pl.multiple_of(source * size, size)
        term = lax.dot_general(
            values[k],
            panel[pl.ds(source, size), :],
            (((0 if backward else 1,), (0,)), ((), ())),
            preferred_element_type=F32,
        )
        total[pl.ds(to, size), :] += term

    def steps(count):
        def step(g, carry):
            for part in range(count // GROUP):
                load(g * (count // GROUP) + part).wait()
            for u in range(count):
                add_slot(g * count + u)
            return carry

        return step

    long = live // LONG
    lax.fori_loop(0, long, steps(LONG), 0)
    lax.fori_loop(long * (LONG // GROUP), used, steps(GROUP), 0)
    for out_ref, members in zip(out_refs, outs):
        rows = out_ref.shape[0] // len(members)
        for at, m in enumerate(members):
            start = pl.multiple_of((mine ^ m) * rows, rows)
            out_ref[at * rows : (at + 1) * rows, :] = total[pl.ds(start, rows), :].astype(
                out_ref.dtype
            )


def sparse_product(panel_parts, values, row_of, col_of, here, mine, blocks, outs, backward):
    counts = [len(part) for part in panel_parts]
    operands = [operand for part in panel_parts for operand in part]
    parts = len(counts)
    slots, size, _ = values.shape
    chunk, width = operands[0].shape
    flops = 2 * slots * size * size * width
    return pl.pallas_call(
        functools.partial(sparse_kernel, counts, outs, backward),
        out_shape=[jax.ShapeDtypeStruct((chunk * len(members), width), BF16) for members in outs],
        in_specs=[SMEM] * 4 + [VMEM] * len(operands) + [ANY],
        out_specs=[VMEM] * len(outs),
        scratch_shapes=[
            pltpu.VMEM((parts * chunk, width), BF16),
            pltpu.VMEM((slots, size, size), BF16),
            pltpu.VMEM(((blocks + 1) * size, width), F32),
            pltpu.SemaphoreType.DMA((slots // GROUP,)),
        ],
        compiler_params=params(48),
        cost_estimate=cost(flops, 2 * values.size + 2 * parts * chunk * width),
    )(row_of, col_of, here, mine, *operands[::-1], values)


def split(value):
    high = value.astype(BF16)
    return high, (value - high.astype(F32)).astype(BF16)


def mm(a, b, dims):
    return lax.dot_general(a, b, (dims, ((), ())), preferred_element_type=F32)


def middle_kernel(count, *refs):
    terms = refs[:count]
    weight_ref, cotangent_ref, act_ref, back_ref, agg_ref, grad_ref = refs[count:]
    aggregated = terms[0][...].astype(F32)
    for term in terms[1:]:
        aggregated += term[...].astype(F32)
    agg_ref[...] = aggregated
    weight = weight_ref[...]
    high, low = split(aggregated)
    mixed = mm(high, weight, ((1,), (0,))) + mm(low, weight, ((1,), (0,)))
    sigma = jax.nn.sigmoid(mixed)
    act_ref[...] = (mixed * sigma).astype(BF16)
    mixed_grad = cotangent_ref[...].astype(F32) * (sigma * (1.0 + mixed * (1.0 - sigma)))
    grad_ref[...] = mixed_grad
    high, low = split(mixed_grad)
    back = mm(high, weight, ((1,), (1,))) + mm(low, weight, ((1,), (1,)))
    back_ref[...] = back.astype(BF16)


def middle(terms, weight, cotangent):
    rows, width = cotangent.shape
    return pl.pallas_call(
        functools.partial(middle_kernel, len(terms)),
        out_shape=[
            jax.ShapeDtypeStruct((rows, width), BF16),
            jax.ShapeDtypeStruct((rows, width), BF16),
            jax.ShapeDtypeStruct((rows, width), F32),
            jax.ShapeDtypeStruct((rows, width), F32),
        ],
        in_specs=[VMEM] * (len(terms) + 2),
        out_specs=[VMEM] * 4,
        compiler_params=params(40),
        cost_estimate=cost(8 * rows * width * width, 20 * rows * width),
    )(*terms, weight, cotangent)


def weight_kernel(chunks, me, agg_ref, grad_ref, own_ref, other_ref, scratch):
    high, low = split(agg_ref[...])
    grad_high, grad_low = split(grad_ref[...])
    contract = ((0,), (0,))
    scratch[...] = (
        mm(high, grad_high, contract) + mm(low, grad_high, contract) + mm(high, grad_low, contract)
    )
    depth = scratch.shape[0] // chunks
    for c in range(chunks // 2):
        for ref, other in ((own_ref, 0), (other_ref, 1)):
            start = pl.multiple_of((2 * c + (me[0] % 2 ^ other)) * depth, depth)
            ref[c * depth : (c + 1) * depth, :] = scratch[pl.ds(start, depth), :]


def weight_term(aggregated, mixed_grad, me, chunks):
    rows, width = aggregated.shape
    return pl.pallas_call(
        functools.partial(weight_kernel, chunks),
        out_shape=[jax.ShapeDtypeStruct((width // 2, width), F32)] * 2,
        in_specs=[SMEM, VMEM, VMEM],
        out_specs=[VMEM, VMEM],
        scratch_shapes=[pltpu.VMEM((width, width), F32)],
        compiler_params=params(40),
        cost_estimate=cost(6 * rows * width * width, 8 * rows * width),
    )(me, aggregated, mixed_grad)


def assemble_kernel(chunks, me, own_ref, other_ref, out_ref):
    depth = own_ref.shape[0] // chunks
    for c in range(chunks):
        for ref, other in ((own_ref, 0), (other_ref, 1)):
            start = pl.multiple_of((2 * c + (me[0] % 2 ^ other)) * depth, depth)
            out_ref[pl.ds(start, depth), :] = ref[c * depth : (c + 1) * depth, :]


def assemble(own, other, me, chunks):
    depth, width = own.shape
    return pl.pallas_call(
        functools.partial(assemble_kernel, chunks),
        out_shape=jax.ShapeDtypeStruct((2 * depth, width), own.dtype),
        in_specs=[SMEM, VMEM, VMEM],
        out_specs=VMEM,
        compiler_params=params(32),
    )(me, own, other)


def pair_kernel(count, own_ref, other_ref, *outs):
    rows = own_ref.shape[0] // count
    for m in range(count):
        span = slice(m * rows, (m + 1) * rows)
        outs[m][...] = (own_ref[span, :].astype(F32) + other_ref[span, :].astype(F32)).astype(BF16)


def pair_sum(own, other, count):
    rows, width = own.shape
    return pl.pallas_call(
        functools.partial(pair_kernel, count),
        out_shape=[jax.ShapeDtypeStruct((rows // count, width), BF16)] * count,
        in_specs=[VMEM] * 2,
        out_specs=[VMEM] * count,
        compiler_params=params(40),
        cost_estimate=cost(rows * width, 6 * rows * width),
    )(own, other)


def swap(x, axis, n, m):
    return lax.ppermute(x, axis, [(i, i ^ m) for i in range(n)])


def copies_kernel(parts, copies, in_ref, out_ref):
    rows = in_ref.shape[0] // parts
    result = in_ref[:rows, :]
    for p in range(1, parts):
        result += in_ref[p * rows : (p + 1) * rows, :]
    result = result.astype(BF16)
    for c in range(copies):
        out_ref[c * rows : (c + 1) * rows, :] = result


def sum_copies(stacked, parts, copies):
    rows, width = stacked.shape
    return pl.pallas_call(
        functools.partial(copies_kernel, parts, copies),
        out_shape=jax.ShapeDtypeStruct((rows // parts * copies, width), BF16),
        in_specs=[VMEM],
        out_specs=VMEM,
        compiler_params=params(32),
        cost_estimate=cost(0, 0),
    )(stacked)


def add_kernel(*refs):
    result = refs[0][...].astype(F32)
    for ref in refs[1:-1]:
        result += ref[...].astype(F32)
    refs[-1][...] = result


def add_up(terms):
    return pl.pallas_call(
        add_kernel,
        out_shape=jax.ShapeDtypeStruct(terms[0].shape, F32),
        in_specs=[VMEM] * len(terms),
        out_specs=VMEM,
        compiler_params=params(32),
        cost_estimate=cost(0, 64 * terms[0].size),
    )(*terms)


def exchange_terms(terms, n):
    if n != 4:
        return [terms[0]] + [swap(terms[m], "col", n, m) for m in range(n - 1, 0, -1)]
    far = lax.ppermute(terms[3], "col", [(0, 1), (3, 2)])
    cross = lax.ppermute(terms[3], "col", [(1, 2), (2, 1)])
    inward = lax.ppermute(terms[2], "col", [(0, 2), (3, 1)])
    near = swap(terms[1], "col", n, 1)
    relay = total_of([terms[2], far]).astype(BF16)
    outward = lax.ppermute(relay, "col", [(1, 3), (2, 0)])
    return [add_up([cross, inward, near, terms[0]]), outward]


def gather_parts(own, n, first):
    if n != 4:
        return [[own]] + [[swap(own, "col", n, m)] for m in range(n - 1, 0, -1)][::-1], first
    inward = lax.ppermute(own, "col", [(0, 2), (3, 1)])
    cross = lax.ppermute(own, "col", [(1, 2), (2, 1)])
    outward = lax.ppermute(own, "col", [(1, 3), (2, 0)])
    near = swap(own, "col", n, 1)
    inward, first = lax.optimization_barrier((inward, first))
    far = lax.ppermute(inward, "col", [(2, 3), (1, 0)])
    return [[own], [near], [inward, outward], [cross, far]], first


def total_of(terms):
    result = terms[0].astype(F32)
    for term in terms[1:]:
        result = result + term.astype(F32)
    return result


def exchange(x, axis):
    return lax.all_to_all(x, axis, 0, 0, tiled=True)


def on_device(n_row, n_col, features, weight, block_cols, row_starts, block_values, cotangent):
    values = block_values[0, 0]
    size = values.shape[1]
    row_blocks = row_starts.shape[2] - 1
    col_blocks = n_row * features.shape[0] // size
    me_row = lax.axis_index("row")[None].astype(jnp.int32)
    me_col = lax.axis_index("col")[None].astype(jnp.int32)

    panel = [features] + [None] * (n_row - 1)
    for m in range(n_row - 2, 0, -2):
        panel[m] = swap(features, "row", n_row, m)
    prepared = prepare(row_starts, block_cols, features)
    panel[n_row - 2], (row_of, col_of, panel[0]) = lax.optimization_barrier(
        (panel[n_row - 2], prepared)
    )
    for m in range(0, n_row, 2):
        panel[m + 1] = swap(panel[m], "row", n_row, 1)

    each = [[m] for m in range(n_col)]
    terms = sparse_product(
        [[part] for part in panel], values, row_of, col_of, me_row, me_col, row_blocks, each, False
    )
    terms = exchange_terms(terms, n_col)
    activations, back, aggregated, mixed_grad = middle(terms, weight, cotangent)

    own_term, other_term = weight_term(aggregated, mixed_grad, me_row, n_row)
    term = own_term + swap(other_term, "row", n_row, 1)
    back_panel, term = gather_parts(back, n_col, term)
    cores = [list(range(0, n_row, 2)), list(range(1, n_row, 2))]
    half = lax.all_gather(term, "row", axis=0, axis_index_groups=cores, tiled=True)
    copies = sum_copies(half, n_row // 2, n_col)
    copies, back_panel[0] = lax.optimization_barrier((copies, back_panel[0]))

    even = list(range(0, n_row, 2))
    pair = [even, [m + 1 for m in even]]
    own, other = sparse_product(
        back_panel, values, row_of, col_of, me_col, me_row, col_blocks, pair, True
    )
    sums = pair_sum(own, swap(other, "row", n_row, 1), len(even))
    feature_grad = total_of(
        [swap(s, "row", n_row, m) for s, m in zip(sums[:0:-1], even[:0:-1])] + [sums[0]]
    ).astype(BF16)
    halves = exchange(copies, "col")
    half = jnp.sum(halves.reshape(n_col, -1, halves.shape[1]).astype(F32), axis=0)
    other = swap(half, "row", n_row, 1)
    weight_grad = assemble(half, other, me_row, n_row // 2)
    return (activations, feature_grad, weight_grad)


def solution(mesh):
    placed = (
        P(("col", "row"), None),
        P(),
        P("row", "col", None),
        P("row", "col", None),
        P("row", "col", None, None, None),
        P(("row", "col"), None),
    )
    return jax.shard_map(
        functools.partial(on_device, mesh.shape["row"], mesh.shape["col"]),
        mesh=mesh,
        in_specs=placed,
        out_specs=(P(("row", "col"), None), P(("col", "row"), None), P()),
        check_vma=False,
    )
```

```python
import functools

import jax
import jax.numpy as jnp
from jax import lax
from jax.experimental import pallas as pl
from jax.experimental.pallas import tpu as pltpu
from jax.sharding import PartitionSpec as P

F32 = jnp.float32
BF16 = jnp.bfloat16
GROUP = 8
LONG = 32
ANY = pl.BlockSpec(memory_space=pl.ANY)
VMEM = pl.BlockSpec(memory_space=pltpu.VMEM)
SMEM = pl.BlockSpec(memory_space=pltpu.SMEM)


def params(mib):
    return pltpu.CompilerParams(vmem_limit_bytes=mib << 20)


def cost(flops, nbytes):
    return pl.CostEstimate(flops=flops, bytes_accessed=nbytes, transcendentals=0)


def prepare_kernel(starts, cols, features, row_of, col_of, own):
    own[...] = features[...]
    slots = cols.shape[2]
    row_blocks = starts.shape[2] - 1

    def name_row(i, carry):
        def name_slot(k, carry):
            row_of[k] = i
            return carry

        return lax.fori_loop(starts[0, 0, i], starts[0, 0, i + 1], name_slot, carry)

    lax.fori_loop(0, row_blocks, name_row, 0)
    live = starts[0, 0, row_blocks]

    def name_dead(k, carry):
        row_of[k] = row_blocks
        return carry

    lax.fori_loop(live, slots, name_dead, 0)
    row_of[slots] = live

    def name_col(k, carry):
        col_of[k] = cols[0, 0, k]
        return carry

    lax.fori_loop(0, slots, name_col, 0)


def prepare(starts, cols, features):
    slots = cols.shape[2]
    return pl.pallas_call(
        prepare_kernel,
        out_shape=[
            jax.ShapeDtypeStruct((slots + 1,), jnp.int32),
            jax.ShapeDtypeStruct((slots,), jnp.int32),
            jax.ShapeDtypeStruct(features.shape, BF16),
        ],
        in_specs=[SMEM, SMEM, VMEM],
        out_specs=[SMEM, SMEM, VMEM],
        compiler_params=params(32),
    )(starts, cols, features)


def order(parts, backward):
    return parts if backward else parts[::-1]


def sparse_kernel(counts, outs, backward, row_of, col_of, here_ref, mine_ref, *refs):
    parts = sum(counts)
    panel_refs = refs[:parts]
    values_ref = refs[parts]
    out_refs = refs[parts + 1 : parts + 1 + len(outs)]
    panel, values, total, values_sem = refs[parts + 1 + len(outs) :]
    slots, size, _ = values.shape
    live, here, mine = row_of[slots], here_ref[0], mine_ref[0]
    chunk = panel_refs[0].shape[0]
    def load(g):
        span = pl.ds(pl.multiple_of(g * GROUP, GROUP), GROUP)
        return pltpu.make_async_copy(values_ref.at[span], values.at[span], values_sem.at[g])

    def begin(g, carry):
        load(g).start()
        return carry

    used = (live + GROUP - 1) // GROUP
    lax.fori_loop(0, used, begin, 0)
    total[...] = jnp.zeros_like(total)
    at = 0
    for m, count in order(list(enumerate(counts)), backward):
        start = pl.multiple_of((here ^ m) * chunk, chunk)
        part = panel_refs[at][...]
        for ref in panel_refs[at + 1 : at + count]:
            part += ref[...]
        panel[pl.ds(start, chunk), :] = part
        at += count
    spare = total.shape[0] // size - 1
    last = panel.shape[0] // size - 1

    def add_slot(k):
        row, col = row_of[k], col_of[k]
        to, source = (col, jnp.minimum(row, last)) if backward else (row, col)
        to = pl.multiple_of(jnp.where(k < live, to, spare) * size, size)
        source = pl.multiple_of(source * size, size)
        term = lax.dot_general(
            values[k],
            panel[pl.ds(source, size), :],
            (((0 if backward else 1,), (0,)), ((), ())),
            preferred_element_type=F32,
        )
        total[pl.ds(to, size), :] += term

    def steps(count):
        def step(g, carry):
            for part in range(count // GROUP):
                load(g * (count // GROUP) + part).wait()
            for u in range(count):
                add_slot(g * count + u)
            return carry

        return step

    long = live // LONG
    lax.fori_loop(0, long, steps(LONG), 0)
    lax.fori_loop(long * (LONG // GROUP), used, steps(GROUP), 0)
    for out_ref, members in zip(out_refs, outs):
        rows = out_ref.shape[0] // len(members)
        for at, m in enumerate(members):
            start = pl.multiple_of((mine ^ m) * rows, rows)
            out_ref[at * rows : (at + 1) * rows, :] = total[pl.ds(start, rows), :].astype(
                out_ref.dtype
            )


def sparse_product(panel_parts, values, row_of, col_of, here, mine, blocks, outs, backward):
    counts = [len(part) for part in panel_parts]
    operands = [operand for part in order(panel_parts, backward) for operand in part]
    parts = len(counts)
    slots, size, _ = values.shape
    chunk, width = operands[0].shape
    flops = 2 * slots * size * size * width
    return pl.pallas_call(
        functools.partial(sparse_kernel, counts, outs, backward),
        out_shape=[jax.ShapeDtypeStruct((chunk * len(members), width), BF16) for members in outs],
        in_specs=[SMEM] * 4 + [VMEM] * len(operands) + [ANY],
        out_specs=[VMEM] * len(outs),
        scratch_shapes=[
            pltpu.VMEM((parts * chunk, width), BF16),
            pltpu.VMEM((slots, size, size), BF16),
            pltpu.VMEM(((blocks + 1) * size, width), F32),
            pltpu.SemaphoreType.DMA((slots // GROUP,)),
        ],
        compiler_params=params(48),
        cost_estimate=cost(flops, 2 * values.size + 2 * parts * chunk * width),
    )(row_of, col_of, here, mine, *operands, values)


def split(value):
    high = value.astype(BF16)
    return high, (value - high.astype(F32)).astype(BF16)


def mm(a, b, dims):
    return lax.dot_general(a, b, (dims, ((), ())), preferred_element_type=F32)


def middle_kernel(count, *refs):
    terms = refs[:count]
    weight_ref, cotangent_ref, act_ref, back_ref, agg_ref, grad_ref = refs[count:]
    aggregated = terms[0][...].astype(F32)
    for term in terms[1:]:
        aggregated += term[...].astype(F32)
    agg_ref[...] = aggregated
    weight = weight_ref[...]
    high, low = split(aggregated)
    mixed = mm(high, weight, ((1,), (0,))) + mm(low, weight, ((1,), (0,)))
    sigma = jax.nn.sigmoid(mixed)
    act_ref[...] = (mixed * sigma).astype(BF16)
    mixed_grad = cotangent_ref[...].astype(F32) * (sigma * (1.0 + mixed * (1.0 - sigma)))
    grad_ref[...] = mixed_grad
    high, low = split(mixed_grad)
    back = mm(high, weight, ((1,), (1,))) + mm(low, weight, ((1,), (1,)))
    back_ref[...] = back.astype(BF16)


def middle(terms, weight, cotangent):
    rows, width = cotangent.shape
    return pl.pallas_call(
        functools.partial(middle_kernel, len(terms)),
        out_shape=[
            jax.ShapeDtypeStruct((rows, width), BF16),
            jax.ShapeDtypeStruct((rows, width), BF16),
            jax.ShapeDtypeStruct((rows, width), F32),
            jax.ShapeDtypeStruct((rows, width), F32),
        ],
        in_specs=[VMEM] * (len(terms) + 2),
        out_specs=[VMEM] * 4,
        compiler_params=params(40),
        cost_estimate=cost(8 * rows * width * width, 20 * rows * width),
    )(*terms, weight, cotangent)


def weight_kernel(chunks, me, agg_ref, grad_ref, own_ref, other_ref, scratch):
    high, low = split(agg_ref[...])
    grad_high, grad_low = split(grad_ref[...])
    contract = ((0,), (0,))
    scratch[...] = (
        mm(high, grad_high, contract) + mm(low, grad_high, contract) + mm(high, grad_low, contract)
    )
    depth = scratch.shape[0] // chunks
    for c in range(chunks // 2):
        for ref, other in ((own_ref, 0), (other_ref, 1)):
            start = pl.multiple_of((2 * c + (me[0] % 2 ^ other)) * depth, depth)
            ref[c * depth : (c + 1) * depth, :] = scratch[pl.ds(start, depth), :]


def weight_term(aggregated, mixed_grad, me, chunks):
    rows, width = aggregated.shape
    return pl.pallas_call(
        functools.partial(weight_kernel, chunks),
        out_shape=[jax.ShapeDtypeStruct((width // 2, width), F32)] * 2,
        in_specs=[SMEM, VMEM, VMEM],
        out_specs=[VMEM, VMEM],
        scratch_shapes=[pltpu.VMEM((width, width), F32)],
        compiler_params=params(40),
        cost_estimate=cost(6 * rows * width * width, 8 * rows * width),
    )(me, aggregated, mixed_grad)


def assemble_kernel(chunks, me, own_ref, other_ref, out_ref):
    depth = own_ref.shape[0] // chunks
    for c in range(chunks):
        for ref, other in ((own_ref, 0), (other_ref, 1)):
            start = pl.multiple_of((2 * c + (me[0] % 2 ^ other)) * depth, depth)
            out_ref[pl.ds(start, depth), :] = ref[c * depth : (c + 1) * depth, :]


def assemble(own, other, me, chunks):
    depth, width = own.shape
    return pl.pallas_call(
        functools.partial(assemble_kernel, chunks),
        out_shape=jax.ShapeDtypeStruct((2 * depth, width), own.dtype),
        in_specs=[SMEM, VMEM, VMEM],
        out_specs=VMEM,
        compiler_params=params(32),
    )(me, own, other)


def pair_kernel(count, own_ref, other_ref, *outs):
    rows = own_ref.shape[0] // count
    for m in range(count):
        span = slice(m * rows, (m + 1) * rows)
        outs[m][...] = (own_ref[span, :].astype(F32) + other_ref[span, :].astype(F32)).astype(BF16)


def pair_sum(own, other, count):
    rows, width = own.shape
    return pl.pallas_call(
        functools.partial(pair_kernel, count),
        out_shape=[jax.ShapeDtypeStruct((rows // count, width), BF16)] * count,
        in_specs=[VMEM] * 2,
        out_specs=[VMEM] * count,
        compiler_params=params(40),
        cost_estimate=cost(rows * width, 6 * rows * width),
    )(own, other)


def swap(x, axis, n, m):
    return lax.ppermute(x, axis, [(i, i ^ m) for i in range(n)])


def copies_kernel(parts, copies, in_ref, out_ref):
    rows = in_ref.shape[0] // parts
    result = in_ref[:rows, :]
    for p in range(1, parts):
        result += in_ref[p * rows : (p + 1) * rows, :]
    result = result.astype(BF16)
    for c in range(copies):
        out_ref[c * rows : (c + 1) * rows, :] = result


def sum_copies(stacked, parts, copies):
    rows, width = stacked.shape
    return pl.pallas_call(
        functools.partial(copies_kernel, parts, copies),
        out_shape=jax.ShapeDtypeStruct((rows // parts * copies, width), BF16),
        in_specs=[VMEM],
        out_specs=VMEM,
        compiler_params=params(32),
        cost_estimate=cost(0, 0),
    )(stacked)


def add_kernel(*refs):
    result = refs[0][...].astype(F32)
    for ref in refs[1:-1]:
        result += ref[...].astype(F32)
    refs[-1][...] = result


def add_up(terms):
    return pl.pallas_call(
        add_kernel,
        out_shape=jax.ShapeDtypeStruct(terms[0].shape, F32),
        in_specs=[VMEM] * len(terms),
        out_specs=VMEM,
        compiler_params=params(32),
        cost_estimate=cost(0, 64 * terms[0].size),
    )(*terms)


def exchange_terms(terms, n):
    if n != 4:
        return [terms[0]] + [swap(terms[m], "col", n, m) for m in range(n - 1, 0, -1)]
    far = lax.ppermute(terms[3], "col", [(0, 1), (3, 2)])
    cross = lax.ppermute(terms[3], "col", [(1, 2), (2, 1)])
    inward = lax.ppermute(terms[2], "col", [(0, 2), (3, 1)])
    near = swap(terms[1], "col", n, 1)
    relay = total_of([terms[2], far]).astype(BF16)
    outward = lax.ppermute(relay, "col", [(1, 3), (2, 0)])
    return [add_up([cross, inward, near, terms[0]]), outward]


def gather_parts(own, n, first):
    if n != 4:
        return [[own]] + [[swap(own, "col", n, m)] for m in range(n - 1, 0, -1)][::-1], first
    inward = lax.ppermute(own, "col", [(0, 2), (3, 1)])
    cross = lax.ppermute(own, "col", [(1, 2), (2, 1)])
    outward = lax.ppermute(own, "col", [(1, 3), (2, 0)])
    near = swap(own, "col", n, 1)
    inward, first = lax.optimization_barrier((inward, first))
    far = lax.ppermute(inward, "col", [(2, 3), (1, 0)])
    return [[own], [near], [inward, outward], [cross, far]], first


def total_of(terms):
    result = terms[0].astype(F32)
    for term in terms[1:]:
        result = result + term.astype(F32)
    return result


def exchange(x, axis):
    return lax.all_to_all(x, axis, 0, 0, tiled=True)


def on_device(n_row, n_col, features, weight, block_cols, row_starts, block_values, cotangent):
    values = block_values[0, 0]
    size = values.shape[1]
    row_blocks = row_starts.shape[2] - 1
    col_blocks = n_row * features.shape[0] // size
    me_row = lax.axis_index("row")[None].astype(jnp.int32)
    me_col = lax.axis_index("col")[None].astype(jnp.int32)

    panel = [features] + [None] * (n_row - 1)
    for m in range(n_row - 2, 0, -2):
        panel[m] = swap(features, "row", n_row, m)
    prepared = prepare(row_starts, block_cols, features)
    panel[n_row - 2], (row_of, col_of, panel[0]) = lax.optimization_barrier(
        (panel[n_row - 2], prepared)
    )
    for m in range(0, n_row, 2):
        panel[m + 1] = swap(panel[m], "row", n_row, 1)

    each = [[m] for m in range(n_col)]
    terms = sparse_product(
        [[part] for part in panel], values, row_of, col_of, me_row, me_col, row_blocks, each, False
    )
    terms = exchange_terms(terms, n_col)
    activations, back, aggregated, mixed_grad = middle(terms, weight, cotangent)

    own_term, other_term = weight_term(aggregated, mixed_grad, me_row, n_row)
    term = own_term + swap(other_term, "row", n_row, 1)
    back_panel, term = gather_parts(back, n_col, term)
    cores = [list(range(0, n_row, 2)), list(range(1, n_row, 2))]
    half = lax.all_gather(term, "row", axis=0, axis_index_groups=cores, tiled=True)
    copies = sum_copies(half, n_row // 2, n_col)
    copies, back_panel[0] = lax.optimization_barrier((copies, back_panel[0]))

    even = list(range(0, n_row, 2))
    pair = [even, [m + 1 for m in even]]
    own, other = sparse_product(
        back_panel, values, row_of, col_of, me_col, me_row, col_blocks, pair, True
    )
    sums = pair_sum(own, swap(other, "row", n_row, 1), len(even))
    feature_grad = total_of(
        [swap(s, "row", n_row, m) for s, m in zip(sums[:0:-1], even[:0:-1])] + [sums[0]]
    ).astype(BF16)
    halves = exchange(copies, "col")
    half = jnp.sum(halves.reshape(n_col, -1, halves.shape[1]).astype(F32), axis=0)
    other = swap(half, "row", n_row, 1)
    weight_grad = assemble(half, other, me_row, n_row // 2)
    return (activations, feature_grad, weight_grad)


def solution(mesh):
    placed = (
        P(("col", "row"), None),
        P(),
        P("row", "col", None),
        P("row", "col", None),
        P("row", "col", None, None, None),
        P(("row", "col"), None),
    )
    return jax.shard_map(
        functools.partial(on_device, mesh.shape["row"], mesh.shape["col"]),
        mesh=mesh,
        in_specs=placed,
        out_specs=(P(("row", "col"), None), P(("col", "row"), None), P()),
        check_vma=False,
    )
```

```python
import functools

import jax
import jax.numpy as jnp
from jax import lax
from jax.experimental import pallas as pl
from jax.experimental.pallas import tpu as pltpu
from jax.sharding import PartitionSpec as P

F32 = jnp.float32
BF16 = jnp.bfloat16
GROUP = 8
LONG = 32
ANY = pl.BlockSpec(memory_space=pl.ANY)
VMEM = pl.BlockSpec(memory_space=pltpu.VMEM)
SMEM = pl.BlockSpec(memory_space=pltpu.SMEM)


def params(mib):
    return pltpu.CompilerParams(vmem_limit_bytes=mib << 20)


def cost(flops, nbytes):
    return pl.CostEstimate(flops=flops, bytes_accessed=nbytes, transcendentals=0)


def prepare_kernel(starts, cols, features, row_of, col_of, own):
    own[...] = features[...]
    slots = cols.shape[2]
    row_blocks = starts.shape[2] - 1

    def name_row(i, carry):
        def name_slot(k, carry):
            row_of[k] = i
            return carry

        return lax.fori_loop(starts[0, 0, i], starts[0, 0, i + 1], name_slot, carry)

    lax.fori_loop(0, row_blocks, name_row, 0)
    live = starts[0, 0, row_blocks]

    def name_dead(k, carry):
        row_of[k] = row_blocks
        return carry

    lax.fori_loop(live, slots, name_dead, 0)
    row_of[slots] = live

    def name_col(k, carry):
        col_of[k] = cols[0, 0, k]
        return carry

    lax.fori_loop(0, slots, name_col, 0)


def prepare(starts, cols, features):
    slots = cols.shape[2]
    return pl.pallas_call(
        prepare_kernel,
        out_shape=[
            jax.ShapeDtypeStruct((slots + 1,), jnp.int32),
            jax.ShapeDtypeStruct((slots,), jnp.int32),
            jax.ShapeDtypeStruct(features.shape, BF16),
        ],
        in_specs=[SMEM, SMEM, VMEM],
        out_specs=[SMEM, SMEM, VMEM],
        compiler_params=params(32),
    )(starts, cols, features)


def sparse_kernel(counts, outs, backward, row_of, col_of, here_ref, mine_ref, *refs):
    parts = sum(counts)
    panel_refs = refs[:parts]
    values_ref = refs[parts]
    out_refs = refs[parts + 1 : parts + 1 + len(outs)]
    panel, values, total, values_sem = refs[parts + 1 + len(outs) :]
    slots, size, _ = values.shape
    live, here, mine = row_of[slots], here_ref[0], mine_ref[0]
    chunk = panel_refs[0].shape[0]
    def load(g):
        span = pl.ds(pl.multiple_of(g * GROUP, GROUP), GROUP)
        return pltpu.make_async_copy(values_ref.at[span], values.at[span], values_sem.at[g])

    def begin(g, carry):
        load(g).start()
        return carry

    used = (live + GROUP - 1) // GROUP
    lax.fori_loop(0, used, begin, 0)
    total[...] = jnp.zeros_like(total)
    at = parts
    for m, count in enumerate(counts):
        start = pl.multiple_of((here ^ m) * chunk, chunk)
        part = panel_refs[at - 1][...]
        for ref in panel_refs[at - count : at - 1]:
            part += ref[...]
        panel[pl.ds(start, chunk), :] = part
        at -= count
    spare = total.shape[0] // size - 1
    last = panel.shape[0] // size - 1

    def add_slot(k):
        row, col = row_of[k], col_of[k]
        to, source = (col, jnp.minimum(row, last)) if backward else (row, col)
        to = pl.multiple_of(jnp.where(k < live, to, spare) * size, size)
        source = pl.multiple_of(source * size, size)
        term = lax.dot_general(
            values[k],
            panel[pl.ds(source, size), :],
            (((0 if backward else 1,), (0,)), ((), ())),
            preferred_element_type=F32,
        )
        total[pl.ds(to, size), :] += term

    def steps(count):
        def step(g, carry):
            for part in range(count // GROUP):
                load(g * (count // GROUP) + part).wait()
            for u in range(count):
                add_slot(g * count + u)
            return carry

        return step

    longest, long = live // (2 * LONG), live // LONG
    lax.fori_loop(0, longest, steps(2 * LONG), 0)
    lax.fori_loop(longest * 2, long, steps(LONG), 0)
    lax.fori_loop(long * (LONG // GROUP), used, steps(GROUP), 0)
    for out_ref, members in zip(out_refs, outs):
        rows = out_ref.shape[0] // len(members)
        for at, m in enumerate(members):
            start = pl.multiple_of((mine ^ m) * rows, rows)
            out_ref[at * rows : (at + 1) * rows, :] = total[pl.ds(start, rows), :].astype(
                out_ref.dtype
            )


def sparse_product(panel_parts, values, row_of, col_of, here, mine, blocks, outs, backward):
    counts = [len(part) for part in panel_parts]
    operands = [operand for part in panel_parts for operand in part]
    parts = len(counts)
    slots, size, _ = values.shape
    chunk, width = operands[0].shape
    flops = 2 * slots * size * size * width
    return pl.pallas_call(
        functools.partial(sparse_kernel, counts, outs, backward),
        out_shape=[jax.ShapeDtypeStruct((chunk * len(members), width), BF16) for members in outs],
        in_specs=[SMEM] * 4 + [VMEM] * len(operands) + [ANY],
        out_specs=[VMEM] * len(outs),
        scratch_shapes=[
            pltpu.VMEM((parts * chunk, width), BF16),
            pltpu.VMEM((slots, size, size), BF16),
            pltpu.VMEM(((blocks + 1) * size, width), F32),
            pltpu.SemaphoreType.DMA((slots // GROUP,)),
        ],
        compiler_params=params(48),
        cost_estimate=cost(flops, 2 * values.size + 2 * parts * chunk * width),
    )(row_of, col_of, here, mine, *operands[::-1], values)


def split(value):
    high = value.astype(BF16)
    return high, (value - high.astype(F32)).astype(BF16)


def mm(a, b, dims):
    return lax.dot_general(a, b, (dims, ((), ())), preferred_element_type=F32)


def middle_kernel(count, *refs):
    terms = refs[:count]
    weight_ref, cotangent_ref, act_ref, back_ref, agg_ref, grad_ref = refs[count:]
    aggregated = terms[0][...].astype(F32)
    for term in terms[1:]:
        aggregated += term[...].astype(F32)
    agg_ref[...] = aggregated
    weight = weight_ref[...]
    high, low = split(aggregated)
    mixed = mm(high, weight, ((1,), (0,))) + mm(low, weight, ((1,), (0,)))
    sigma = jax.nn.sigmoid(mixed)
    act_ref[...] = (mixed * sigma).astype(BF16)
    mixed_grad = cotangent_ref[...].astype(F32) * (sigma * (1.0 + mixed * (1.0 - sigma)))
    grad_ref[...] = mixed_grad
    high, low = split(mixed_grad)
    back = mm(high, weight, ((1,), (1,))) + mm(low, weight, ((1,), (1,)))
    back_ref[...] = back.astype(BF16)


def middle(terms, weight, cotangent):
    rows, width = cotangent.shape
    return pl.pallas_call(
        functools.partial(middle_kernel, len(terms)),
        out_shape=[
            jax.ShapeDtypeStruct((rows, width), BF16),
            jax.ShapeDtypeStruct((rows, width), BF16),
            jax.ShapeDtypeStruct((rows, width), F32),
            jax.ShapeDtypeStruct((rows, width), F32),
        ],
        in_specs=[VMEM] * (len(terms) + 2),
        out_specs=[VMEM] * 4,
        compiler_params=params(40),
        cost_estimate=cost(8 * rows * width * width, 20 * rows * width),
    )(*terms, weight, cotangent)


def weight_kernel(chunks, me, agg_ref, grad_ref, own_ref, other_ref, scratch):
    high, low = split(agg_ref[...])
    grad_high, grad_low = split(grad_ref[...])
    contract = ((0,), (0,))
    scratch[...] = (
        mm(high, grad_high, contract) + mm(low, grad_high, contract) + mm(high, grad_low, contract)
    )
    depth = scratch.shape[0] // chunks
    for c in range(chunks // 2):
        for ref, other in ((own_ref, 0), (other_ref, 1)):
            start = pl.multiple_of((2 * c + (me[0] % 2 ^ other)) * depth, depth)
            ref[c * depth : (c + 1) * depth, :] = scratch[pl.ds(start, depth), :]


def weight_term(aggregated, mixed_grad, me, chunks):
    rows, width = aggregated.shape
    return pl.pallas_call(
        functools.partial(weight_kernel, chunks),
        out_shape=[jax.ShapeDtypeStruct((width // 2, width), F32)] * 2,
        in_specs=[SMEM, VMEM, VMEM],
        out_specs=[VMEM, VMEM],
        scratch_shapes=[pltpu.VMEM((width, width), F32)],
        compiler_params=params(40),
        cost_estimate=cost(6 * rows * width * width, 8 * rows * width),
    )(me, aggregated, mixed_grad)


def assemble_kernel(chunks, me, own_ref, other_ref, out_ref):
    depth = own_ref.shape[0] // chunks
    for c in range(chunks):
        for ref, other in ((own_ref, 0), (other_ref, 1)):
            start = pl.multiple_of((2 * c + (me[0] % 2 ^ other)) * depth, depth)
            out_ref[pl.ds(start, depth), :] = ref[c * depth : (c + 1) * depth, :]


def assemble(own, other, me, chunks):
    depth, width = own.shape
    return pl.pallas_call(
        functools.partial(assemble_kernel, chunks),
        out_shape=jax.ShapeDtypeStruct((2 * depth, width), own.dtype),
        in_specs=[SMEM, VMEM, VMEM],
        out_specs=VMEM,
        compiler_params=params(32),
    )(me, own, other)


def pair_kernel(count, own_ref, other_ref, *outs):
    rows = own_ref.shape[0] // count
    for m in range(count):
        span = slice(m * rows, (m + 1) * rows)
        outs[m][...] = (own_ref[span, :].astype(F32) + other_ref[span, :].astype(F32)).astype(BF16)


def pair_sum(own, other, count):
    rows, width = own.shape
    return pl.pallas_call(
        functools.partial(pair_kernel, count),
        out_shape=[jax.ShapeDtypeStruct((rows // count, width), BF16)] * count,
        in_specs=[VMEM] * 2,
        out_specs=[VMEM] * count,
        compiler_params=params(40),
        cost_estimate=cost(rows * width, 6 * rows * width),
    )(own, other)


def swap(x, axis, n, m):
    return lax.ppermute(x, axis, [(i, i ^ m) for i in range(n)])


def copies_kernel(parts, copies, in_ref, out_ref):
    rows = in_ref.shape[0] // parts
    result = in_ref[:rows, :]
    for p in range(1, parts):
        result += in_ref[p * rows : (p + 1) * rows, :]
    result = result.astype(BF16)
    for c in range(copies):
        out_ref[c * rows : (c + 1) * rows, :] = result


def sum_copies(stacked, parts, copies):
    rows, width = stacked.shape
    return pl.pallas_call(
        functools.partial(copies_kernel, parts, copies),
        out_shape=jax.ShapeDtypeStruct((rows // parts * copies, width), BF16),
        in_specs=[VMEM],
        out_specs=VMEM,
        compiler_params=params(32),
        cost_estimate=cost(0, 0),
    )(stacked)


def add_kernel(*refs):
    result = refs[0][...].astype(F32)
    for ref in refs[1:-1]:
        result += ref[...].astype(F32)
    refs[-1][...] = result


def add_up(terms):
    return pl.pallas_call(
        add_kernel,
        out_shape=jax.ShapeDtypeStruct(terms[0].shape, F32),
        in_specs=[VMEM] * len(terms),
        out_specs=VMEM,
        compiler_params=params(32),
        cost_estimate=cost(0, 64 * terms[0].size),
    )(*terms)


def exchange_terms(terms, n):
    if n != 4:
        return [terms[0]] + [swap(terms[m], "col", n, m) for m in range(n - 1, 0, -1)]
    far = lax.ppermute(terms[3], "col", [(0, 1), (3, 2)])
    cross = lax.ppermute(terms[3], "col", [(1, 2), (2, 1)])
    inward = lax.ppermute(terms[2], "col", [(0, 2), (3, 1)])
    near = swap(terms[1], "col", n, 1)
    relay = total_of([terms[2], far]).astype(BF16)
    outward = lax.ppermute(relay, "col", [(1, 3), (2, 0)])
    return [add_up([cross, inward, near, terms[0]]), outward]


def gather_parts(own, n, first):
    if n != 4:
        return [[own]] + [[swap(own, "col", n, m)] for m in range(n - 1, 0, -1)][::-1], first
    inward = lax.ppermute(own, "col", [(0, 2), (3, 1)])
    cross = lax.ppermute(own, "col", [(1, 2), (2, 1)])
    outward = lax.ppermute(own, "col", [(1, 3), (2, 0)])
    near = swap(own, "col", n, 1)
    inward, first = lax.optimization_barrier((inward, first))
    far = lax.ppermute(inward, "col", [(2, 3), (1, 0)])
    return [[own], [near], [inward, outward], [cross, far]], first


def total_of(terms):
    result = terms[0].astype(F32)
    for term in terms[1:]:
        result = result + term.astype(F32)
    return result


def exchange(x, axis):
    return lax.all_to_all(x, axis, 0, 0, tiled=True)


def on_device(n_row, n_col, features, weight, block_cols, row_starts, block_values, cotangent):
    values = block_values[0, 0]
    size = values.shape[1]
    row_blocks = row_starts.shape[2] - 1
    col_blocks = n_row * features.shape[0] // size
    me_row = lax.axis_index("row")[None].astype(jnp.int32)
    me_col = lax.axis_index("col")[None].astype(jnp.int32)

    panel = [features] + [None] * (n_row - 1)
    for m in range(n_row - 2, 0, -2):
        panel[m] = swap(features, "row", n_row, m)
    prepared = prepare(row_starts, block_cols, features)
    panel[n_row - 2], (row_of, col_of, panel[0]) = lax.optimization_barrier(
        (panel[n_row - 2], prepared)
    )
    for m in range(0, n_row, 2):
        panel[m + 1] = swap(panel[m], "row", n_row, 1)

    each = [[m] for m in range(n_col)]
    terms = sparse_product(
        [[part] for part in panel], values, row_of, col_of, me_row, me_col, row_blocks, each, False
    )
    terms = exchange_terms(terms, n_col)
    activations, back, aggregated, mixed_grad = middle(terms, weight, cotangent)

    own_term, other_term = weight_term(aggregated, mixed_grad, me_row, n_row)
    term = own_term + swap(other_term, "row", n_row, 1)
    back_panel, term = gather_parts(back, n_col, term)
    cores = [list(range(0, n_row, 2)), list(range(1, n_row, 2))]
    half = lax.all_gather(term, "row", axis=0, axis_index_groups=cores, tiled=True)
    copies = sum_copies(half, n_row // 2, n_col)
    copies, back_panel[0] = lax.optimization_barrier((copies, back_panel[0]))

    even = list(range(0, n_row, 2))
    pair = [even, [m + 1 for m in even]]
    own, other = sparse_product(
        back_panel, values, row_of, col_of, me_col, me_row, col_blocks, pair, True
    )
    sums = pair_sum(own, swap(other, "row", n_row, 1), len(even))
    feature_grad = total_of(
        [swap(s, "row", n_row, m) for s, m in zip(sums[:0:-1], even[:0:-1])] + [sums[0]]
    ).astype(BF16)
    halves = exchange(copies, "col")
    half = jnp.sum(halves.reshape(n_col, -1, halves.shape[1]).astype(F32), axis=0)
    other = swap(half, "row", n_row, 1)
    weight_grad = assemble(half, other, me_row, n_row // 2)
    return (activations, feature_grad, weight_grad)


def solution(mesh):
    placed = (
        P(("col", "row"), None),
        P(),
        P("row", "col", None),
        P("row", "col", None),
        P("row", "col", None, None, None),
        P(("row", "col"), None),
    )
    return jax.shard_map(
        functools.partial(on_device, mesh.shape["row"], mesh.shape["col"]),
        mesh=mesh,
        in_specs=placed,
        out_specs=(P(("row", "col"), None), P(("col", "row"), None), P()),
        check_vma=False,
    )
```
